128 devices in a mesh: item: 32 (over z, x, core), req: 4 (over y).
Axes of the slice: x: 4, y: 4, z: 4, core: 2. Of those that a mesh axis runs over, the one named last changes fastest.
Arguments:
- user_emb: bfloat16 [128, 256], P('req'), may hold values from -6 to 6
- codebooks: bfloat16 [32, 256, 8], P('item'), may hold values from -1 to 1
- item_codes: int32 [131072, 32], P('item'), may hold values from 0 to 255
- item_place: int32 [131072], replicated, may hold values from 0 to 131071, as said below
- candidates: int32 [128, 512], P('req', 'item'), may hold values from 0 to 131071, as said below
- item_features: bfloat16 [131072, 768], P(('item', 'req')), may hold values from -6 to 6
- cross_weights: bfloat16 [4, 1024, 1024], replicated, may hold values from -0.25 to 0.25
- cross_bias: float32 [4, 1024], replicated, may hold values from -6 to 6
- out_weight: float32 [1024], replicated, may hold values from -0.5 to 0.5
Outputs:
- scores: float32 [128, 131072], P('req', 'item')
- logits: float32 [128, 512], P('req', 'item')
The draws below stay inside these ranges and needn't reach their ends.
Inputs may be any that keep to these rules, and one draw needn't show every extreme that they name: A permutation of the item ids: item_place[i] is the storage row of item i; storage row s is held by the device at flat index s // 1024 of item+req (item slowest). Item ids. In each aligned block of 32 requests by 16 candidates (one device's share), at most 12 candidates have storage rows on any one owner; in every draw one owner, the same for all blocks, is named exactly 12 times in every block.
All inputs are finite; a program needn't handle non-finite values.
Results may differ from the reference program's by a relative error of at most 0.0033.
Values may be sent and summed in bfloat16 or wider, within the bound.
No kernel may reach another device: no remote copies, remote signals or barrier semaphores. Data moves between devices by JAX's collectives and lax.ppermute only.
A program may use at most 64 MiB of HBM per device.

```python
import jax
import jax.numpy as jnp
from jax import lax

M = 32
K = 256
SUB = 8
F_ITEM = 768
LAYERS = 4
ITEMS_DEV = 4096
R_DEV = 32
CAND_DEV = 16
D_USER = 256
W = 1024
ITEMS = 131072
REQS = 128
CAND = 512
OWNERS = 128
ROWS_DEV = 1024
CAP = 12
N_ITEM = 32


def shared_place(key):
    return jax.random.permutation(jax.random.fold_in(key, 11), ITEMS).astype(jnp.int32)


def draw_item_place(key, part):
    return shared_place(key)


def one_block(block_key, hottest, stored):
    keys = jax.random.split(block_key, 4)
    rest = R_DEV * CAND_DEV - CAP
    others = OWNERS - 1
    base = rest // others
    extra = rest % others
    pairs = others // 2
    counts = base + (jnp.arange(others, dtype=jnp.int32) < extra).astype(jnp.int32)
    shifts = jax.random.randint(keys[0], (pairs,), 0, base // 2 + 1, dtype=jnp.int32)
    counts = counts.at[0:2 * pairs:2].add(shifts).at[1:2 * pairs:2].add(-shifts)
    bounds = jnp.cumsum(counts).astype(jnp.int32)
    bucket = jnp.searchsorted(bounds, jnp.arange(rest, dtype=jnp.int32), side='right').astype(jnp.int32)
    mapping = jax.random.permutation(keys[1], others).astype(jnp.int32)
    other_owner = (hottest + 1 + mapping[bucket]) % OWNERS
    owner_seq = jnp.concatenate([jnp.full((CAP,), hottest, jnp.int32), other_owner])
    owner_seq = jax.random.permutation(keys[2], owner_seq)
    within = jax.random.randint(keys[3], (R_DEV * CAND_DEV,), 0, ROWS_DEV, dtype=jnp.int32)
    return stored[owner_seq * ROWS_DEV + within]


def draw_candidates(key, part):
    stored = jnp.argsort(shared_place(key)).astype(jnp.int32)
    key = jax.random.fold_in(key, 5)
    hot_key, block_key = jax.random.split(key)
    hottest = jax.random.randint(hot_key, (), 0, OWNERS, dtype=jnp.int32)
    groups = REQS // R_DEV
    columns = CAND // CAND_DEV
    block_keys = jax.random.split(block_key, groups * columns)
    blocks = jax.vmap(lambda one: one_block(one, hottest, stored))(block_keys)
    blocks = blocks.reshape(groups, columns, R_DEV, CAND_DEV)
    return jnp.transpose(blocks, (0, 2, 1, 3)).reshape(REQS, CAND).astype(jnp.int32)


def touch_ends(values, rng, least, high):
    index_at = [jax.random.randint(jax.random.fold_in(rng, axis), (), 0, length) for axis, length in enumerate(values.shape)]
    longest = values.shape.index(max(values.shape))
    neighbour = index_at[:longest] + [(index_at[longest] + 1) % values.shape[longest]] + index_at[longest + 1:]
    return values.at[tuple(index_at)].set(least).at[tuple(neighbour)].set(high)


def block_levels(own_key, dims, pieces, smallest, top_value):
    factor_of = 1.0
    for axis_at, blocks in pieces:
        heights = jax.random.uniform(jax.random.fold_in(jax.random.fold_in(own_key, 6), axis_at), (blocks,), jnp.float32, smallest / len(pieces), top_value / len(pieces))
        factor_of = factor_of * jnp.repeat(jnp.exp(heights), dims[axis_at] // blocks).reshape((-1,) + (1,) * (len(dims) - 1 - axis_at))
    return factor_of


def noise(key, extent, deviation, most, shards=(), kind=jnp.bfloat16):
    entries = deviation * jax.random.normal(key, extent, jnp.float32)
    if shards:
        entries = entries * block_levels(key, extent, shards, -0.22, 0.18)
    return jnp.clip(entries, -most, most).astype(kind)


def setup_inputs(seed: int = 0) -> dict:
    streams_of = jax.random.split(jax.random.key(seed), 10)
    user_emb = noise(streams_of[0], (REQS, D_USER), 1.0, 6.0, ((0, 4),))
    codebooks = noise(streams_of[1], (M, K, SUB), 0.0625, 1.0, ((0, 32),))
    item_codes = touch_ends(jax.random.randint(streams_of[2], (ITEMS, M), 0, K), jax.random.fold_in(streams_of[2], 1), 0, K - 1).astype(jnp.int32)
    item_place = draw_item_place(jax.random.fold_in(streams_of[9], 71), 0)
    candidates = draw_candidates(jax.random.fold_in(streams_of[9], 71), 0)
    item_features = noise(streams_of[5], (ITEMS, F_ITEM), 1.0, 6.0, ((0, 128),))
    cross_weights = noise(streams_of[6], (LAYERS, W, W), (0.5 / W ** 0.5), 0.25)
    cross_bias = noise(streams_of[7], (LAYERS, W), 0.5, 6.0, (), jnp.float32)
    out_weight = noise(streams_of[8], (W,), (1.0 / W ** 0.5), 0.5, (), jnp.float32)
    return dict(user_emb=user_emb, codebooks=codebooks, item_codes=item_codes, item_place=item_place, candidates=candidates, item_features=item_features, cross_weights=cross_weights, cross_bias=cross_bias, out_weight=out_weight)


def reference(user_emb, codebooks, item_codes, item_place, candidates, item_features, cross_weights, cross_bias, out_weight):
    parts = user_emb.astype(jnp.float32).reshape(REQS, M, SUB)
    tables = jnp.einsum("rms,mks->rmk", parts, codebooks.astype(jnp.float32)).astype(jnp.bfloat16)
    flat_tables = tables.reshape(REQS, M * K).astype(jnp.float32)
    offsets = (jnp.arange(M, dtype=jnp.int32) * K)[None, :]

    def score_block(codes_block):
        index = (codes_block + offsets).reshape(-1)
        picked = jnp.take(flat_tables, index, axis=1).reshape(REQS, codes_block.shape[0], M)
        return jnp.sum(picked, axis=2)

    score_parts = lax.map(score_block, item_codes.reshape(N_ITEM, ITEMS_DEV, M))
    scores = jnp.transpose(score_parts, (1, 0, 2)).reshape(REQS, ITEMS)

    def rank_block(inputs):
        users, item_ids = inputs
        slots = item_place[item_ids.reshape(-1)]
        rows = item_features[slots]
        repeated = jnp.repeat(users, CAND, axis=0)
        first = jnp.concatenate([repeated, rows], axis=1)
        state = first.astype(jnp.float32)
        for layer in range(LAYERS):
            product = jnp.dot(state.astype(jnp.bfloat16), cross_weights[layer], preferred_element_type=jnp.float32) + cross_bias[layer]
            state = first.astype(jnp.float32) * product + state
        return jnp.sum(state * out_weight, axis=1).reshape(8, CAND)

    ranked = lax.map(rank_block, (user_emb.reshape(REQS // 8, 8, D_USER), candidates.reshape(REQS // 8, 8, CAND)))
    logits = ranked.reshape(REQS, CAND)
    return scores, logits
```

```python
import functools

import jax
import jax.numpy as jnp
from jax import lax
from jax.experimental import pallas as pl
from jax.experimental.pallas import tpu as pltpu
from jax.sharding import PartitionSpec as P

F32 = jnp.float32
BF16 = jnp.bfloat16
I32 = jnp.int32
VMEM = pl.BlockSpec(memory_space=pltpu.VMEM)
LANES = 128
MSG = 8
CB_ROWS = 4
USER_ROW = 4
WANT_ROW = 6
HALF = 64


def dot(a, b, dims=(((1,), (0,)), ((), ()))):
    return lax.dot_general(a, b, dims, preferred_element_type=F32)


def iota(shape, axis):
    return lax.broadcasted_iota(I32, shape, axis)


def lane_sum(x):
    return jnp.sum(x, axis=1, keepdims=True)


def as_bf16(mask):
    return jnp.where(mask, 1.0, 0.0).astype(BF16)


def prepare_kernel(cand, place, codebook, user, message, meta, tiles):
    cand_dev, requests = cand.shape
    total = cand_dev * requests
    owners = message.shape[0]
    blocks = place.shape[0]
    item = lax.axis_index("item")
    req = lax.axis_index("req")
    ids = cand[...].astype(F32)
    spread = jnp.concatenate(
        [jnp.broadcast_to(ids[c : c + 1, :], (requests, requests)) for c in range(cand_dev)], axis=0
    )
    own_request = iota((total, requests), 0) % requests
    diagonal = own_request == iota((total, requests), 1)
    ids = lane_sum(jnp.where(diagonal, spread, 0.0)).astype(I32)
    where_row = as_bf16((ids >> 7) == iota((total, blocks), 1))
    stored = place[...]
    parts = jnp.concatenate(
        [
            (stored & 255).astype(F32).astype(BF16),
            ((stored >> 8) & 255).astype(F32).astype(BF16),
            (stored >> 16).astype(F32).astype(BF16),
        ],
        axis=1,
    )
    found = dot(where_row, parts)
    found = found[:, :LANES] + 256.0 * found[:, LANES : 2 * LANES] + 65536.0 * found[:, 2 * LANES :]
    lane = iota((total, LANES), 1)
    slot = lane_sum(jnp.where((ids & 127) == lane, found, 0.0)).astype(I32)
    rows_dev = blocks * LANES // owners
    shift = rows_dev.bit_length() - 1
    owner = slot >> shift
    within = slot & (rows_dev - 1)
    hit = owner == lane
    hits = as_bf16(hit)
    earlier = as_bf16(iota((total, total), 1) < iota((total, total), 0))
    rank = lane_sum(jnp.where(hit, dot(earlier, hits), 0.0)).astype(I32)
    meta[...] = jnp.where(lane == 0, owner, rank)
    request = iota((total, 1), 0) % requests
    low = (within & 255).astype(F32)
    high = ((within >> 8) + 4 * request + 128).astype(F32)
    entry = jnp.where(lane == rank, low, 0.0) + jnp.where(lane == rank + HALF, high, 0.0)
    wanted = dot(hits, entry.astype(BF16), (((0,), (0,)), ((), ())))
    book = codebook[...].astype(F32)
    sub = iota(book.shape, 0)
    first = jnp.sum(jnp.where(sub == 2 * req, book, 0.0), axis=0, keepdims=True)
    second = jnp.sum(jnp.where(sub == 2 * req + 1, book, 0.0), axis=0, keepdims=True)
    people = user[...].astype(F32)
    person = jnp.sum(jnp.where(iota(people.shape, 0) == item, people, 0.0), axis=0, keepdims=True)
    tile = jnp.concatenate(
        [
            first[:, :LANES],
            first[:, LANES:],
            second[:, :LANES],
            second[:, LANES:],
            person[:, :LANES],
            person[:, LANES:],
            jnp.zeros((2, LANES), F32),
        ],
        axis=0,
    )
    tiles[...] = jnp.broadcast_to(tile[None], (owners, MSG, LANES)).reshape(owners * MSG, LANES)
    tiles[pl.ds(WANT_ROW, owners, stride=MSG), :] = wanted
    message[...] = tiles[...].reshape(owners, MSG, LANES).astype(BF16)


def rank_kernel(chunk, got, items, weights, bias, out_weight, logits, tiles, first, rounded, state):
    sources = got.shape[0]
    rows = chunk * sources
    width = state.shape[1]
    layers = weights.shape[0]
    d_user = 2 * LANES
    tiles[...] = got[...].astype(F32).reshape(sources * MSG, LANES)
    wanted = tiles[pl.ds(WANT_ROW, sources, stride=MSG), :]
    people = jnp.concatenate(
        [tiles[pl.ds(USER_ROW + i, sources, stride=MSG), :] for i in range(2)], axis=1
    ).astype(BF16)
    lane = iota((sources, LANES), 1)
    high_lane = (lane >= HALF) & (wanted > 0.0)
    most = jnp.max(jnp.where(high_lane, lane - HALF + 1, 0))
    reqs = lax.axis_size("req")
    logits[...] = jnp.zeros(logits.shape, F32)

    def step(t, carry):
        lows, highs = [], []
        for k in range(chunk):
            j = t * chunk + k
            lows.append(lane_sum(jnp.where(lane == j, wanted, 0.0)))
            highs.append(lane_sum(jnp.where(lane == j + HALF, wanted, 0.0)))
        low = jnp.concatenate(lows, axis=0).astype(I32)
        high = jnp.concatenate(highs, axis=0).astype(I32)
        within = low + 256 * (high & 3)
        source = iota((rows, 1), 0) % sources
        person = ((high >> 2) & 31) * reqs + source % reqs
        pick_user = as_bf16(person == iota((rows, sources), 1))
        pick_item = as_bf16(within == iota((rows, items.shape[0]), 1))
        first[:, :d_user] = dot(pick_user, people).astype(BF16)
        first[:, d_user:] = dot(pick_item, items[...]).astype(BF16)
        state[...] = first[...].astype(F32)
        rounded[...] = first[...]

        def layer(l, carry):
            product = dot(rounded[...], weights[l]) + bias[pl.ds(l, 1), :]
            new = first[...].astype(F32) * product + state[...]
            state[...] = new
            rounded[...] = new.astype(BF16)
            return carry

        lax.fori_loop(0, layers, layer, 0)
        value = lane_sum(state[...] * out_weight[...])
        for k in range(chunk):
            j = t * chunk + k
            mine = value[k * sources : (k + 1) * sources]
            logits[...] += jnp.where(lane == j, mine, 0.0).reshape(logits.shape)
        return carry

    lax.fori_loop(0, (most + chunk - 1) // chunk, step, 0)


def score_kernel(block, got, user, codes, scores, tiles, tables):
    sources = got.shape[0]
    requests = user.shape[0]
    subs, count = codes.shape
    tiles[...] = got[...].astype(F32).reshape(sources * MSG, LANES)
    book = [tiles[pl.ds(i, sources, stride=MSG), :].astype(BF16) for i in range(CB_ROWS)]
    even = jnp.concatenate(book[:2], axis=1)
    odd = jnp.concatenate(book[2:], axis=1)
    d_user = user.shape[1]
    column = iota((d_user, sources), 0)
    people = user[...]
    of_even = dot(people, as_bf16(column == 2 * iota((d_user, sources), 1))).astype(BF16)
    of_odd = dot(people, as_bf16(column == 2 * iota((d_user, sources), 1) + 1)).astype(BF16)
    per_sub = sources // subs
    for m in range(subs):
        mine = iota((requests, sources), 1) // per_sub == m
        zero = jnp.zeros((), BF16)
        table = dot(jnp.where(mine, of_even, zero), even) + dot(jnp.where(mine, of_odd, zero), odd)
        tables[:, m * 256 : (m + 1) * 256] = table.astype(BF16)

    code = lax.broadcasted_iota(jnp.int16, (256, block), 0)

    def step(j, carry):
        at = pl.ds(pl.multiple_of(j * block, block), block)
        total = jnp.zeros((requests, block), F32)
        for m in range(subs):
            now = jnp.broadcast_to(codes[m : m + 1, at], (16, block)).astype(jnp.int16)
            now = jnp.concatenate([now] * 16, axis=0)
            onehot = jnp.where(code == now, jnp.ones((), BF16), jnp.zeros((), BF16))
            total = total + dot(tables[:, m * 256 : (m + 1) * 256], onehot)
        scores[:, at] = total
        return carry

    lax.fori_loop(0, count // block, step, 0)


def collect_kernel(back, meta, logits):
    cand_dev, requests = logits.shape
    total = meta.shape[0]
    owners = back.shape[0]
    lane = iota((total, owners), 1)
    answers = back[...].reshape(owners, LANES)
    pick = as_bf16(meta[:, 0:1] == lane)
    top = answers.astype(BF16)
    rest = answers - top.astype(F32)
    middle = rest.astype(BF16)
    last = (rest - middle.astype(F32)).astype(BF16)
    rows = dot(pick, top) + dot(pick, middle) + dot(pick, last)
    value = lane_sum(jnp.where(meta[:, 1:2] == lane, rows, 0.0))
    diagonal = iota((total, requests), 0) % requests == iota((total, requests), 1)
    spread = jnp.where(diagonal, value, 0.0)
    logits[...] = jnp.sum(spread.reshape(cand_dev, requests, requests), axis=1)


def on_device(
    user_emb,
    codebooks,
    item_codes,
    item_place,
    candidates,
    item_features,
    cross_weights,
    cross_bias,
    out_weight,
):
    requests, d_user = user_emb.shape
    cand_dev = candidates.shape[1]
    total = requests * cand_dev
    owners = lax.axis_size("item") * lax.axis_size("req")
    items = item_codes.shape[0]
    layers, width, _ = cross_weights.shape
    limit = pltpu.CompilerParams(vmem_limit_bytes=48 << 20)
    message, meta = pl.pallas_call(
        prepare_kernel,
        out_shape=(
            jax.ShapeDtypeStruct((owners, MSG, LANES), BF16),
            jax.ShapeDtypeStruct((total, LANES), I32),
        ),
        in_specs=[VMEM] * 4,
        out_specs=(VMEM, VMEM),
        scratch_shapes=[pltpu.VMEM((owners * MSG, LANES), F32)],
        compiler_params=limit,
        name="prepare",
    )(
        candidates.T,
        item_place.reshape(-1, LANES),
        jnp.swapaxes(codebooks, 1, 2)[0],
        user_emb,
    )
    got = lax.all_to_all(message, ("item", "req"), split_axis=0, concat_axis=0, tiled=True)
    chunk = 2
    rows = chunk * owners
    answers = pl.pallas_call(
        functools.partial(rank_kernel, chunk),
        out_shape=jax.ShapeDtypeStruct((owners, 1, LANES), F32),
        in_specs=[VMEM] * 5,
        out_specs=VMEM,
        scratch_shapes=[
            pltpu.VMEM((owners * MSG, LANES), F32),
            pltpu.VMEM((rows, width), BF16),
            pltpu.VMEM((rows, width), BF16),
            pltpu.VMEM((rows, width), F32),
        ],
        compiler_params=limit,
        name="rank",
    )(got, item_features, cross_weights, cross_bias, out_weight.reshape(1, width))
    back = lax.all_to_all(answers, ("item", "req"), split_axis=0, concat_axis=0, tiled=True)
    scores = pl.pallas_call(
        functools.partial(score_kernel, 512),
        out_shape=jax.ShapeDtypeStruct((requests, items), F32),
        in_specs=[VMEM] * 3,
        out_specs=VMEM,
        scratch_shapes=[
            pltpu.VMEM((owners * MSG, LANES), F32),
            pltpu.VMEM((requests, item_codes.shape[1] * 256), BF16),
        ],
        compiler_params=limit,
        name="scores",
        cost_estimate=pl.CostEstimate(flops=2 << 30, bytes_accessed=40 << 20, transcendentals=0),
    )(got, user_emb, item_codes.T)
    logits = pl.pallas_call(
        collect_kernel,
        out_shape=jax.ShapeDtypeStruct((cand_dev, requests), F32),
        in_specs=[VMEM] * 2,
        out_specs=VMEM,
        compiler_params=limit,
        name="collect",
    )(back, meta)
    return scores, logits.T


def solution(mesh):
    placed = (
        P("req", None),
        P("item", None, None),
        P("item", None),
        P(),
        P("req", "item"),
        P(("item", "req"), None),
        P(),
        P(),
        P(),
    )
    return jax.shard_map(
        on_device,
        mesh=mesh,
        in_specs=placed,
        out_specs=(P("req", "item"), P("req", "item")),
        check_vma=False,
    )
```

```python
import functools

import jax
import jax.numpy as jnp
from jax import lax
from jax.experimental import pallas as pl
from jax.experimental.pallas import tpu as pltpu
from jax.sharding import PartitionSpec as P

F32 = jnp.float32
BF16 = jnp.bfloat16
I32 = jnp.int32
HBM = pl.BlockSpec(memory_space=pltpu.HBM)
VMEM = pl.BlockSpec(memory_space=pltpu.VMEM)
LANES = 128
MSG = 8
CB_ROWS = 4
USER_ROW = 4
WANT_ROW = 6
HALF = 64


def dot(a, b, dims=(((1,), (0,)), ((), ()))):
    return lax.dot_general(a, b, dims, preferred_element_type=F32)


def iota(shape, axis):
    return lax.broadcasted_iota(I32, shape, axis)


def lane_sum(x):
    return jnp.sum(x, axis=1, keepdims=True)


def as_bf16(mask):
    return jnp.where(mask, 1.0, 0.0).astype(BF16)


def prepare_kernel(
    cand_in, place_in, codebook_in, user_in, message, meta, tiles, cand, place, codebook, user, sems
):
    pairs = ((cand_in, cand), (place_in, place), (codebook_in, codebook), (user_in, user))
    copies = [pltpu.make_async_copy(a, b, sems.at[i]) for i, (a, b) in enumerate(pairs)]
    for copy in copies:
        copy.start()
    for copy in copies:
        copy.wait()
    cand_dev, requests = cand.shape
    total = cand_dev * requests
    owners = message.shape[0]
    blocks = place.shape[0]
    item = lax.axis_index("item")
    req = lax.axis_index("req")
    ids = cand[...].astype(F32)
    spread = jnp.concatenate(
        [jnp.broadcast_to(ids[c : c + 1, :], (requests, requests)) for c in range(cand_dev)], axis=0
    )
    own_request = iota((total, requests), 0) % requests
    diagonal = own_request == iota((total, requests), 1)
    ids = lane_sum(jnp.where(diagonal, spread, 0.0)).astype(I32)
    where_row = as_bf16((ids >> 7) == iota((total, blocks), 1))
    stored = place[...]
    parts = jnp.concatenate(
        [
            (stored & 255).astype(F32).astype(BF16),
            ((stored >> 8) & 255).astype(F32).astype(BF16),
            (stored >> 16).astype(F32).astype(BF16),
        ],
        axis=1,
    )
    found = dot(where_row, parts)
    found = found[:, :LANES] + 256.0 * found[:, LANES : 2 * LANES] + 65536.0 * found[:, 2 * LANES :]
    lane = iota((total, LANES), 1)
    slot = lane_sum(jnp.where((ids & 127) == lane, found, 0.0)).astype(I32)
    rows_dev = blocks * LANES // owners
    shift = rows_dev.bit_length() - 1
    owner = slot >> shift
    within = slot & (rows_dev - 1)
    hit = owner == lane
    hits = as_bf16(hit)
    earlier = as_bf16(iota((total, total), 1) < iota((total, total), 0))
    rank = lane_sum(jnp.where(hit, dot(earlier, hits), 0.0)).astype(I32)
    meta[...] = jnp.where(lane == 0, owner, rank)
    request = iota((total, 1), 0) % requests
    low = (within & 255).astype(F32)
    high = ((within >> 8) + 4 * request + 128).astype(F32)
    entry = jnp.where(lane == rank, low, 0.0) + jnp.where(lane == rank + HALF, high, 0.0)
    wanted = dot(hits, entry.astype(BF16), (((0,), (0,)), ((), ())))
    book = codebook[...].astype(F32)
    sub = iota(book.shape, 0)
    first = jnp.sum(jnp.where(sub == 2 * req, book, 0.0), axis=0, keepdims=True)
    second = jnp.sum(jnp.where(sub == 2 * req + 1, book, 0.0), axis=0, keepdims=True)
    people = user[...].astype(F32)
    person = jnp.sum(jnp.where(iota(people.shape, 0) == item, people, 0.0), axis=0, keepdims=True)
    tile = jnp.concatenate(
        [
            first[:, :LANES],
            first[:, LANES:],
            second[:, :LANES],
            second[:, LANES:],
            person[:, :LANES],
            person[:, LANES:],
            jnp.zeros((2, LANES), F32),
        ],
        axis=0,
    )
    tiles[...] = jnp.broadcast_to(tile[None], (owners, MSG, LANES)).reshape(owners * MSG, LANES)
    tiles[pl.ds(WANT_ROW, owners, stride=MSG), :] = wanted
    message[...] = tiles[...].reshape(owners, MSG, LANES).astype(BF16)


def rank_kernel(
    chunk,
    block,
    got_in,
    items_in,
    weights_in,
    bias_in,
    out_weight_in,
    logits,
    got,
    items,
    weights,
    bias,
    out_weight,
    tiles,
    first,
    rounded,
    state,
    sems,
):
    pairs = [(got_in, got), (items_in, items), (bias_in, bias), (out_weight_in, out_weight)]
    pairs += [(weights_in.at[i], weights.at[i]) for i in range(weights.shape[0])]
    copies = [pltpu.make_async_copy(a, b, sems.at[i]) for i, (a, b) in enumerate(pairs)]
    for copy in copies:
        copy.start()
    copies[0].wait()
    sources = got.shape[0]
    halves = 2
    per = chunk // halves
    rows = per * sources
    width = state.shape[1]
    layers = weights.shape[0]
    features = items.shape[1]
    d_user = width - features
    tiles[...] = got[...].astype(F32).reshape(sources * MSG, LANES)
    wanted = tiles[pl.ds(WANT_ROW, sources, stride=MSG), :]
    people = jnp.concatenate(
        [tiles[pl.ds(USER_ROW + i, sources, stride=MSG), :] for i in range(2)], axis=1
    ).astype(BF16)
    lane = iota((sources, LANES), 1)
    high_lane = (lane >= HALF) & (wanted > 0.0)
    most = jnp.max(jnp.where(high_lane, lane - HALF + 1, 0))
    reqs = lax.axis_size("req")
    logits[...] = jnp.zeros(logits.shape, F32)
    source = iota((rows, 1), 0) % sources

    def arrive(t, some):
        @pl.when(t == 0)
        def _():
            for copy in some:
                copy.wait()

    def step(t, carry):
        arrive(t, copies[1:4])
        for h in range(halves):
            at = slice(h * rows, (h + 1) * rows)
            lows, highs = [], []
            for k in range(per):
                j = t * chunk + h * per + k
                lows.append(lane_sum(jnp.where(lane == j, wanted, 0.0)))
                highs.append(lane_sum(jnp.where(lane == j + HALF, wanted, 0.0)))
            low = jnp.concatenate(lows, axis=0).astype(I32)
            high = jnp.concatenate(highs, axis=0).astype(I32)
            within = low + 256 * (high & 3)
            person = ((high >> 2) & 31) * reqs + source % reqs
            pick_user = as_bf16(person == iota((rows, sources), 1))
            pick_item = as_bf16(within == iota((rows, items.shape[0]), 1))
            first[at, :d_user] = dot(pick_user, people).astype(BF16)
            for n in range(0, features, block):
                first[at, d_user + n : d_user + n + block] = dot(
                    pick_item, items[:, n : n + block]
                ).astype(BF16)
        parts = [jnp.zeros((rows, LANES), F32) for _ in range(halves)]
        for layer in range(layers):
            if layer < 2:
                arrive(t, copies[4:5] if layer == 0 else copies[5:])
            for h in range(halves):
                at = slice(h * rows, (h + 1) * rows)
                left = first[at, :] if layer == 0 else rounded[(layer + 1) % 2, at, :]
                for n in range(0, width, block):
                    to = slice(n, n + block)
                    product = dot(left, weights[layer, :, to]) + bias[layer : layer + 1, to]
                    start = first[at, to].astype(F32)
                    new = start * product + (start if layer == 0 else state[at, to])
                    if layer < layers - 1:
                        state[at, to] = new
                        rounded[layer % 2, at, to] = new.astype(BF16)
                    else:
                        new = new * out_weight[:, to]
                        for i in range(0, block, LANES):
                            parts[h] = parts[h] + new[:, i : i + LANES]
        for h in range(halves):
            value = lane_sum(parts[h])
            for k in range(per):
                j = t * chunk + h * per + k
                mine = value[k * sources : (k + 1) * sources]
                logits[...] += jnp.where(lane == j, mine, 0.0).reshape(logits.shape)
        return carry

    lax.fori_loop(0, jnp.maximum((most + chunk - 1) // chunk, 1), step, 0)


def score_kernel(block, got, user, codes, scores, tiles, tables):
    sources = got.shape[0]
    requests = user.shape[0]
    subs, count = codes.shape
    tiles[...] = got[...].astype(F32).reshape(sources * MSG, LANES)
    book = [tiles[pl.ds(i, sources, stride=MSG), :].astype(BF16) for i in range(CB_ROWS)]
    even = jnp.concatenate(book[:2], axis=1)
    odd = jnp.concatenate(book[2:], axis=1)
    d_user = user.shape[1]
    column = iota((d_user, sources), 0)
    people = user[...]
    of_even = dot(people, as_bf16(column == 2 * iota((d_user, sources), 1))).astype(BF16)
    of_odd = dot(people, as_bf16(column == 2 * iota((d_user, sources), 1) + 1)).astype(BF16)
    per_sub = sources // subs
    for m in range(subs):
        mine = iota((requests, sources), 1) // per_sub == m
        zero = jnp.zeros((), BF16)
        table = dot(jnp.where(mine, of_even, zero), even) + dot(jnp.where(mine, of_odd, zero), odd)
        tables[:, m * 256 : (m + 1) * 256] = table.astype(BF16)

    code = lax.broadcasted_iota(jnp.int16, (256, block), 0)

    def step(j, carry):
        at = pl.ds(pl.multiple_of(j * block, block), block)
        total = jnp.zeros((requests, block), F32)
        for m in range(subs):
            now = jnp.broadcast_to(codes[m : m + 1, at], (16, block)).astype(jnp.int16)
            now = jnp.concatenate([now] * 16, axis=0)
            onehot = jnp.where(code == now, jnp.ones((), BF16), jnp.zeros((), BF16))
            total = total + dot(tables[:, m * 256 : (m + 1) * 256], onehot)
        scores[:, at] = total
        return carry

    lax.fori_loop(0, count // block, step, 0)


def collect_kernel(back, meta, logits):
    cand_dev, requests = logits.shape
    total = meta.shape[0]
    owners = back.shape[0]
    lane = iota((total, owners), 1)
    answers = back[...].reshape(owners, LANES)
    pick = as_bf16(meta[:, 0:1] == lane)
    top = answers.astype(BF16)
    rest = answers - top.astype(F32)
    middle = rest.astype(BF16)
    last = (rest - middle.astype(F32)).astype(BF16)
    rows = dot(pick, top) + dot(pick, middle) + dot(pick, last)
    value = lane_sum(jnp.where(meta[:, 1:2] == lane, rows, 0.0))
    diagonal = iota((total, requests), 0) % requests == iota((total, requests), 1)
    spread = jnp.where(diagonal, value, 0.0)
    logits[...] = jnp.sum(spread.reshape(cand_dev, requests, requests), axis=1)


def on_device(
    user_emb,
    codebooks,
    item_codes,
    item_place,
    candidates,
    item_features,
    cross_weights,
    cross_bias,
    out_weight,
):
    requests, d_user = user_emb.shape
    cand_dev = candidates.shape[1]
    total = requests * cand_dev
    owners = lax.axis_size("item") * lax.axis_size("req")
    items = item_codes.shape[0]
    layers, width, _ = cross_weights.shape
    whole = pltpu.CompilerParams(vmem_limit_bytes=60 << 20)
    limit = pltpu.CompilerParams(vmem_limit_bytes=24 << 20)
    message, meta = pl.pallas_call(
        prepare_kernel,
        out_shape=(
            jax.ShapeDtypeStruct((owners, MSG, LANES), BF16),
            jax.ShapeDtypeStruct((total, LANES), I32),
        ),
        in_specs=[HBM] * 4,
        out_specs=(VMEM, VMEM),
        scratch_shapes=[
            pltpu.VMEM((owners * MSG, LANES), F32),
            pltpu.VMEM((cand_dev, requests), I32),
            pltpu.VMEM((item_place.shape[0] // LANES, LANES), I32),
            pltpu.VMEM(codebooks.shape[:0:-1], BF16),
            pltpu.VMEM(user_emb.shape, BF16),
            pltpu.SemaphoreType.DMA((4,)),
        ],
        compiler_params=whole,
        name="prepare",
    )(
        candidates.T,
        item_place.reshape(-1, LANES),
        jnp.swapaxes(codebooks, 1, 2)[0],
        user_emb,
    )
    got = lax.all_to_all(message, ("item", "req"), split_axis=0, concat_axis=0, tiled=True)
    chunk = 4
    rows = chunk * owners
    answers = pl.pallas_call(
        functools.partial(rank_kernel, chunk, 256),
        out_shape=jax.ShapeDtypeStruct((owners, 1, LANES), F32),
        in_specs=[HBM] * 5,
        out_specs=VMEM,
        scratch_shapes=[
            pltpu.VMEM((owners, MSG, LANES), BF16),
            pltpu.VMEM(item_features.shape, BF16),
            pltpu.VMEM(cross_weights.shape, BF16),
            pltpu.VMEM(cross_bias.shape, F32),
            pltpu.VMEM((1, width), F32),
            pltpu.VMEM((owners * MSG, LANES), F32),
            pltpu.VMEM((rows, width), BF16),
            pltpu.VMEM((2, rows, width), BF16),
            pltpu.VMEM((rows, width), F32),
            pltpu.SemaphoreType.DMA((4 + layers,)),
        ],
        compiler_params=whole,
        name="rank",
        cost_estimate=pl.CostEstimate(flops=12 << 30, bytes_accessed=10 << 20, transcendentals=0),
    )(got, item_features, cross_weights, cross_bias, out_weight.reshape(1, width))
    back = lax.all_to_all(answers, ("item", "req"), split_axis=0, concat_axis=0, tiled=True)
    scores = pl.pallas_call(
        functools.partial(score_kernel, 512),
        out_shape=jax.ShapeDtypeStruct((requests, items), F32),
        in_specs=[VMEM] * 3,
        out_specs=VMEM,
        scratch_shapes=[
            pltpu.VMEM((owners * MSG, LANES), F32),
            pltpu.VMEM((requests, item_codes.shape[1] * 256), BF16),
        ],
        compiler_params=limit,
        name="scores",
        cost_estimate=pl.CostEstimate(flops=2 << 30, bytes_accessed=40 << 20, transcendentals=0),
    )(got, user_emb, item_codes.T)
    logits = pl.pallas_call(
        collect_kernel,
        out_shape=jax.ShapeDtypeStruct((cand_dev, requests), F32),
        in_specs=[VMEM] * 2,
        out_specs=VMEM,
        compiler_params=limit,
        name="collect",
    )(back, meta)
    return scores, logits.T


def solution(mesh):
    placed = (
        P("req", None),
        P("item", None, None),
        P("item", None),
        P(),
        P("req", "item"),
        P(("item", "req"), None),
        P(),
        P(),
        P(),
    )
    return jax.shard_map(
        on_device,
        mesh=mesh,
        in_specs=placed,
        out_specs=(P("req", "item"), P("req", "item")),
        check_vma=False,
    )
```

```python
import functools

import jax
import jax.numpy as jnp
from jax import lax
from jax.experimental import pallas as pl
from jax.experimental.pallas import tpu as pltpu
from jax.sharding import PartitionSpec as P

F32 = jnp.float32
BF16 = jnp.bfloat16
I32 = jnp.int32
HBM = pl.BlockSpec(memory_space=pltpu.HBM)
VMEM = pl.BlockSpec(memory_space=pltpu.VMEM)
LANES = 128
MSG = 8
CB_ROWS = 4
USER_ROW = 4
WANT_ROW = 6
HALF = 64
CODES = 256


def dot(a, b, dims=(((1,), (0,)), ((), ()))):
    return lax.dot_general(a, b, dims, preferred_element_type=F32)


def iota(shape, axis):
    return lax.broadcasted_iota(I32, shape, axis)


def lane_sum(x):
    return jnp.sum(x, axis=1, keepdims=True)


def as_bf16(mask):
    return jnp.where(mask, 1.0, 0.0).astype(BF16)


def prepare_kernel(
    cand_in, place_in, codebook_in, user_in, message, meta, tiles, cand, place, codebook, user, sems
):
    pairs = ((cand_in, cand), (place_in, place), (codebook_in, codebook), (user_in, user))
    copies = [pltpu.make_async_copy(a, b, sems.at[i]) for i, (a, b) in enumerate(pairs)]
    for copy in copies:
        copy.start()
    for copy in copies:
        copy.wait()
    cand_dev, requests = cand.shape
    total = cand_dev * requests
    owners = message.shape[0]
    blocks = place.shape[0]
    item = lax.axis_index("item")
    req = lax.axis_index("req")
    ids = cand[...].astype(F32)
    spread = jnp.concatenate(
        [jnp.broadcast_to(ids[c : c + 1, :], (requests, requests)) for c in range(cand_dev)], axis=0
    )
    own_request = iota((total, requests), 0) % requests
    diagonal = own_request == iota((total, requests), 1)
    ids = lane_sum(jnp.where(diagonal, spread, 0.0)).astype(I32)
    where_row = as_bf16((ids >> 7) == iota((total, blocks), 1))
    stored = place[...]
    parts = jnp.concatenate(
        [
            (stored & 255).astype(F32).astype(BF16),
            ((stored >> 8) & 255).astype(F32).astype(BF16),
            (stored >> 16).astype(F32).astype(BF16),
        ],
        axis=1,
    )
    found = dot(where_row, parts)
    found = found[:, :LANES] + 256.0 * found[:, LANES : 2 * LANES] + 65536.0 * found[:, 2 * LANES :]
    lane = iota((total, LANES), 1)
    slot = lane_sum(jnp.where((ids & 127) == lane, found, 0.0)).astype(I32)
    rows_dev = blocks * LANES // owners
    shift = rows_dev.bit_length() - 1
    owner = slot >> shift
    within = slot & (rows_dev - 1)
    hit = owner == lane
    hits = as_bf16(hit)
    earlier = as_bf16(iota((total, total), 1) < iota((total, total), 0))
    rank = lane_sum(jnp.where(hit, dot(earlier, hits), 0.0)).astype(I32)
    meta[...] = jnp.where(lane == 0, owner, rank)
    request = iota((total, 1), 0) % requests
    low = (within & 255).astype(F32)
    high = ((within >> 8) + 4 * request + 128).astype(F32)
    entry = jnp.where(lane == rank, low, 0.0) + jnp.where(lane == rank + HALF, high, 0.0)
    wanted = dot(hits, entry.astype(BF16), (((0,), (0,)), ((), ())))
    book = codebook[...].astype(F32)
    sub = iota(book.shape, 0)
    first = jnp.sum(jnp.where(sub == 2 * req, book, 0.0), axis=0, keepdims=True)
    second = jnp.sum(jnp.where(sub == 2 * req + 1, book, 0.0), axis=0, keepdims=True)
    people = user[...].astype(F32)
    person = jnp.sum(jnp.where(iota(people.shape, 0) == item, people, 0.0), axis=0, keepdims=True)
    tile = jnp.concatenate(
        [
            first[:, :LANES],
            first[:, LANES:],
            second[:, :LANES],
            second[:, LANES:],
            person[:, :LANES],
            person[:, LANES:],
            jnp.zeros((2, LANES), F32),
        ],
        axis=0,
    )
    tiles[...] = jnp.broadcast_to(tile[None], (owners, MSG, LANES)).reshape(owners * MSG, LANES)
    tiles[pl.ds(WANT_ROW, owners, stride=MSG), :] = wanted
    message[...] = tiles[...].reshape(owners, MSG, LANES).astype(BF16)


def rank_kernel(
    chunk,
    block,
    got_in,
    items_in,
    weights_in,
    bias_in,
    out_weight_in,
    logits,
    got,
    items,
    weights,
    bias,
    out_weight,
    tiles,
    first,
    rounded,
    state,
    answer,
    sems,
):
    pairs = [(got_in, got), (items_in, items), (bias_in, bias), (out_weight_in, out_weight)]
    pairs += [(weights_in.at[i], weights.at[i]) for i in range(weights.shape[0])]
    copies = [pltpu.make_async_copy(a, b, sems.at[i]) for i, (a, b) in enumerate(pairs)]
    for copy in copies:
        copy.start()
    copies[0].wait()
    sources = got.shape[0]
    halves = 2
    per = chunk // halves
    rows = per * sources
    width = state.shape[1]
    layers = weights.shape[0]
    features = items.shape[1]
    d_user = width - features
    tiles[...] = got[...].astype(F32).reshape(sources * MSG, LANES)
    wanted = tiles[pl.ds(WANT_ROW, sources, stride=MSG), :]
    people = jnp.concatenate(
        [tiles[pl.ds(USER_ROW + i, sources, stride=MSG), :] for i in range(2)], axis=1
    ).astype(BF16)
    lane = iota((sources, LANES), 1)
    high_lane = (lane >= HALF) & (wanted > 0.0)
    most = jnp.max(jnp.where(high_lane, lane - HALF + 1, 0))
    reqs = lax.axis_size("req")
    answer[...] = jnp.zeros(answer.shape, F32)
    source = iota((rows, 1), 0) % sources

    def arrive(t, some):
        @pl.when(t == 0)
        def _():
            for copy in some:
                copy.wait()

    def step(t, carry):
        arrive(t, copies[1:4])
        for h in range(halves):
            at = slice(h * rows, (h + 1) * rows)
            lows, highs = [], []
            for k in range(per):
                j = t * chunk + h * per + k
                lows.append(lane_sum(jnp.where(lane == j, wanted, 0.0)))
                highs.append(lane_sum(jnp.where(lane == j + HALF, wanted, 0.0)))
            low = jnp.concatenate(lows, axis=0).astype(I32)
            high = jnp.concatenate(highs, axis=0).astype(I32)
            within = low + 256 * (high & 3)
            person = ((high >> 2) & 31) * reqs + source % reqs
            pick_user = as_bf16(person == iota((rows, sources), 1))
            pick_item = as_bf16(within == iota((rows, items.shape[0]), 1))
            first[at, :d_user] = dot(pick_user, people).astype(BF16)
            for n in range(0, features, block):
                first[at, d_user + n : d_user + n + block] = dot(
                    pick_item, items[:, n : n + block]
                ).astype(BF16)
        parts = [jnp.zeros((rows, LANES), F32) for _ in range(halves)]
        for layer in range(layers):
            if layer < 2:
                arrive(t, copies[4:5] if layer == 0 else copies[5:])
            for h in range(halves):
                at = slice(h * rows, (h + 1) * rows)
                left = first[at, :] if layer == 0 else rounded[(layer + 1) % 2, at, :]
                for n in range(0, width, block):
                    to = slice(n, n + block)
                    product = dot(left, weights[layer, :, to]) + bias[layer : layer + 1, to]
                    start = first[at, to].astype(F32)
                    new = start * product + (start if layer == 0 else state[at, to])
                    if layer < layers - 1:
                        state[at, to] = new
                        rounded[layer % 2, at, to] = new.astype(BF16)
                    else:
                        new = new * out_weight[:, to]
                        for i in range(0, block, LANES):
                            parts[h] = parts[h] + new[:, i : i + LANES]
        for h in range(halves):
            value = lane_sum(parts[h])
            for k in range(per):
                j = t * chunk + h * per + k
                mine = value[k * sources : (k + 1) * sources]
                answer[...] += jnp.where(lane == j, mine, 0.0)
        return carry

    lax.fori_loop(0, jnp.maximum((most + chunk - 1) // chunk, 1), step, 0)
    logits[...] = answer[...].reshape(logits.shape)


def score_kernel(block, looked, got, user, codes, scores, tiles, tables, wide):
    sources = got.shape[0]
    requests, d_user = user.shape
    subs, count = codes.shape
    tiles[...] = got[...].astype(F32).reshape(sources * MSG, LANES)
    book = [tiles[pl.ds(i, sources, stride=MSG), :].astype(BF16) for i in range(CB_ROWS)]
    even = jnp.concatenate(book[:2], axis=1)
    odd = jnp.concatenate(book[2:], axis=1)
    column = iota((d_user, sources), 0)
    people = user[...]
    of_even = dot(people, as_bf16(column == 2 * iota((d_user, sources), 1))).astype(BF16)
    of_odd = dot(people, as_bf16(column == 2 * iota((d_user, sources), 1) + 1)).astype(BF16)
    per_sub = sources // subs
    zero = jnp.zeros((), BF16)
    for m in range(subs):
        mine = iota((requests, sources), 1) // per_sub == m
        table = dot(jnp.where(mine, of_even, zero), even) + dot(jnp.where(mine, of_odd, zero), odd)
        table = table.astype(BF16)
        if m < looked:
            wide[m] = table.astype(F32)
        else:
            tables[:, m * CODES : (m + 1) * CODES] = table

    code = lax.broadcasted_iota(jnp.int16, (CODES, block), 0)
    one = jnp.ones((), BF16)
    groups, spans = requests // 8, block // LANES
    order = sorted(
        [((i + 0.5) / looked, i) for i in range(looked)]
        + [((i + 0.5) / (subs - looked), i + looked) for i in range(subs - looked)]
    )

    def pick(values, index):
        return jnp.take_along_axis(values, index, axis=1, mode="promise_in_bounds")

    def step(j, carry):
        at = pl.ds(pl.multiple_of(j * block, block), block)
        total = jnp.zeros((requests, block), F32)
        sums = [[jnp.zeros((8, LANES), F32) for _ in range(spans)] for _ in range(groups)]
        for _, m in order:
            row = codes[m : m + 1, at]
            if m >= looked:
                now = jnp.broadcast_to(row, (16, block)).astype(jnp.int16)
                now = jnp.concatenate([now] * (CODES // 16), axis=0)
                onehot = jnp.where(code == now, one, zero)
                total = total + dot(tables[:, m * CODES : (m + 1) * CODES], onehot)
                continue
            for b in range(spans):
                now = jnp.broadcast_to(row[:, b * LANES : (b + 1) * LANES], (8, LANES))
                index = now & (LANES - 1)
                upper = now >= LANES
                for g in range(groups):
                    low = pick(wide[m, g * 8 : (g + 1) * 8, :LANES], index)
                    high = pick(wide[m, g * 8 : (g + 1) * 8, LANES:], index)
                    sums[g][b] = sums[g][b] + jnp.where(upper, high, low)
        rows = [jnp.concatenate(group, axis=1) for group in sums]
        scores[:, at] = total + jnp.concatenate(rows, axis=0)
        return carry

    lax.fori_loop(0, count // block, step, 0)


def collect_kernel(back, meta, logits):
    cand_dev, requests = logits.shape
    total = meta.shape[0]
    owners = back.shape[0]
    lane = iota((total, owners), 1)
    answers = back[...].reshape(owners, LANES)
    pick = as_bf16(meta[:, 0:1] == lane)
    top = answers.astype(BF16)
    rest = answers - top.astype(F32)
    middle = rest.astype(BF16)
    last = (rest - middle.astype(F32)).astype(BF16)
    rows = dot(pick, top) + dot(pick, middle) + dot(pick, last)
    value = lane_sum(jnp.where(meta[:, 1:2] == lane, rows, 0.0))
    diagonal = iota((total, requests), 0) % requests == iota((total, requests), 1)
    spread = jnp.where(diagonal, value, 0.0)
    logits[...] = jnp.sum(spread.reshape(cand_dev, requests, requests), axis=1)


def on_device(
    user_emb,
    codebooks,
    item_codes,
    item_place,
    candidates,
    item_features,
    cross_weights,
    cross_bias,
    out_weight,
):
    requests, d_user = user_emb.shape
    cand_dev = candidates.shape[1]
    total = requests * cand_dev
    owners = lax.axis_size("item") * lax.axis_size("req")
    items = item_codes.shape[0]
    layers, width, _ = cross_weights.shape
    whole = pltpu.CompilerParams(vmem_limit_bytes=60 << 20)
    limit = pltpu.CompilerParams(vmem_limit_bytes=24 << 20)
    message, meta = pl.pallas_call(
        prepare_kernel,
        out_shape=(
            jax.ShapeDtypeStruct((owners, MSG, LANES), BF16),
            jax.ShapeDtypeStruct((total, LANES), I32),
        ),
        in_specs=[HBM] * 4,
        out_specs=(VMEM, VMEM),
        scratch_shapes=[
            pltpu.VMEM((owners * MSG, LANES), F32),
            pltpu.VMEM((cand_dev, requests), I32),
            pltpu.VMEM((item_place.shape[0] // LANES, LANES), I32),
            pltpu.VMEM(codebooks.shape[:0:-1], BF16),
            pltpu.VMEM(user_emb.shape, BF16),
            pltpu.SemaphoreType.DMA((4,)),
        ],
        compiler_params=whole,
        name="prepare",
    )(
        candidates.T,
        item_place.reshape(-1, LANES),
        jnp.swapaxes(codebooks, 1, 2)[0],
        user_emb,
    )
    got = lax.all_to_all(message, ("item", "req"), split_axis=0, concat_axis=0, tiled=True)
    chunk = 4
    rows = chunk * owners
    answers = pl.pallas_call(
        functools.partial(rank_kernel, chunk, 256),
        out_shape=jax.ShapeDtypeStruct((owners, 1, LANES), F32),
        in_specs=[HBM] * 5,
        out_specs=VMEM,
        scratch_shapes=[
            pltpu.VMEM((owners, MSG, LANES), BF16),
            pltpu.VMEM(item_features.shape, BF16),
            pltpu.VMEM(cross_weights.shape, BF16),
            pltpu.VMEM(cross_bias.shape, F32),
            pltpu.VMEM((1, width), F32),
            pltpu.VMEM((owners * MSG, LANES), F32),
            pltpu.VMEM((rows, width), BF16),
            pltpu.VMEM((2, rows, width), BF16),
            pltpu.VMEM((rows, width), F32),
            pltpu.VMEM((owners, LANES), F32),
            pltpu.SemaphoreType.DMA((4 + layers,)),
        ],
        compiler_params=whole,
        name="rank",
        cost_estimate=pl.CostEstimate(flops=12 << 30, bytes_accessed=10 << 20, transcendentals=0),
    )(got, item_features, cross_weights, cross_bias, out_weight.reshape(1, width))
    back = lax.all_to_all(answers, ("item", "req"), split_axis=0, concat_axis=0, tiled=True)
    looked = 14
    scores = pl.pallas_call(
        functools.partial(score_kernel, 512, looked),
        out_shape=jax.ShapeDtypeStruct((requests, items), F32),
        in_specs=[VMEM] * 3,
        out_specs=VMEM,
        scratch_shapes=[
            pltpu.VMEM((owners * MSG, LANES), F32),
            pltpu.VMEM((requests, item_codes.shape[1] * CODES), BF16),
            pltpu.VMEM((looked, requests, CODES), F32),
        ],
        compiler_params=limit,
        name="scores",
        cost_estimate=pl.CostEstimate(flops=2 << 30, bytes_accessed=40 << 20, transcendentals=0),
    )(got, user_emb, item_codes.T)
    logits = pl.pallas_call(
        collect_kernel,
        out_shape=jax.ShapeDtypeStruct((cand_dev, requests), F32),
        in_specs=[VMEM] * 2,
        out_specs=VMEM,
        compiler_params=limit,
        name="collect",
    )(back, meta)
    return scores, logits.T


def solution(mesh):
    placed = (
        P("req", None),
        P("item", None, None),
        P("item", None),
        P(),
        P("req", "item"),
        P(("item", "req"), None),
        P(),
        P(),
        P(),
    )
    return jax.shard_map(
        on_device,
        mesh=mesh,
        in_specs=placed,
        out_specs=(P("req", "item"), P("req", "item")),
        check_vma=False,
    )
```

```python
import functools

import jax
import jax.numpy as jnp
from jax import lax
from jax.experimental import pallas as pl
from jax.experimental.pallas import tpu as pltpu
from jax.sharding import PartitionSpec as P

F32 = jnp.float32
BF16 = jnp.bfloat16
I32 = jnp.int32
HBM = pl.BlockSpec(memory_space=pltpu.HBM)
VMEM = pl.BlockSpec(memory_space=pltpu.VMEM)
LANES = 128
MSG = 8
CB_ROWS = 4
USER_ROW = 4
WANT_ROW = 6
HALF = 64
CODES = 256


def dot(a, b, dims=(((1,), (0,)), ((), ()))):
    return lax.dot_general(a, b, dims, preferred_element_type=F32)


def iota(shape, axis):
    return lax.broadcasted_iota(I32, shape, axis)


def lane_sum(x):
    return jnp.sum(x, axis=1, keepdims=True)


def as_bf16(mask):
    return jnp.where(mask, 1.0, 0.0).astype(BF16)


def prepare_kernel(
    cand_in, place_in, codebook_in, user_in, message, meta, tiles, cand, place, codebook, user, sems
):
    pairs = ((cand_in, cand), (place_in, place), (codebook_in, codebook), (user_in, user))
    copies = [pltpu.make_async_copy(a, b, sems.at[i]) for i, (a, b) in enumerate(pairs)]
    for copy in copies:
        copy.start()
    for copy in copies:
        copy.wait()
    cand_dev, requests = cand.shape
    total = cand_dev * requests
    owners = message.shape[0]
    blocks = place.shape[0]
    item = lax.axis_index("item")
    req = lax.axis_index("req")
    ids = cand[...].astype(F32)
    spread = jnp.concatenate(
        [jnp.broadcast_to(ids[c : c + 1, :], (requests, requests)) for c in range(cand_dev)], axis=0
    )
    own_request = iota((total, requests), 0) % requests
    diagonal = own_request == iota((total, requests), 1)
    ids = lane_sum(jnp.where(diagonal, spread, 0.0)).astype(I32)
    where_row = as_bf16((ids >> 7) == iota((total, blocks), 1))
    stored = place[...]
    parts = jnp.concatenate(
        [
            (stored & 255).astype(F32).astype(BF16),
            ((stored >> 8) & 255).astype(F32).astype(BF16),
            (stored >> 16).astype(F32).astype(BF16),
        ],
        axis=1,
    )
    found = dot(where_row, parts)
    found = found[:, :LANES] + 256.0 * found[:, LANES : 2 * LANES] + 65536.0 * found[:, 2 * LANES :]
    lane = iota((total, LANES), 1)
    slot = lane_sum(jnp.where((ids & 127) == lane, found, 0.0)).astype(I32)
    rows_dev = blocks * LANES // owners
    shift = rows_dev.bit_length() - 1
    owner = slot >> shift
    within = slot & (rows_dev - 1)
    hit = owner == lane
    hits = as_bf16(hit)
    earlier = as_bf16(iota((total, total), 1) < iota((total, total), 0))
    rank = lane_sum(jnp.where(hit, dot(earlier, hits), 0.0)).astype(I32)
    meta[...] = jnp.where(lane == 0, owner, rank)
    request = iota((total, 1), 0) % requests
    low = (within & 255).astype(F32)
    high = ((within >> 8) + 4 * request + 128).astype(F32)
    entry = jnp.where(lane == rank, low, 0.0) + jnp.where(lane == rank + HALF, high, 0.0)
    wanted = dot(hits, entry.astype(BF16), (((0,), (0,)), ((), ())))
    book = codebook[...].astype(F32)
    sub = iota(book.shape, 0)
    first = jnp.sum(jnp.where(sub == 2 * req, book, 0.0), axis=0, keepdims=True)
    second = jnp.sum(jnp.where(sub == 2 * req + 1, book, 0.0), axis=0, keepdims=True)
    people = user[...].astype(F32)
    person = jnp.sum(jnp.where(iota(people.shape, 0) == item, people, 0.0), axis=0, keepdims=True)
    tile = jnp.concatenate(
        [
            first[:, :LANES],
            first[:, LANES:],
            second[:, :LANES],
            second[:, LANES:],
            person[:, :LANES],
            person[:, LANES:],
            jnp.zeros((2, LANES), F32),
        ],
        axis=0,
    )
    tiles[...] = jnp.broadcast_to(tile[None], (owners, MSG, LANES)).reshape(owners * MSG, LANES)
    tiles[pl.ds(WANT_ROW, owners, stride=MSG), :] = wanted
    message[...] = tiles[...].reshape(owners, MSG, LANES).astype(BF16)


def project_kernel(band, items_in, weights_in, table, items, weights, tiles, sems):
    stored, features = items.shape
    width = weights.shape[1]
    d_user = width - features
    copies = [
        pltpu.make_async_copy(items_in, items, sems.at[0]),
        pltpu.make_async_copy(weights_in.at[0, pl.ds(d_user, features)], weights, sems.at[1]),
    ]
    for copy in copies:
        copy.start()
    for copy in copies:
        copy.wait()
    chunks = width // LANES
    lines = band * 2 * chunks
    copies = []
    for n in range(stored // band):
        rows = slice(n * band, (n + 1) * band)
        for c in range(chunks):
            at = c * LANES - d_user
            part = jnp.zeros((band, LANES), F32)
            if at >= 0:
                part = items[rows, at : at + LANES].astype(F32)
            tiles[pl.ds(n * lines + c, band, stride=2 * chunks), :] = part
        for c in range(0, chunks, 2):
            product = dot(items[rows, :], weights[:, c * LANES : (c + 2) * LANES])
            for i in range(2):
                to = pl.ds(n * lines + chunks + c + i, band, stride=2 * chunks)
                tiles[to, :] = product[:, i * LANES : (i + 1) * LANES]
        whole = pl.ds(n * lines, lines)
        copies.append(pltpu.make_async_copy(tiles.at[whole], table.at[whole], sems.at[2 + n]))
        copies[-1].start()
    for copy in copies:
        copy.wait()


def rank_kernel(
    chunk,
    block,
    stretch,
    got,
    table_in,
    weights_in,
    bias,
    out_weight,
    logits,
    table,
    early,
    weights,
    tiles,
    users,
    first,
    state,
    rounded,
    answer,
    picks,
    picked,
    sems,
):
    sources = got.shape[0]
    halves = 2
    per = chunk // halves
    rows = per * sources
    layers, width, _ = weights_in.shape
    chunks = width // LANES
    double = 2 * chunks
    d_user = 2 * LANES
    pairs = [(weights_in.at[0, pl.ds(0, d_user)], early), (table_in, table)]
    pairs += [(weights_in.at[i], weights.at[i - 1]) for i in range(1, layers)]
    copies = [pltpu.make_async_copy(a, b, sems.at[i]) for i, (a, b) in enumerate(pairs)]
    for copy in copies:
        copy.start()
    reqs = lax.axis_size("req")
    tiles[...] = got[...].astype(F32).reshape(sources * MSG, LANES)
    wanted = tiles[pl.ds(WANT_ROW, sources, stride=MSG), :]
    lane = iota((sources, LANES), 1)
    low = wanted.astype(I32)
    high = pltpu.roll(wanted, HALF, axis=1).astype(I32)
    within = low + 256 * (high & 3)
    person = ((high >> 2) & 31) * reqs + iota((sources, LANES), 0) % reqs
    split = (table.shape[0] - 1).bit_length()
    picks[...] = within * double + ((person * double) << split)
    copy = pltpu.make_async_copy(picks, picked, sems.at[len(copies)])
    copy.start()
    most = jnp.max(jnp.where((lane < HALF) & (high > 0), lane + 1, 0))
    people = [tiles[pl.ds(USER_ROW + i, sources, stride=MSG), :] for i in range(2)]
    flat = jnp.concatenate(people, axis=1).astype(BF16)
    for c in range(chunks):
        part = people[c] if c < 2 else jnp.zeros((sources, LANES), F32)
        users[pl.ds(c, sources, stride=double), :] = part
    copies[0].wait()
    for c in range(0, chunks, 2):
        to = slice(c * LANES, (c + 2) * LANES)
        product = dot(flat, early[:, to]) + bias[0:1, to]
        for i in range(2):
            part = product[:, i * LANES : (i + 1) * LANES]
            users[pl.ds(chunks + c + i, sources, stride=double), :] = part
    answer[...] = jnp.zeros(answer.shape, F32)
    copy.wait()
    copies[1].wait()

    def arrive(t, some):
        @pl.when(t == 0)
        def _():
            for copy in some:
                copy.wait()

    def step(t, carry):
        def gather(s, carry):
            values = []
            for u in range(8):
                source = s * 8 + u
                for k in range(chunk):
                    both = picked[source, t * chunk + k]
                    row = pl.multiple_of(both & ((1 << split) - 1), double)
                    man = pl.multiple_of(both >> split, double)
                    start = table[pl.ds(row, chunks), :] + users[pl.ds(man, chunks), :]
                    product = (
                        table[pl.ds(row + chunks, chunks), :]
                        + users[pl.ds(man + chunks, chunks), :]
                    )
                    values.append((k * sources + source, start, start * product + start))
            for at, start, new in values:
                first[pl.ds(at, chunks, stride=stretch), :] = start
                state[pl.ds(at, chunks, stride=stretch), :] = new
            return carry

        lax.fori_loop(0, sources // 8, gather, 0)
        for h in range(halves):
            at = slice(h * rows, (h + 1) * rows)
            for c in range(chunks):
                lines = slice(c * stretch + h * rows, c * stretch + (h + 1) * rows)
                rounded[0, at, c * LANES : (c + 1) * LANES] = state[lines, :].astype(BF16)
        parts = [jnp.zeros((rows, LANES), F32) for _ in range(halves)]
        for layer in range(1, layers):
            if layer < 3:
                arrive(t, copies[2:3] if layer == 1 else copies[3:])
            for h in range(halves):
                at = slice(h * rows, (h + 1) * rows)
                left = rounded[(layer + 1) % 2, at, :]
                for n in range(0, width, block):
                    to = slice(n, n + block)
                    product = dot(left, weights[layer - 1, :, to]) + bias[layer : layer + 1, to]
                    for i in range(0, block, LANES):
                        c = (n + i) // LANES
                        lines = slice(c * stretch + h * rows, c * stretch + (h + 1) * rows)
                        new = first[lines, :] * product[:, i : i + LANES] + state[lines, :]
                        if layer < layers - 1:
                            state[lines, :] = new
                            rounded[layer % 2, at, n + i : n + i + LANES] = new.astype(BF16)
                        else:
                            parts[h] = parts[h] + new * out_weight[:, n + i : n + i + LANES]
        for h in range(halves):
            value = lane_sum(parts[h])
            for k in range(per):
                j = t * chunk + h * per + k
                mine = value[k * sources : (k + 1) * sources]
                answer[...] += jnp.where(lane == j, mine, 0.0)
        return carry

    lax.fori_loop(0, jnp.maximum((most + chunk - 1) // chunk, 1), step, 0)
    logits[...] = answer[...].reshape(logits.shape)


def score_kernel(block, looked, got, user, codes, scores, tiles, tables, wide):
    sources = got.shape[0]
    requests, d_user = user.shape
    subs, count = codes.shape
    tiles[...] = got[...].astype(F32).reshape(sources * MSG, LANES)
    book = [tiles[pl.ds(i, sources, stride=MSG), :].astype(BF16) for i in range(CB_ROWS)]
    even = jnp.concatenate(book[:2], axis=1)
    odd = jnp.concatenate(book[2:], axis=1)
    column = iota((d_user, sources), 0)
    people = user[...]
    of_even = dot(people, as_bf16(column == 2 * iota((d_user, sources), 1))).astype(BF16)
    of_odd = dot(people, as_bf16(column == 2 * iota((d_user, sources), 1) + 1)).astype(BF16)
    per_sub = sources // subs
    zero = jnp.zeros((), BF16)
    for m in range(subs):
        mine = iota((requests, sources), 1) // per_sub == m
        table = dot(jnp.where(mine, of_even, zero), even) + dot(jnp.where(mine, of_odd, zero), odd)
        table = table.astype(BF16)
        if m < looked:
            wide[m] = table.astype(F32)
        else:
            tables[:, m * CODES : (m + 1) * CODES] = table

    code = lax.broadcasted_iota(jnp.int16, (CODES, block), 0)
    one = jnp.ones((), BF16)
    groups, spans = requests // 8, block // LANES
    order = sorted(
        [((i + 0.5) / looked, i) for i in range(looked)]
        + [((i + 0.5) / (subs - looked), i + looked) for i in range(subs - looked)]
    )

    def pick(values, index):
        return jnp.take_along_axis(values, index, axis=1, mode="promise_in_bounds")

    def step(j, carry):
        at = pl.ds(pl.multiple_of(j * block, block), block)
        total = jnp.zeros((requests, block), F32)
        sums = [[jnp.zeros((8, LANES), F32) for _ in range(spans)] for _ in range(groups)]
        for _, m in order:
            row = codes[m : m + 1, at]
            if m >= looked:
                now = jnp.broadcast_to(row, (16, block)).astype(jnp.int16)
                now = jnp.concatenate([now] * (CODES // 16), axis=0)
                onehot = jnp.where(code == now, one, zero)
                total = total + dot(tables[:, m * CODES : (m + 1) * CODES], onehot)
                continue
            for b in range(spans):
                now = jnp.broadcast_to(row[:, b * LANES : (b + 1) * LANES], (8, LANES))
                index = now & (LANES - 1)
                upper = now >= LANES
                for g in range(groups):
                    low = pick(wide[m, g * 8 : (g + 1) * 8, :LANES], index)
                    high = pick(wide[m, g * 8 : (g + 1) * 8, LANES:], index)
                    sums[g][b] = sums[g][b] + jnp.where(upper, high, low)
        rows = [jnp.concatenate(group, axis=1) for group in sums]
        scores[:, at] = total + jnp.concatenate(rows, axis=0)
        return carry

    lax.fori_loop(0, count // block, step, 0)


def collect_kernel(back, meta, logits):
    cand_dev, requests = logits.shape
    total = meta.shape[0]
    owners = back.shape[0]
    lane = iota((total, owners), 1)
    answers = back[...].reshape(owners, LANES)
    pick = as_bf16(meta[:, 0:1] == lane)
    top = answers.astype(BF16)
    rest = answers - top.astype(F32)
    middle = rest.astype(BF16)
    last = (rest - middle.astype(F32)).astype(BF16)
    rows = dot(pick, top) + dot(pick, middle) + dot(pick, last)
    value = lane_sum(jnp.where(meta[:, 1:2] == lane, rows, 0.0))
    diagonal = iota((total, requests), 0) % requests == iota((total, requests), 1)
    spread = jnp.where(diagonal, value, 0.0)
    logits[...] = jnp.sum(spread.reshape(cand_dev, requests, requests), axis=1)


def on_device(
    user_emb,
    codebooks,
    item_codes,
    item_place,
    candidates,
    item_features,
    cross_weights,
    cross_bias,
    out_weight,
):
    requests, d_user = user_emb.shape
    cand_dev = candidates.shape[1]
    total = requests * cand_dev
    owners = lax.axis_size("item") * lax.axis_size("req")
    items = item_codes.shape[0]
    layers, width, _ = cross_weights.shape
    whole = pltpu.CompilerParams(vmem_limit_bytes=60 << 20)
    limit = pltpu.CompilerParams(vmem_limit_bytes=24 << 20)
    message, meta = pl.pallas_call(
        prepare_kernel,
        out_shape=(
            jax.ShapeDtypeStruct((owners, MSG, LANES), BF16),
            jax.ShapeDtypeStruct((total, LANES), I32),
        ),
        in_specs=[HBM] * 4,
        out_specs=(VMEM, VMEM),
        scratch_shapes=[
            pltpu.VMEM((owners * MSG, LANES), F32),
            pltpu.VMEM((cand_dev, requests), I32),
            pltpu.VMEM((item_place.shape[0] // LANES, LANES), I32),
            pltpu.VMEM(codebooks.shape[:0:-1], BF16),
            pltpu.VMEM(user_emb.shape, BF16),
            pltpu.SemaphoreType.DMA((4,)),
        ],
        compiler_params=whole,
        name="prepare",
    )(
        candidates.T,
        item_place.reshape(-1, LANES),
        jnp.swapaxes(codebooks, 1, 2)[0],
        user_emb,
    )
    got = lax.all_to_all(message, ("item", "req"), split_axis=0, concat_axis=0, tiled=True)
    stored, features = item_features.shape
    lines = stored * 2 * width // LANES
    band = stored // 4
    table = pl.pallas_call(
        functools.partial(project_kernel, band),
        out_shape=jax.ShapeDtypeStruct((lines, LANES), F32),
        in_specs=[HBM, HBM],
        out_specs=HBM,
        scratch_shapes=[
            pltpu.VMEM(item_features.shape, BF16),
            pltpu.VMEM((features, width), BF16),
            pltpu.VMEM((lines, LANES), F32),
            pltpu.SemaphoreType.DMA((2 + stored // band,)),
        ],
        compiler_params=whole,
        name="project",
        cost_estimate=pl.CostEstimate(flops=2 << 30, bytes_accessed=12 << 20, transcendentals=0),
    )(item_features, cross_weights)
    chunk = 4
    rows = chunk * owners
    stretch = rows + 8
    answers = pl.pallas_call(
        functools.partial(rank_kernel, chunk, 256, stretch),
        out_shape=jax.ShapeDtypeStruct((owners, 1, LANES), F32),
        in_specs=[VMEM, HBM, HBM, VMEM, VMEM],
        out_specs=VMEM,
        scratch_shapes=[
            pltpu.VMEM((lines, LANES), F32),
            pltpu.VMEM((d_user, width), BF16),
            pltpu.VMEM((layers - 1, width, width), BF16),
            pltpu.VMEM((owners * MSG, LANES), F32),
            pltpu.VMEM((owners * 2 * width // LANES, LANES), F32),
            pltpu.VMEM((stretch * width // LANES, LANES), F32),
            pltpu.VMEM((stretch * width // LANES, LANES), F32),
            pltpu.VMEM((2, rows, width), BF16),
            pltpu.VMEM((owners, LANES), F32),
            pltpu.VMEM((owners, LANES), I32),
            pltpu.SMEM((owners, LANES), I32),
            pltpu.SemaphoreType.DMA((layers + 2,)),
        ],
        compiler_params=pltpu.CompilerParams(vmem_limit_bytes=52 << 20),
        name="rank",
        cost_estimate=pl.CostEstimate(flops=12 << 30, bytes_accessed=10 << 20, transcendentals=0),
    )(got, table, cross_weights, cross_bias, out_weight.reshape(1, width))
    back = lax.all_to_all(answers, ("item", "req"), split_axis=0, concat_axis=0, tiled=True)
    looked = 14
    scores = pl.pallas_call(
        functools.partial(score_kernel, 512, looked),
        out_shape=jax.ShapeDtypeStruct((requests, items), F32),
        in_specs=[VMEM] * 3,
        out_specs=VMEM,
        scratch_shapes=[
            pltpu.VMEM((owners * MSG, LANES), F32),
            pltpu.VMEM((requests, item_codes.shape[1] * CODES), BF16),
            pltpu.VMEM((looked, requests, CODES), F32),
        ],
        compiler_params=limit,
        name="scores",
        cost_estimate=pl.CostEstimate(flops=2 << 30, bytes_accessed=40 << 20, transcendentals=0),
    )(got, user_emb, item_codes.T)
    logits = pl.pallas_call(
        collect_kernel,
        out_shape=jax.ShapeDtypeStruct((cand_dev, requests), F32),
        in_specs=[VMEM] * 2,
        out_specs=VMEM,
        compiler_params=limit,
        name="collect",
    )(back, meta)
    return scores, logits.T


def solution(mesh):
    placed = (
        P("req", None),
        P("item", None, None),
        P("item", None),
        P(),
        P("req", "item"),
        P(("item", "req"), None),
        P(),
        P(),
        P(),
    )
    return jax.shard_map(
        on_device,
        mesh=mesh,
        in_specs=placed,
        out_specs=(P("req", "item"), P("req", "item")),
        check_vma=False,
    )
```

```python
import functools

import jax
import jax.numpy as jnp
from jax import lax
from jax.experimental import pallas as pl
from jax.experimental.pallas import tpu as pltpu
from jax.sharding import PartitionSpec as P

F32 = jnp.float32
BF16 = jnp.bfloat16
I32 = jnp.int32
HBM = pl.BlockSpec(memory_space=pltpu.HBM)
VMEM = pl.BlockSpec(memory_space=pltpu.VMEM)
LANES = 128
MSG = 8
CB_ROWS = 4
USER_ROW = 4
WANT_ROW = 6
HALF = 64
CODES = 256


def dot(a, b, dims=(((1,), (0,)), ((), ()))):
    return lax.dot_general(a, b, dims, preferred_element_type=F32)


def iota(shape, axis):
    return lax.broadcasted_iota(I32, shape, axis)


def lane_sum(x):
    return jnp.sum(x, axis=1, keepdims=True)


def as_bf16(mask):
    return jnp.where(mask, 1.0, 0.0).astype(BF16)


def prepare_kernel(
    cand_in, place_in, codebook_in, user_in, message, meta, tiles, cand, place, codebook, user, sems
):
    pairs = ((cand_in, cand), (place_in, place), (codebook_in, codebook), (user_in, user))
    copies = [pltpu.make_async_copy(a, b, sems.at[i]) for i, (a, b) in enumerate(pairs)]
    for copy in copies:
        copy.start()
    for copy in copies:
        copy.wait()
    cand_dev, requests = cand.shape
    total = cand_dev * requests
    owners = message.shape[0]
    blocks = place.shape[0]
    item = lax.axis_index("item")
    req = lax.axis_index("req")
    ids = cand[...].astype(F32)
    spread = jnp.concatenate(
        [jnp.broadcast_to(ids[c : c + 1, :], (requests, requests)) for c in range(cand_dev)], axis=0
    )
    own_request = iota((total, requests), 0) % requests
    diagonal = own_request == iota((total, requests), 1)
    ids = lane_sum(jnp.where(diagonal, spread, 0.0)).astype(I32)
    where_row = as_bf16((ids >> 7) == iota((total, blocks), 1))
    stored = place[...]
    parts = jnp.concatenate(
        [
            (stored & 255).astype(F32).astype(BF16),
            ((stored >> 8) & 255).astype(F32).astype(BF16),
            (stored >> 16).astype(F32).astype(BF16),
        ],
        axis=1,
    )
    found = dot(where_row, parts)
    found = found[:, :LANES] + 256.0 * found[:, LANES : 2 * LANES] + 65536.0 * found[:, 2 * LANES :]
    lane = iota((total, LANES), 1)
    slot = lane_sum(jnp.where((ids & 127) == lane, found, 0.0)).astype(I32)
    rows_dev = blocks * LANES // owners
    shift = rows_dev.bit_length() - 1
    owner = slot >> shift
    within = slot & (rows_dev - 1)
    hit = owner == lane
    hits = as_bf16(hit)
    earlier = as_bf16(iota((total, total), 1) < iota((total, total), 0))
    rank = lane_sum(jnp.where(hit, dot(earlier, hits), 0.0)).astype(I32)
    meta[...] = jnp.where(lane == 0, owner, rank)
    request = iota((total, 1), 0) % requests
    low = (within & 255).astype(F32)
    high = ((within >> 8) + 4 * request + 128).astype(F32)
    entry = jnp.where(lane == rank, low, 0.0) + jnp.where(lane == rank + HALF, high, 0.0)
    wanted = dot(hits, entry.astype(BF16), (((0,), (0,)), ((), ())))
    book = codebook[...].astype(F32)
    sub = iota(book.shape, 0)
    first = jnp.sum(jnp.where(sub == 2 * req, book, 0.0), axis=0, keepdims=True)
    second = jnp.sum(jnp.where(sub == 2 * req + 1, book, 0.0), axis=0, keepdims=True)
    people = user[...].astype(F32)
    person = jnp.sum(jnp.where(iota(people.shape, 0) == item, people, 0.0), axis=0, keepdims=True)
    tile = jnp.concatenate(
        [
            first[:, :LANES],
            first[:, LANES:],
            second[:, :LANES],
            second[:, LANES:],
            person[:, :LANES],
            person[:, LANES:],
            jnp.zeros((2, LANES), F32),
        ],
        axis=0,
    )
    tiles[...] = jnp.broadcast_to(tile[None], (owners, MSG, LANES)).reshape(owners * MSG, LANES)
    tiles[pl.ds(WANT_ROW, owners, stride=MSG), :] = wanted
    message[...] = tiles[...].reshape(owners, MSG, LANES).astype(BF16)


def project_kernel(band, items_in, weights_in, table, items, weights, tiles, sems):
    stored, features = items.shape
    width = weights.shape[1]
    copies = [
        pltpu.make_async_copy(items_in, items, sems.at[0]),
        pltpu.make_async_copy(weights_in.at[0, pl.ds(width - features, features)], weights, sems.at[1]),
    ]
    for copy in copies:
        copy.start()
    for copy in copies:
        copy.wait()
    chunks = width // LANES
    copies = []
    for n in range(stored // band):
        for c in range(0, chunks, 2):
            left = items[n * band : (n + 1) * band, :]
            product = dot(left, weights[:, c * LANES : (c + 2) * LANES])
            for i in range(2):
                to = pl.ds(n * band * chunks + c + i, band, stride=chunks)
                tiles[to, :] = product[:, i * LANES : (i + 1) * LANES]
        whole = pl.ds(n * band * chunks, band * chunks)
        copies.append(pltpu.make_async_copy(tiles.at[whole], table.at[whole], sems.at[2 + n]))
        copies[-1].start()
    for copy in copies:
        copy.wait()


def rank_kernel(
    ranks,
    block,
    stretch,
    got,
    table_in,
    items_in,
    weights_in,
    bias,
    out_weight,
    logits,
    table,
    items,
    early,
    weights,
    tiles,
    features,
    people,
    greetings,
    first,
    state,
    rounded,
    answer,
    picks,
    picked,
    sems,
):
    sources = got.shape[0]
    rows = ranks * sources
    layers, width, _ = weights_in.shape
    stored = items.shape[0]
    chunks = width // LANES
    own = early.shape[0] // LANES
    copies = [
        (weights_in.at[0, pl.ds(0, own * LANES)], early),
        (items_in, items),
        (table_in, table),
    ]
    copies += [(weights_in.at[i], weights.at[i - 1]) for i in range(1, layers)]
    copies = [pltpu.make_async_copy(a, b, sems.at[i]) for i, (a, b) in enumerate(copies)]
    for copy in copies:
        copy.start()
    reqs = lax.axis_size("req")
    tiles[...] = got[...].astype(F32).reshape(sources * MSG, LANES)
    wanted = tiles[pl.ds(WANT_ROW, sources, stride=MSG), :]
    lane = iota((sources, LANES), 1)
    low = wanted.astype(I32)
    high = pltpu.roll(wanted, HALF, axis=1).astype(I32)
    within = low + 256 * (high & 3)
    person = ((high >> 2) & 31) * reqs + iota((sources, LANES), 0) % reqs
    split = (stored * chunks - 1).bit_length()
    picks[...] = within * chunks + ((person * chunks) << split)
    fetch = pltpu.make_async_copy(picks, picked, sems.at[len(copies)])
    fetch.start()
    most = jnp.max(jnp.where((lane < HALF) & (high > 0), lane + 1, 0))
    users = [tiles[pl.ds(USER_ROW + i, sources, stride=MSG), :] for i in range(own)]
    blank = jnp.zeros((sources, LANES), F32)
    for c in range(chunks):
        people[pl.ds(c, sources, stride=chunks), :] = users[c] if c < own else blank
    copies[0].wait()
    flat = jnp.concatenate(users, axis=1).astype(BF16)
    for c in range(0, chunks, 2):
        to = slice(c * LANES, (c + 2) * LANES)
        product = dot(flat, early[:, to]) + bias[0:1, to]
        for i in range(2):
            part = product[:, i * LANES : (i + 1) * LANES]
            greetings[pl.ds(c + i, sources, stride=chunks), :] = part
    copies[1].wait()
    for c in range(chunks):
        part = jnp.zeros((stored, LANES), F32)
        if c >= own:
            part = items[:, (c - own) * LANES : (c - own + 1) * LANES].astype(F32)
        features[pl.ds(c, stored, stride=chunks), :] = part
    answer[...] = jnp.zeros(answer.shape, F32)
    fetch.wait()
    copies[2].wait()

    def gather(slot, unit, some):
        values = []
        for n in some:
            k, source = n // sources, n % sources
            both = picked[source, unit * ranks + k]
            row = pl.ds(pl.multiple_of(both & ((1 << split) - 1), chunks), chunks)
            man = pl.ds(pl.multiple_of(both >> split, chunks), chunks)
            start = features[row, :] + people[man, :]
            values.append((n, start, start * (table[row, :] + greetings[man, :]) + start))
        for n, start, new in values:
            first[slot, pl.ds(n, chunks, stride=stretch), :] = start
            state[slot, pl.ds(n, chunks, stride=stretch), :] = new

    def lines(c):
        return slice(c * stretch, c * stretch + rows)

    def run(slot, unit, waits):
        following = list(range(rows))
        parts = jnp.zeros((rows, LANES), F32)
        left = layers - 1
        share = -(-rows // (left * width // block))
        for c in range(chunks):
            rounded[0, :, c * LANES : (c + 1) * LANES] = state[slot, lines(c), :].astype(BF16)
        for layer in range(1, layers):
            if waits is not None and layer < 3:
                waits(copies[3:4] if layer == 1 else copies[4:])
            source = rounded[(layer + 1) % 2]
            for n in range(0, width, block):
                product = dot(source, weights[layer - 1, :, n : n + block])
                product = product + bias[layer : layer + 1, n : n + block]
                gather(1 - slot, unit + 1, following[:share])
                following = following[share:]
                for i in range(0, block, LANES):
                    at = lines((n + i) // LANES)
                    new = first[slot, at, :] * product[:, i : i + LANES] + state[slot, at, :]
                    if layer < layers - 1:
                        state[slot, at, :] = new
                        rounded[layer % 2, :, n + i : n + i + LANES] = new.astype(BF16)
                    else:
                        parts = parts + new * out_weight[:, n + i : n + i + LANES]
        value = lane_sum(parts)
        for k in range(ranks):
            mine = value[k * sources : (k + 1) * sources]
            answer[...] += jnp.where(lane == unit * ranks + k, mine, 0.0)

    def begin(s, carry):
        for k in range(ranks):
            values = []
            for u in range(8):
                source = s * 8 + u
                both = picked[source, k]
                row = pl.ds(pl.multiple_of(both & ((1 << split) - 1), chunks), chunks)
                man = pl.ds(pl.multiple_of(both >> split, chunks), chunks)
                start = features[row, :] + people[man, :]
                new = start * (table[row, :] + greetings[man, :]) + start
                values.append((k * sources + source, start, new))
            for n, start, new in values:
                first[0, pl.ds(n, chunks, stride=stretch), :] = start
                state[0, pl.ds(n, chunks, stride=stretch), :] = new
        return carry

    lax.fori_loop(0, sources // 8, begin, 0)

    def step(t, carry):
        def waits(some):
            @pl.when(t == 0)
            def _():
                for copy in some:
                    copy.wait()

        run(0, 2 * t, waits)
        run(1, 2 * t + 1, None)
        return carry

    steps = jnp.maximum((most + 2 * ranks - 1) // (2 * ranks), 1)
    lax.fori_loop(0, steps, step, 0)
    logits[...] = answer[...].reshape(logits.shape)


def score_kernel(block, looked, got, user, codes, scores, tiles, tables, wide):
    sources = got.shape[0]
    requests, d_user = user.shape
    subs, count = codes.shape
    tiles[...] = got[...].astype(F32).reshape(sources * MSG, LANES)
    book = [tiles[pl.ds(i, sources, stride=MSG), :].astype(BF16) for i in range(CB_ROWS)]
    even = jnp.concatenate(book[:2], axis=1)
    odd = jnp.concatenate(book[2:], axis=1)
    column = iota((d_user, sources), 0)
    people = user[...]
    of_even = dot(people, as_bf16(column == 2 * iota((d_user, sources), 1))).astype(BF16)
    of_odd = dot(people, as_bf16(column == 2 * iota((d_user, sources), 1) + 1)).astype(BF16)
    per_sub = sources // subs
    zero = jnp.zeros((), BF16)
    for m in range(subs):
        mine = iota((requests, sources), 1) // per_sub == m
        table = dot(jnp.where(mine, of_even, zero), even) + dot(jnp.where(mine, of_odd, zero), odd)
        table = table.astype(BF16)
        if m < looked:
            wide[m] = table.astype(F32)
        else:
            tables[:, m * CODES : (m + 1) * CODES] = table

    code = lax.broadcasted_iota(jnp.int16, (CODES, block), 0)
    one = jnp.ones((), BF16)
    groups, spans = requests // 8, block // LANES
    order = sorted(
        [((i + 0.5) / looked, i) for i in range(looked)]
        + [((i + 0.5) / (subs - looked), i + looked) for i in range(subs - looked)]
    )

    def pick(values, index):
        return jnp.take_along_axis(values, index, axis=1, mode="promise_in_bounds")

    def step(j, carry):
        at = pl.ds(pl.multiple_of(j * block, block), block)
        total = jnp.zeros((requests, block), F32)
        sums = [[jnp.zeros((8, LANES), F32) for _ in range(spans)] for _ in range(groups)]
        for _, m in order:
            row = codes[m : m + 1, at]
            if m >= looked:
                now = jnp.broadcast_to(row, (16, block)).astype(jnp.int16)
                now = jnp.concatenate([now] * (CODES // 16), axis=0)
                onehot = jnp.where(code == now, one, zero)
                total = total + dot(tables[:, m * CODES : (m + 1) * CODES], onehot)
                continue
            for b in range(spans):
                now = jnp.broadcast_to(row[:, b * LANES : (b + 1) * LANES], (8, LANES))
                index = now & (LANES - 1)
                upper = now >= LANES
                for g in range(groups):
                    low = pick(wide[m, g * 8 : (g + 1) * 8, :LANES], index)
                    high = pick(wide[m, g * 8 : (g + 1) * 8, LANES:], index)
                    sums[g][b] = sums[g][b] + jnp.where(upper, high, low)
        rows = [jnp.concatenate(group, axis=1) for group in sums]
        scores[:, at] = total + jnp.concatenate(rows, axis=0)
        return carry

    lax.fori_loop(0, count // block, step, 0)


def collect_kernel(back, meta, logits):
    cand_dev, requests = logits.shape
    total = meta.shape[0]
    owners = back.shape[0]
    lane = iota((total, owners), 1)
    answers = back[...].reshape(owners, LANES)
    pick = as_bf16(meta[:, 0:1] == lane)
    top = answers.astype(BF16)
    rest = answers - top.astype(F32)
    middle = rest.astype(BF16)
    last = (rest - middle.astype(F32)).astype(BF16)
    rows = dot(pick, top) + dot(pick, middle) + dot(pick, last)
    value = lane_sum(jnp.where(meta[:, 1:2] == lane, rows, 0.0))
    diagonal = iota((total, requests), 0) % requests == iota((total, requests), 1)
    spread = jnp.where(diagonal, value, 0.0)
    logits[...] = jnp.sum(spread.reshape(cand_dev, requests, requests), axis=1)


def on_device(
    user_emb,
    codebooks,
    item_codes,
    item_place,
    candidates,
    item_features,
    cross_weights,
    cross_bias,
    out_weight,
):
    requests, d_user = user_emb.shape
    cand_dev = candidates.shape[1]
    total = requests * cand_dev
    owners = lax.axis_size("item") * lax.axis_size("req")
    items = item_codes.shape[0]
    layers, width, _ = cross_weights.shape
    whole = pltpu.CompilerParams(vmem_limit_bytes=60 << 20)
    limit = pltpu.CompilerParams(vmem_limit_bytes=24 << 20)
    message, meta = pl.pallas_call(
        prepare_kernel,
        out_shape=(
            jax.ShapeDtypeStruct((owners, MSG, LANES), BF16),
            jax.ShapeDtypeStruct((total, LANES), I32),
        ),
        in_specs=[HBM] * 4,
        out_specs=(VMEM, VMEM),
        scratch_shapes=[
            pltpu.VMEM((owners * MSG, LANES), F32),
            pltpu.VMEM((cand_dev, requests), I32),
            pltpu.VMEM((item_place.shape[0] // LANES, LANES), I32),
            pltpu.VMEM(codebooks.shape[:0:-1], BF16),
            pltpu.VMEM(user_emb.shape, BF16),
            pltpu.SemaphoreType.DMA((4,)),
        ],
        compiler_params=whole,
        name="prepare",
    )(
        candidates.T,
        item_place.reshape(-1, LANES),
        jnp.swapaxes(codebooks, 1, 2)[0],
        user_emb,
    )
    got = lax.all_to_all(message, ("item", "req"), split_axis=0, concat_axis=0, tiled=True)
    stored, features = item_features.shape
    chunks = width // LANES
    lines = stored * chunks
    band = stored // 4
    table = pl.pallas_call(
        functools.partial(project_kernel, band),
        out_shape=jax.ShapeDtypeStruct((lines, LANES), F32),
        in_specs=[HBM, HBM],
        out_specs=HBM,
        scratch_shapes=[
            pltpu.VMEM(item_features.shape, BF16),
            pltpu.VMEM((features, width), BF16),
            pltpu.VMEM((lines, LANES), F32),
            pltpu.SemaphoreType.DMA((2 + stored // band,)),
        ],
        compiler_params=whole,
        name="project",
        cost_estimate=pl.CostEstimate(flops=2 << 30, bytes_accessed=12 << 20, transcendentals=0),
    )(item_features, cross_weights)
    ranks = 2
    rows = ranks * owners
    stretch = rows + 8
    answers = pl.pallas_call(
        functools.partial(rank_kernel, ranks, 256, stretch),
        out_shape=jax.ShapeDtypeStruct((owners, 1, LANES), F32),
        in_specs=[VMEM, HBM, HBM, HBM, VMEM, VMEM],
        out_specs=VMEM,
        scratch_shapes=[
            pltpu.VMEM((lines, LANES), F32),
            pltpu.VMEM(item_features.shape, BF16),
            pltpu.VMEM((d_user, width), BF16),
            pltpu.VMEM((layers - 1, width, width), BF16),
            pltpu.VMEM((owners * MSG, LANES), F32),
            pltpu.VMEM((lines, LANES), F32),
            pltpu.VMEM((owners * chunks, LANES), F32),
            pltpu.VMEM((owners * chunks, LANES), F32),
            pltpu.VMEM((2, stretch * chunks, LANES), F32),
            pltpu.VMEM((2, stretch * chunks, LANES), F32),
            pltpu.VMEM((2, rows, width), BF16),
            pltpu.VMEM((owners, LANES), F32),
            pltpu.VMEM((owners, LANES), I32),
            pltpu.SMEM((owners, LANES), I32),
            pltpu.SemaphoreType.DMA((layers + 3,)),
        ],
        compiler_params=pltpu.CompilerParams(vmem_limit_bytes=53 << 20),
        name="rank",
        cost_estimate=pl.CostEstimate(flops=12 << 30, bytes_accessed=10 << 20, transcendentals=0),
    )(got, table, item_features, cross_weights, cross_bias, out_weight.reshape(1, width))
    back = lax.all_to_all(answers, ("item", "req"), split_axis=0, concat_axis=0, tiled=True)
    looked = 14
    scores = pl.pallas_call(
        functools.partial(score_kernel, 512, looked),
        out_shape=jax.ShapeDtypeStruct((requests, items), F32),
        in_specs=[VMEM] * 3,
        out_specs=VMEM,
        scratch_shapes=[
            pltpu.VMEM((owners * MSG, LANES), F32),
            pltpu.VMEM((requests, item_codes.shape[1] * CODES), BF16),
            pltpu.VMEM((looked, requests, CODES), F32),
        ],
        compiler_params=limit,
        name="scores",
        cost_estimate=pl.CostEstimate(flops=2 << 30, bytes_accessed=40 << 20, transcendentals=0),
    )(got, user_emb, item_codes.T)
    logits = pl.pallas_call(
        collect_kernel,
        out_shape=jax.ShapeDtypeStruct((cand_dev, requests), F32),
        in_specs=[VMEM] * 2,
        out_specs=VMEM,
        compiler_params=limit,
        name="collect",
    )(back, meta)
    return scores, logits.T


def solution(mesh):
    placed = (
        P("req", None),
        P("item", None, None),
        P("item", None),
        P(),
        P("req", "item"),
        P(("item", "req"), None),
        P(),
        P(),
        P(),
    )
    return jax.shard_map(
        on_device,
        mesh=mesh,
        in_specs=placed,
        out_specs=(P("req", "item"), P("req", "item")),
        check_vma=False,
    )
```

```python
import functools

import jax
import jax.numpy as jnp
from jax import lax
from jax.experimental import pallas as pl
from jax.experimental.pallas import tpu as pltpu
from jax.sharding import PartitionSpec as P

F32 = jnp.float32
BF16 = jnp.bfloat16
I32 = jnp.int32
HBM = pl.BlockSpec(memory_space=pltpu.HBM)
VMEM = pl.BlockSpec(memory_space=pltpu.VMEM)
LANES = 128
MSG = 8
CB_ROWS = 4
USER_ROW = 4
WANT_ROW = 6
HALF = 64
CODES = 256


def dot(a, b, dims=(((1,), (0,)), ((), ()))):
    return lax.dot_general(a, b, dims, preferred_element_type=F32)


def iota(shape, axis):
    return lax.broadcasted_iota(I32, shape, axis)


def lane_sum(x):
    return jnp.sum(x, axis=1, keepdims=True)


def as_bf16(mask):
    return jnp.where(mask, 1.0, 0.0).astype(BF16)


def prepare_kernel(
    cand_in, place_in, codebook_in, user_in, message, meta, tiles, cand, place, codebook, user, sems
):
    pairs = ((cand_in, cand), (place_in, place), (codebook_in, codebook), (user_in, user))
    copies = [pltpu.make_async_copy(a, b, sems.at[i]) for i, (a, b) in enumerate(pairs)]
    for copy in copies:
        copy.start()
    cand_dev, requests = cand.shape
    total = cand_dev * requests
    owners = message.shape[0]
    blocks = place.shape[0]
    item = lax.axis_index("item")
    req = lax.axis_index("req")
    copies[2].wait()
    copies[3].wait()
    book = codebook[...].astype(F32)
    sub = iota(book.shape, 0)
    first = jnp.sum(jnp.where(sub == 2 * req, book, 0.0), axis=0, keepdims=True)
    second = jnp.sum(jnp.where(sub == 2 * req + 1, book, 0.0), axis=0, keepdims=True)
    people = user[...].astype(F32)
    person = jnp.sum(jnp.where(iota(people.shape, 0) == item, people, 0.0), axis=0, keepdims=True)
    tile = jnp.concatenate(
        [
            first[:, :LANES],
            first[:, LANES:],
            second[:, :LANES],
            second[:, LANES:],
            person[:, :LANES],
            person[:, LANES:],
            jnp.zeros((2, LANES), F32),
        ],
        axis=0,
    )
    tiles[...] = jnp.broadcast_to(tile[None], (owners, MSG, LANES)).reshape(owners * MSG, LANES)
    copies[0].wait()
    ids = cand[...].astype(F32)
    spread = jnp.concatenate(
        [jnp.broadcast_to(ids[c : c + 1, :], (requests, requests)) for c in range(cand_dev)], axis=0
    )
    own_request = iota((total, requests), 0) % requests
    diagonal = own_request == iota((total, requests), 1)
    ids = lane_sum(jnp.where(diagonal, spread, 0.0)).astype(I32)
    where_row = as_bf16((ids >> 7) == iota((total, blocks), 1))
    copies[1].wait()
    stored = place[...]
    parts = jnp.concatenate(
        [
            (stored & 255).astype(F32).astype(BF16),
            ((stored >> 8) & 255).astype(F32).astype(BF16),
            (stored >> 16).astype(F32).astype(BF16),
        ],
        axis=1,
    )
    found = dot(where_row, parts)
    found = found[:, :LANES] + 256.0 * found[:, LANES : 2 * LANES] + 65536.0 * found[:, 2 * LANES :]
    lane = iota((total, LANES), 1)
    slot = lane_sum(jnp.where((ids & 127) == lane, found, 0.0)).astype(I32)
    rows_dev = blocks * LANES // owners
    shift = rows_dev.bit_length() - 1
    owner = slot >> shift
    within = slot & (rows_dev - 1)
    hit = owner == lane
    hits = as_bf16(hit)
    earlier = as_bf16(iota((total, total), 1) < iota((total, total), 0))
    rank = lane_sum(jnp.where(hit, dot(earlier, hits), 0.0)).astype(I32)
    meta[...] = jnp.where(lane == 0, owner, rank)
    request = iota((total, 1), 0) % requests
    low = (within & 255).astype(F32)
    high = ((within >> 8) + 4 * request + 128).astype(F32)
    entry = jnp.where(lane == rank, low, 0.0) + jnp.where(lane == rank + HALF, high, 0.0)
    wanted = dot(hits, entry.astype(BF16), (((0,), (0,)), ((), ())))
    tiles[pl.ds(WANT_ROW, owners, stride=MSG), :] = wanted
    message[...] = tiles[...].reshape(owners, MSG, LANES).astype(BF16)


def project_kernel(band, items_in, weights_in, table, items, weights, tiles, sems):
    stored, features = items.shape
    width = weights.shape[1]
    copies = [
        pltpu.make_async_copy(items_in, items, sems.at[0]),
        pltpu.make_async_copy(weights_in.at[0, pl.ds(width - features, features)], weights, sems.at[1]),
    ]
    for copy in copies:
        copy.start()
    for copy in copies:
        copy.wait()
    chunks = width // LANES
    copies = []
    for n in range(stored // band):
        for c in range(0, chunks, 2):
            left = items[n * band : (n + 1) * band, :]
            product = dot(left, weights[:, c * LANES : (c + 2) * LANES])
            for i in range(2):
                to = pl.ds(n * band * chunks + c + i, band, stride=chunks)
                tiles[to, :] = product[:, i * LANES : (i + 1) * LANES]
        whole = pl.ds(n * band * chunks, band * chunks)
        copies.append(pltpu.make_async_copy(tiles.at[whole], table.at[whole], sems.at[2 + n]))
        copies[-1].start()
    for copy in copies:
        copy.wait()


def rank_kernel(
    units,
    ranks,
    block,
    stretch,
    got,
    table_in,
    items_in,
    weights_in,
    bias,
    out_weight,
    logits,
    table,
    items,
    early,
    weights,
    tiles,
    features,
    people,
    greetings,
    first,
    state,
    rounded,
    answer,
    picks,
    picked,
    sems,
):
    sources = got.shape[0]
    rows = ranks * sources
    layers, width, _ = weights_in.shape
    stored = items.shape[0]
    chunks = width // LANES
    own = early.shape[0] // LANES
    copies = [
        (weights_in.at[0, pl.ds(0, own * LANES)], early),
        (items_in, items),
        (table_in, table),
    ]
    copies += [(weights_in.at[i], weights.at[i - 1]) for i in range(1, layers)]
    copies = [pltpu.make_async_copy(a, b, sems.at[i]) for i, (a, b) in enumerate(copies)]
    for copy in copies:
        copy.start()
    reqs = lax.axis_size("req")
    tiles[...] = got[...].astype(F32).reshape(sources * MSG, LANES)
    wanted = tiles[pl.ds(WANT_ROW, sources, stride=MSG), :]
    lane = iota((sources, LANES), 1)
    low = wanted.astype(I32)
    high = pltpu.roll(wanted, HALF, axis=1).astype(I32)
    within = low + 256 * (high & 3)
    person = ((high >> 2) & 31) * reqs + iota((sources, LANES), 0) % reqs
    split = (stored * chunks - 1).bit_length()
    picks[...] = within * chunks + ((person * chunks) << split)
    fetch = pltpu.make_async_copy(picks, picked, sems.at[len(copies)])
    fetch.start()
    users = [tiles[pl.ds(USER_ROW + i, sources, stride=MSG), :] for i in range(own)]
    blank = jnp.zeros((sources, LANES), F32)
    for c in range(chunks):
        people[pl.ds(c, sources, stride=chunks), :] = users[c] if c < own else blank
    copies[0].wait()
    flat = jnp.concatenate(users, axis=1).astype(BF16)
    def greet(sums):
        left = jnp.concatenate([flat] * (ranks // 2), axis=0)
        for turn in range(width // block):
            to = slice(turn * block, (turn + 1) * block)
            pltpu.matmul_push_rhs(early[:, to], turn // 2, turn % 2)
            pltpu.matmul_acc_lhs(sums[turn], left, turn // 2)
        for turn in range(width // block):
            product = pltpu.matmul_pop(sums[turn])[:sources]
            product = product + bias[0:1, turn * block : (turn + 1) * block]
            for i in range(0, block, LANES):
                c = (turn * block + i) // LANES
                greetings[pl.ds(c, sources, stride=chunks), :] = product[:, i : i + LANES]

    copies[1].wait()
    for c in range(chunks):
        part = jnp.zeros((stored, LANES), F32)
        if c >= own:
            part = items[:, (c - own) * LANES : (c - own + 1) * LANES].astype(F32)
        features[pl.ds(c, stored, stride=chunks), :] = part
    answer[...] = jnp.zeros(answer.shape, F32)
    fetch.wait()
    copies[2].wait()

    def gather(slot, unit, some):
        values = []
        for n in some:
            k, source = n // sources, n % sources
            both = picked[source, unit * ranks + k]
            row = pl.ds(pl.multiple_of(both & ((1 << split) - 1), chunks), chunks)
            man = pl.ds(pl.multiple_of(both >> split, chunks), chunks)
            start = features[row, :] + people[man, :]
            values.append((n, start, start * (table[row, :] + greetings[man, :]) + start))
        for n, start, new in values:
            first[slot, pl.ds(n, chunks, stride=stretch), :] = start
            state[slot, pl.ds(n, chunks, stride=stretch), :] = new

    def lines(c, start, count):
        return slice(c * stretch + start, c * stretch + start + count)

    def begin(s, carry):
        for k in range(ranks):
            values = []
            for u in range(8):
                source = s * 8 + u
                both = picked[source, k]
                row = pl.ds(pl.multiple_of(both & ((1 << split) - 1), chunks), chunks)
                man = pl.ds(pl.multiple_of(both >> split, chunks), chunks)
                start = features[row, :] + people[man, :]
                new = start * (table[row, :] + greetings[man, :]) + start
                values.append((k * sources + source, start, new))
            for n, start, new in values:
                first[0, pl.ds(n, chunks, stride=stretch), :] = start
                state[0, pl.ds(n, chunks, stride=stretch), :] = new
        return carry

    halves = 2
    half = rows // halves
    depth = width // block
    blocks = [(u, l, p) for u in range(units) for l in range(1, layers) for p in range(depth // 2)]
    turns = [(*b, k) for b in blocks for k in range(depth)]
    share = -(-rows // (((layers - 1) * depth - 2) * halves))
    following = [list(range(rows)) for _ in range(units - 1)] + [[]]
    parts = [[jnp.zeros((half, LANES), F32) for _ in range(halves)] for _ in range(units)]

    def push(turn):
        _, layer, p, k = turns[turn]
        if p == 0 and k == 0 and turns[turn][0] == 0:
            copies[2 + layer].wait()
        for x in range(2):
            n = (2 * p + x) * block
            tile = weights[layer - 1, k * block : (k + 1) * block, n : n + block]
            pltpu.matmul_push_rhs(tile, turn % 2, x)

    def finish(unit, layer, p, h, x, total):
        n = (2 * p + x) * block
        product = pltpu.matmul_pop(total) + bias[layer : layer + 1, n : n + block]
        gather(1 - unit % 2, unit + 1, following[unit][:share])
        del following[unit][:share]
        for i in range(0, block, LANES):
            at = lines((n + i) // LANES, h * half, half)
            new = first[unit % 2, at, :] * product[:, i : i + LANES] + state[unit % 2, at, :]
            if layer < layers - 1:
                state[unit % 2, at, :] = new
                rounded[layer % 2, h * half : (h + 1) * half, n + i : n + i + LANES] = new.astype(BF16)
            else:
                parts[unit][h] = parts[unit][h] + new * out_weight[:, n + i : n + i + LANES]
        if (layer, p, x) == (layers - 1, depth // 2 - 1, 1):
            value = lane_sum(parts[unit][h])
            for k in range(half // sources):
                j = unit * ranks + h * half // sources + k
                mine = value[k * sources : (k + 1) * sources]
                answer[...] += jnp.where(lane == j, mine, 0.0)

    def network(*sums):
        def total(block_at, h, x):
            return sums[(block_at % 2) * 4 + h * 2 + x]

        greet(sums)
        lax.fori_loop(0, sources // 8, begin, 0)
        push(0)
        for at, (unit, layer, p) in enumerate(blocks):
            waiting = [] if at == 0 else [(h, x) for h in range(halves) for x in range(2)]
            for k in range(depth):
                turn = at * depth + k
                if turn + 1 < len(turns):
                    push(turn + 1)
                for h in range(halves):
                    own_rows = slice(h * half, (h + 1) * half)
                    if layer == 1 and p == 0:
                        for c in range(k * block // LANES, (k + 1) * block // LANES):
                            entered = state[unit % 2, lines(c, h * half, half), :]
                            rounded[0, own_rows, c * LANES : (c + 1) * LANES] = entered.astype(BF16)
                    left = rounded[(layer + 1) % 2, own_rows, k * block : (k + 1) * block]
                    for x in range(2):
                        pltpu.matmul_acc_lhs(total(at, h, x), left, None if h else turn % 2)
                for _ in range((1, 2, 1, 0)[k] if waiting else 0):
                    h, x = waiting.pop(0)
                    finish(*blocks[at - 1], h, x, total(at - 1, h, x))
        for h in range(halves):
            for x in range(2):
                finish(*blocks[-1], h, x, total(len(blocks) - 1, h, x))

    pl.run_scoped(network, *[pltpu.ACC(mxu_id=i % 2)((half, block), F32) for i in range(8)])
    logits[...] = answer[...].reshape(logits.shape)


def score_kernel(block, looked, got, user, codes, scores, tiles, tables, wide):
    sources = got.shape[0]
    requests, d_user = user.shape
    subs, count = codes.shape
    tiles[...] = got[...].astype(F32).reshape(sources * MSG, LANES)
    book = [tiles[pl.ds(i, sources, stride=MSG), :].astype(BF16) for i in range(CB_ROWS)]
    even = jnp.concatenate(book[:2], axis=1)
    odd = jnp.concatenate(book[2:], axis=1)
    column = iota((d_user, sources), 0)
    people = user[...]
    of_even = dot(people, as_bf16(column == 2 * iota((d_user, sources), 1))).astype(BF16)
    of_odd = dot(people, as_bf16(column == 2 * iota((d_user, sources), 1) + 1)).astype(BF16)
    per_sub = sources // subs
    zero = jnp.zeros((), BF16)
    for m in range(subs):
        mine = iota((requests, sources), 1) // per_sub == m
        table = dot(jnp.where(mine, of_even, zero), even) + dot(jnp.where(mine, of_odd, zero), odd)
        table = table.astype(BF16)
        if m < looked:
            wide[m] = table.astype(F32)
        else:
            tables[:, m * CODES : (m + 1) * CODES] = table

    code = lax.broadcasted_iota(jnp.int16, (CODES, block), 0)
    one = jnp.ones((), BF16)
    groups, spans = requests // 8, block // LANES
    order = sorted(
        [((i + 0.5) / looked, i) for i in range(looked)]
        + [((i + 0.5) / (subs - looked), i + looked) for i in range(subs - looked)]
    )

    def pick(values, index):
        return jnp.take_along_axis(values, index, axis=1, mode="promise_in_bounds")

    def step(j, carry):
        at = pl.ds(pl.multiple_of(j * block, block), block)
        total = jnp.zeros((requests, block), F32)
        sums = [[jnp.zeros((8, LANES), F32) for _ in range(spans)] for _ in range(groups)]
        for _, m in order:
            row = codes[m : m + 1, at]
            if m >= looked:
                now = jnp.broadcast_to(row, (16, block)).astype(jnp.int16)
                now = jnp.concatenate([now] * (CODES // 16), axis=0)
                onehot = jnp.where(code == now, one, zero)
                total = total + dot(tables[:, m * CODES : (m + 1) * CODES], onehot)
                continue
            for b in range(spans):
                now = jnp.broadcast_to(row[:, b * LANES : (b + 1) * LANES], (8, LANES))
                index = now & (LANES - 1)
                upper = now >= LANES
                for g in range(groups):
                    low = pick(wide[m, g * 8 : (g + 1) * 8, :LANES], index)
                    high = pick(wide[m, g * 8 : (g + 1) * 8, LANES:], index)
                    sums[g][b] = sums[g][b] + jnp.where(upper, high, low)
        rows = [jnp.concatenate(group, axis=1) for group in sums]
        scores[:, at] = total + jnp.concatenate(rows, axis=0)
        return carry

    lax.fori_loop(0, count // block, step, 0)


def collect_kernel(back, meta, logits):
    cand_dev, requests = logits.shape
    total = meta.shape[0]
    owners = back.shape[0]
    lane = iota((total, owners), 1)
    answers = back[...].reshape(owners, LANES)
    pick = as_bf16(meta[:, 0:1] == lane)
    top = answers.astype(BF16)
    rest = answers - top.astype(F32)
    middle = rest.astype(BF16)
    last = (rest - middle.astype(F32)).astype(BF16)
    rows = dot(pick, top) + dot(pick, middle) + dot(pick, last)
    value = lane_sum(jnp.where(meta[:, 1:2] == lane, rows, 0.0))
    diagonal = iota((total, requests), 0) % requests == iota((total, requests), 1)
    spread = jnp.where(diagonal, value, 0.0)
    logits[...] = jnp.sum(spread.reshape(cand_dev, requests, requests), axis=1)


def on_device(
    user_emb,
    codebooks,
    item_codes,
    item_place,
    candidates,
    item_features,
    cross_weights,
    cross_bias,
    out_weight,
):
    requests, d_user = user_emb.shape
    cand_dev = candidates.shape[1]
    total = requests * cand_dev
    owners = lax.axis_size("item") * lax.axis_size("req")
    items = item_codes.shape[0]
    layers, width, _ = cross_weights.shape
    whole = pltpu.CompilerParams(vmem_limit_bytes=60 << 20)
    limit = pltpu.CompilerParams(vmem_limit_bytes=24 << 20)
    message, meta = pl.pallas_call(
        prepare_kernel,
        out_shape=(
            jax.ShapeDtypeStruct((owners, MSG, LANES), BF16),
            jax.ShapeDtypeStruct((total, LANES), I32),
        ),
        in_specs=[HBM] * 4,
        out_specs=(VMEM, VMEM),
        scratch_shapes=[
            pltpu.VMEM((owners * MSG, LANES), F32),
            pltpu.VMEM((cand_dev, requests), I32),
            pltpu.VMEM((item_place.shape[0] // LANES, LANES), I32),
            pltpu.VMEM(codebooks.shape[:0:-1], BF16),
            pltpu.VMEM(user_emb.shape, BF16),
            pltpu.SemaphoreType.DMA((4,)),
        ],
        compiler_params=whole,
        name="prepare",
    )(
        candidates.T,
        item_place.reshape(-1, LANES),
        jnp.swapaxes(codebooks, 1, 2)[0],
        user_emb,
    )
    got = lax.all_to_all(message, ("item", "req"), split_axis=0, concat_axis=0, tiled=True)
    stored, features = item_features.shape
    chunks = width // LANES
    lines = stored * chunks
    band = stored // 4
    table = pl.pallas_call(
        functools.partial(project_kernel, band),
        out_shape=jax.ShapeDtypeStruct((lines, LANES), F32),
        in_specs=[HBM, HBM],
        out_specs=HBM,
        scratch_shapes=[
            pltpu.VMEM(item_features.shape, BF16),
            pltpu.VMEM((features, width), BF16),
            pltpu.VMEM((lines, LANES), F32),
            pltpu.SemaphoreType.DMA((2 + stored // band,)),
        ],
        compiler_params=whole,
        name="project",
        cost_estimate=pl.CostEstimate(flops=2 << 30, bytes_accessed=12 << 20, transcendentals=0),
    )(item_features, cross_weights)
    capacity = 3 * total // owners
    ranks = 4
    rows = ranks * owners
    stretch = rows + 8
    answers = pl.pallas_call(
        functools.partial(rank_kernel, capacity // ranks, ranks, 256, stretch),
        out_shape=jax.ShapeDtypeStruct((owners, 1, LANES), F32),
        in_specs=[VMEM, HBM, HBM, HBM, VMEM, VMEM],
        out_specs=VMEM,
        scratch_shapes=[
            pltpu.VMEM((lines, LANES), F32),
            pltpu.VMEM(item_features.shape, BF16),
            pltpu.VMEM((d_user, width), BF16),
            pltpu.VMEM((layers - 1, width, width), BF16),
            pltpu.VMEM((owners * MSG, LANES), F32),
            pltpu.VMEM((lines, LANES), F32),
            pltpu.VMEM((owners * chunks, LANES), F32),
            pltpu.VMEM((owners * chunks, LANES), F32),
            pltpu.VMEM((2, stretch * chunks, LANES), F32),
            pltpu.VMEM((2, stretch * chunks, LANES), F32),
            pltpu.VMEM((2, rows, width), BF16),
            pltpu.VMEM((owners, LANES), F32),
            pltpu.VMEM((owners, LANES), I32),
            pltpu.SMEM((owners, LANES), I32),
            pltpu.SemaphoreType.DMA((layers + 3,)),
        ],
        compiler_params=pltpu.CompilerParams(vmem_limit_bytes=53 << 20),
        name="rank",
        cost_estimate=pl.CostEstimate(flops=12 << 30, bytes_accessed=10 << 20, transcendentals=0),
    )(got, table, item_features, cross_weights, cross_bias, out_weight.reshape(1, width))
    back = lax.all_to_all(answers, ("item", "req"), split_axis=0, concat_axis=0, tiled=True)
    looked = 14
    scores = pl.pallas_call(
        functools.partial(score_kernel, 512, looked),
        out_shape=jax.ShapeDtypeStruct((requests, items), F32),
        in_specs=[VMEM] * 3,
        out_specs=VMEM,
        scratch_shapes=[
            pltpu.VMEM((owners * MSG, LANES), F32),
            pltpu.VMEM((requests, item_codes.shape[1] * CODES), BF16),
            pltpu.VMEM((looked, requests, CODES), F32),
        ],
        compiler_params=limit,
        name="scores",
        cost_estimate=pl.CostEstimate(flops=2 << 30, bytes_accessed=40 << 20, transcendentals=0),
    )(got, user_emb, item_codes.T)
    logits = pl.pallas_call(
        collect_kernel,
        out_shape=jax.ShapeDtypeStruct((cand_dev, requests), F32),
        in_specs=[VMEM] * 2,
        out_specs=VMEM,
        compiler_params=limit,
        name="collect",
    )(back, meta)
    return scores, logits.T


def solution(mesh):
    placed = (
        P("req", None),
        P("item", None, None),
        P("item", None),
        P(),
        P("req", "item"),
        P(("item", "req"), None),
        P(),
        P(),
        P(),
    )
    return jax.shard_map(
        on_device,
        mesh=mesh,
        in_specs=placed,
        out_specs=(P("req", "item"), P("req", "item")),
        check_vma=False,
    )
```

```python
import functools

import jax
import jax.numpy as jnp
from jax import lax
from jax.experimental import pallas as pl
from jax.experimental.pallas import tpu as pltpu
from jax.sharding import PartitionSpec as P

F32 = jnp.float32
BF16 = jnp.bfloat16
I32 = jnp.int32
HBM = pl.BlockSpec(memory_space=pltpu.HBM)
VMEM = pl.BlockSpec(memory_space=pltpu.VMEM)
LANES = 128
MSG = 8
CB_ROWS = 4
USER_ROW = 4
WANT_ROW = 6
HALF = 64
CODES = 256


def dot(a, b, dims=(((1,), (0,)), ((), ()))):
    return lax.dot_general(a, b, dims, preferred_element_type=F32)


def iota(shape, axis):
    return lax.broadcasted_iota(I32, shape, axis)


def lane_sum(x):
    return jnp.sum(x, axis=1, keepdims=True)


def as_bf16(mask):
    return jnp.where(mask, 1.0, 0.0).astype(BF16)


def prepare_kernel(
    cand_in, place_in, codebook_in, user_in, message, meta, tiles, cand, place, codebook, user, sems
):
    pairs = ((cand_in, cand), (place_in, place), (codebook_in, codebook), (user_in, user))
    copies = [pltpu.make_async_copy(a, b, sems.at[i]) for i, (a, b) in enumerate(pairs)]
    for copy in copies:
        copy.start()
    cand_dev, requests = cand.shape
    total = cand_dev * requests
    owners = message.shape[0]
    blocks = place.shape[0]
    item = lax.axis_index("item")
    req = lax.axis_index("req")
    copies[2].wait()
    copies[3].wait()
    book = codebook[...].astype(F32)
    sub = iota(book.shape, 0)
    first = jnp.sum(jnp.where(sub == 2 * req, book, 0.0), axis=0, keepdims=True)
    second = jnp.sum(jnp.where(sub == 2 * req + 1, book, 0.0), axis=0, keepdims=True)
    people = user[...].astype(F32)
    person = jnp.sum(jnp.where(iota(people.shape, 0) == item, people, 0.0), axis=0, keepdims=True)
    tile = jnp.concatenate(
        [
            first[:, :LANES],
            first[:, LANES:],
            second[:, :LANES],
            second[:, LANES:],
            person[:, :LANES],
            person[:, LANES:],
            jnp.zeros((2, LANES), F32),
        ],
        axis=0,
    )
    tiles[...] = jnp.broadcast_to(tile[None], (owners, MSG, LANES)).reshape(owners * MSG, LANES)
    copies[0].wait()
    ids = cand[...].astype(F32)
    spread = jnp.concatenate(
        [jnp.broadcast_to(ids[c : c + 1, :], (requests, requests)) for c in range(cand_dev)], axis=0
    )
    own_request = iota((total, requests), 0) % requests
    diagonal = own_request == iota((total, requests), 1)
    ids = lane_sum(jnp.where(diagonal, spread, 0.0)).astype(I32)
    where_row = as_bf16((ids >> 7) == iota((total, blocks), 1))
    copies[1].wait()
    stored = place[...]
    parts = jnp.concatenate(
        [
            (stored & 255).astype(F32).astype(BF16),
            ((stored >> 8) & 255).astype(F32).astype(BF16),
            (stored >> 16).astype(F32).astype(BF16),
        ],
        axis=1,
    )
    found = dot(where_row, parts)
    found = found[:, :LANES] + 256.0 * found[:, LANES : 2 * LANES] + 65536.0 * found[:, 2 * LANES :]
    lane = iota((total, LANES), 1)
    slot = lane_sum(jnp.where((ids & 127) == lane, found, 0.0)).astype(I32)
    rows_dev = blocks * LANES // owners
    shift = rows_dev.bit_length() - 1
    owner = slot >> shift
    within = slot & (rows_dev - 1)
    hit = owner == lane
    hits = as_bf16(hit)
    earlier = as_bf16(iota((total, total), 1) < iota((total, total), 0))
    rank = lane_sum(jnp.where(hit, dot(earlier, hits), 0.0)).astype(I32)
    meta[...] = jnp.where(lane == 0, owner, rank)
    request = iota((total, 1), 0) % requests
    low = (within & 255).astype(F32)
    high = ((within >> 8) + 4 * request + 128).astype(F32)
    entry = jnp.where(lane == rank, low, 0.0) + jnp.where(lane == rank + HALF, high, 0.0)
    wanted = dot(hits, entry.astype(BF16), (((0,), (0,)), ((), ())))
    tiles[pl.ds(WANT_ROW, owners, stride=MSG), :] = wanted
    message[...] = tiles[...].reshape(owners, MSG, LANES).astype(BF16)


def project_kernel(band, items_in, weights_in, table, items, weights, tiles, sems):
    stored, features = items.shape
    width = weights.shape[1]
    copies = [
        pltpu.make_async_copy(items_in, items, sems.at[0]),
        pltpu.make_async_copy(weights_in.at[0, pl.ds(width - features, features)], weights, sems.at[1]),
    ]
    for copy in copies:
        copy.start()
    for copy in copies:
        copy.wait()
    chunks = width // LANES
    copies = []
    for n in range(stored // band):
        for c in range(0, chunks, 2):
            left = items[n * band : (n + 1) * band, :]
            product = dot(left, weights[:, c * LANES : (c + 2) * LANES])
            for i in range(2):
                to = pl.ds(n * band * chunks + c + i, band, stride=chunks)
                tiles[to, :] = product[:, i * LANES : (i + 1) * LANES]
        whole = pl.ds(n * band * chunks, band * chunks)
        copies.append(pltpu.make_async_copy(tiles.at[whole], table.at[whole], sems.at[2 + n]))
        copies[-1].start()
    for copy in copies:
        copy.wait()


def rank_kernel(
    units,
    ranks,
    block,
    stretch,
    got,
    table_in,
    items,
    weights_in,
    bias,
    out_weight,
    logits,
    early,
    table,
    weights,
    tiles,
    features,
    people,
    greetings,
    first,
    state,
    rounded,
    answer,
    picks,
    picked,
    sems,
):
    sources = got.shape[0]
    rows = ranks * sources
    layers, width, _ = weights_in.shape
    stored = items.shape[0]
    chunks = width // LANES
    own = early.shape[0] // LANES
    copies = [(weights_in.at[0, pl.ds(0, own * LANES)], early), (table_in, table)]
    copies += [(weights_in.at[i], weights.at[i - 1]) for i in range(1, layers)]
    copies = [pltpu.make_async_copy(a, b, sems.at[i]) for i, (a, b) in enumerate(copies)]
    for copy in copies[:2]:
        copy.start()
    reqs = lax.axis_size("req")
    tiles[...] = got[...].astype(F32).reshape(sources * MSG, LANES)
    wanted = tiles[pl.ds(WANT_ROW, sources, stride=MSG), :]
    lane = iota((sources, LANES), 1)
    low = wanted.astype(I32)
    high = pltpu.roll(wanted, HALF, axis=1).astype(I32)
    within = low + 256 * (high & 3)
    person = ((high >> 2) & 31) * reqs + iota((sources, LANES), 0) % reqs
    split = (stored * chunks - 1).bit_length()
    picks[...] = within * chunks + ((person * chunks) << split)
    fetch = pltpu.make_async_copy(picks, picked, sems.at[len(copies)])
    fetch.start()
    users = [tiles[pl.ds(USER_ROW + i, sources, stride=MSG), :] for i in range(own)]
    blank = jnp.zeros((sources, LANES), F32)
    for c in range(chunks):
        people[pl.ds(c, sources, stride=chunks), :] = users[c] if c < own else blank
    flat = jnp.concatenate(users, axis=1).astype(BF16)

    def greet(sums):
        left = jnp.concatenate([flat] * (ranks // 2), axis=0)
        for turn in range(width // block):
            to = slice(turn * block, (turn + 1) * block)
            pltpu.matmul_push_rhs(early[:, to], turn // 2, turn % 2)
            pltpu.matmul_acc_lhs(sums[turn], left, turn // 2)
        for turn in range(width // block):
            product = pltpu.matmul_pop(sums[turn])[:sources]
            product = product + bias[0:1, turn * block : (turn + 1) * block]
            for i in range(0, block, LANES):
                c = (turn * block + i) // LANES
                greetings[pl.ds(c, sources, stride=chunks), :] = product[:, i : i + LANES]

    for c in range(chunks):
        part = jnp.zeros((stored, LANES), F32)
        if c >= own:
            part = items[:, (c - own) * LANES : (c - own + 1) * LANES].astype(F32)
        features[pl.ds(c, stored, stride=chunks), :] = part
    answer[...] = jnp.zeros(answer.shape, F32)

    def gather(slot, unit, some):
        values = []
        for n in some:
            k, source = n // sources, n % sources
            both = picked[source, unit * ranks + k]
            row = pl.ds(pl.multiple_of(both & ((1 << split) - 1), chunks), chunks)
            man = pl.ds(pl.multiple_of(both >> split, chunks), chunks)
            start = features[row, :] + people[man, :]
            values.append((n, start, start * (table[row, :] + greetings[man, :]) + start))
        for n, start, new in values:
            first[slot, pl.ds(n, chunks, stride=stretch), :] = start
            state[slot, pl.ds(n, chunks, stride=stretch), :] = new

    def lines(c, start, count):
        return slice(c * stretch + start, c * stretch + start + count)

    def begin(s, carry):
        for k in range(ranks):
            values = []
            for u in range(8):
                source = s * 8 + u
                both = picked[source, k]
                row = pl.ds(pl.multiple_of(both & ((1 << split) - 1), chunks), chunks)
                man = pl.ds(pl.multiple_of(both >> split, chunks), chunks)
                start = features[row, :] + people[man, :]
                new = start * (table[row, :] + greetings[man, :]) + start
                values.append((k * sources + source, start, new))
            for n, start, new in values:
                first[0, pl.ds(n, chunks, stride=stretch), :] = start
                state[0, pl.ds(n, chunks, stride=stretch), :] = new
        return carry

    halves = 2
    half = rows // halves
    depth = width // block
    blocks = [(u, l, p) for u in range(units) for l in range(1, layers) for p in range(depth // 2)]
    turns = [(*b, k) for b in blocks for k in range(depth)]
    share = -(-rows // (((layers - 1) * depth - 2) * halves))
    following = [list(range(rows)) for _ in range(units - 1)] + [[]]
    parts = [[jnp.zeros((half, LANES), F32) for _ in range(halves)] for _ in range(units)]

    def push(turn):
        _, layer, p, k = turns[turn]
        if p == 0 and k == 0 and turns[turn][0] == 0:
            copies[1 + layer].wait()
        for x in range(2):
            n = (2 * p + x) * block
            tile = weights[layer - 1, k * block : (k + 1) * block, n : n + block]
            pltpu.matmul_push_rhs(tile, turn % 2, x)

    def finish(unit, layer, p, h, x, total):
        n = (2 * p + x) * block
        product = pltpu.matmul_pop(total) + bias[layer : layer + 1, n : n + block]
        gather(1 - unit % 2, unit + 1, following[unit][:share])
        del following[unit][:share]
        for i in range(0, block, LANES):
            at = lines((n + i) // LANES, h * half, half)
            new = first[unit % 2, at, :] * product[:, i : i + LANES] + state[unit % 2, at, :]
            if layer < layers - 1:
                state[unit % 2, at, :] = new
                rounded[layer % 2, h * half : (h + 1) * half, n + i : n + i + LANES] = new.astype(BF16)
            else:
                parts[unit][h] = parts[unit][h] + new * out_weight[:, n + i : n + i + LANES]
        if (layer, p, x) == (layers - 1, depth // 2 - 1, 1):
            value = lane_sum(parts[unit][h])
            for k in range(half // sources):
                j = unit * ranks + h * half // sources + k
                mine = value[k * sources : (k + 1) * sources]
                answer[...] += jnp.where(lane == j, mine, 0.0)

    def network(*sums):
        def total(block_at, h, x):
            return sums[(block_at % 2) * 4 + h * 2 + x]

        copies[0].wait()
        greet(sums)
        copies[2].start()
        fetch.wait()
        copies[1].wait()
        for copy in copies[3:]:
            copy.start()
        lax.fori_loop(0, sources // 8, begin, 0)
        push(0)
        for at, (unit, layer, p) in enumerate(blocks):
            waiting = [] if at == 0 else [(h, x) for h in range(halves) for x in range(2)]
            for k in range(depth):
                turn = at * depth + k
                if turn + 1 < len(turns):
                    push(turn + 1)
                for h in range(halves):
                    own_rows = slice(h * half, (h + 1) * half)
                    if layer == 1 and p == 0:
                        for c in range(k * block // LANES, (k + 1) * block // LANES):
                            entered = state[unit % 2, lines(c, h * half, half), :]
                            rounded[0, own_rows, c * LANES : (c + 1) * LANES] = entered.astype(BF16)
                    left = rounded[(layer + 1) % 2, own_rows, k * block : (k + 1) * block]
                    for x in range(2):
                        pltpu.matmul_acc_lhs(total(at, h, x), left, None if h else turn % 2)
                for _ in range((1, 2, 1, 0)[k] if waiting else 0):
                    h, x = waiting.pop(0)
                    finish(*blocks[at - 1], h, x, total(at - 1, h, x))
        for h in range(halves):
            for x in range(2):
                finish(*blocks[-1], h, x, total(len(blocks) - 1, h, x))

    pl.run_scoped(network, *[pltpu.ACC(mxu_id=i % 2)((half, block), F32) for i in range(8)])
    logits[...] = answer[...].reshape(logits.shape)


def score_kernel(block, looked, got, user, codes, scores, tiles, tables, wide):
    sources = got.shape[0]
    requests, d_user = user.shape
    subs, count = codes.shape
    tiles[...] = got[...].astype(F32).reshape(sources * MSG, LANES)
    book = [tiles[pl.ds(i, sources, stride=MSG), :].astype(BF16) for i in range(CB_ROWS)]
    even = jnp.concatenate(book[:2], axis=1)
    odd = jnp.concatenate(book[2:], axis=1)
    column = iota((d_user, sources), 0)
    people = user[...]
    of_even = dot(people, as_bf16(column == 2 * iota((d_user, sources), 1))).astype(BF16)
    of_odd = dot(people, as_bf16(column == 2 * iota((d_user, sources), 1) + 1)).astype(BF16)
    per_sub = sources // subs
    zero = jnp.zeros((), BF16)
    for m in range(subs):
        mine = iota((requests, sources), 1) // per_sub == m
        table = dot(jnp.where(mine, of_even, zero), even) + dot(jnp.where(mine, of_odd, zero), odd)
        table = table.astype(BF16)
        if m < looked:
            wide[m] = table.astype(F32)
        else:
            tables[:, m * CODES : (m + 1) * CODES] = table

    code = lax.broadcasted_iota(jnp.int16, (CODES, block), 0)
    one = jnp.ones((), BF16)
    groups, spans = requests // 8, block // LANES
    order = sorted(
        [((i + 0.5) / looked, i) for i in range(looked)]
        + [((i + 0.5) / (subs - looked), i + looked) for i in range(subs - looked)]
    )

    def pick(values, index):
        return jnp.take_along_axis(values, index, axis=1, mode="promise_in_bounds")

    def step(j, carry):
        at = pl.ds(pl.multiple_of(j * block, block), block)
        total = jnp.zeros((requests, block), F32)
        sums = [[jnp.zeros((8, LANES), F32) for _ in range(spans)] for _ in range(groups)]
        for _, m in order:
            row = codes[m : m + 1, at]
            if m >= looked:
                now = jnp.broadcast_to(row, (16, block)).astype(jnp.int16)
                now = jnp.concatenate([now] * (CODES // 16), axis=0)
                onehot = jnp.where(code == now, one, zero)
                total = total + dot(tables[:, m * CODES : (m + 1) * CODES], onehot)
                continue
            for b in range(spans):
                now = jnp.broadcast_to(row[:, b * LANES : (b + 1) * LANES], (8, LANES))
                index = now & (LANES - 1)
                upper = now >= LANES
                for g in range(groups):
                    low = pick(wide[m, g * 8 : (g + 1) * 8, :LANES], index)
                    high = pick(wide[m, g * 8 : (g + 1) * 8, LANES:], index)
                    sums[g][b] = sums[g][b] + jnp.where(upper, high, low)
        rows = [jnp.concatenate(group, axis=1) for group in sums]
        scores[:, at] = total + jnp.concatenate(rows, axis=0)
        return carry

    lax.fori_loop(0, count // block, step, 0)


def collect_kernel(back, meta, logits):
    cand_dev, requests = logits.shape
    total = meta.shape[0]
    owners = back.shape[0]
    lane = iota((total, owners), 1)
    answers = back[...].reshape(owners, LANES)
    pick = as_bf16(meta[:, 0:1] == lane)
    top = answers.astype(BF16)
    rest = answers - top.astype(F32)
    middle = rest.astype(BF16)
    last = (rest - middle.astype(F32)).astype(BF16)
    rows = dot(pick, top) + dot(pick, middle) + dot(pick, last)
    value = lane_sum(jnp.where(meta[:, 1:2] == lane, rows, 0.0))
    diagonal = iota((total, requests), 0) % requests == iota((total, requests), 1)
    spread = jnp.where(diagonal, value, 0.0)
    logits[...] = jnp.sum(spread.reshape(cand_dev, requests, requests), axis=1)


def on_device(
    user_emb,
    codebooks,
    item_codes,
    item_place,
    candidates,
    item_features,
    cross_weights,
    cross_bias,
    out_weight,
):
    requests, d_user = user_emb.shape
    cand_dev = candidates.shape[1]
    total = requests * cand_dev
    owners = lax.axis_size("item") * lax.axis_size("req")
    items = item_codes.shape[0]
    layers, width, _ = cross_weights.shape
    whole = pltpu.CompilerParams(vmem_limit_bytes=60 << 20)
    limit = pltpu.CompilerParams(vmem_limit_bytes=24 << 20)
    message, meta = pl.pallas_call(
        prepare_kernel,
        out_shape=(
            jax.ShapeDtypeStruct((owners, MSG, LANES), BF16),
            jax.ShapeDtypeStruct((total, LANES), I32),
        ),
        in_specs=[HBM] * 4,
        out_specs=(VMEM, VMEM),
        scratch_shapes=[
            pltpu.VMEM((owners * MSG, LANES), F32),
            pltpu.VMEM((cand_dev, requests), I32),
            pltpu.VMEM((item_place.shape[0] // LANES, LANES), I32),
            pltpu.VMEM(codebooks.shape[:0:-1], BF16),
            pltpu.VMEM(user_emb.shape, BF16),
            pltpu.SemaphoreType.DMA((4,)),
        ],
        compiler_params=whole,
        name="prepare",
    )(
        candidates.T,
        item_place.reshape(-1, LANES),
        jnp.swapaxes(codebooks, 1, 2)[0],
        user_emb,
    )
    got = lax.all_to_all(message, ("item", "req"), split_axis=0, concat_axis=0, tiled=True)
    stored, features = item_features.shape
    chunks = width // LANES
    lines = stored * chunks
    band = stored // 4
    table = pl.pallas_call(
        functools.partial(project_kernel, band),
        out_shape=jax.ShapeDtypeStruct((lines, LANES), F32),
        in_specs=[HBM, HBM],
        out_specs=HBM,
        scratch_shapes=[
            pltpu.VMEM(item_features.shape, BF16),
            pltpu.VMEM((features, width), BF16),
            pltpu.VMEM((lines, LANES), F32),
            pltpu.SemaphoreType.DMA((2 + stored // band,)),
        ],
        compiler_params=whole,
        name="project",
        cost_estimate=pl.CostEstimate(flops=2 << 30, bytes_accessed=12 << 20, transcendentals=0),
    )(item_features, cross_weights)
    capacity = 3 * total // owners
    ranks = 4
    rows = ranks * owners
    stretch = rows + 8
    answers = pl.pallas_call(
        functools.partial(rank_kernel, capacity // ranks, ranks, 256, stretch),
        out_shape=jax.ShapeDtypeStruct((owners, 1, LANES), F32),
        in_specs=[VMEM, HBM, VMEM, HBM, VMEM, VMEM],
        out_specs=VMEM,
        scratch_shapes=[
            pltpu.VMEM((d_user, width), BF16),
            pltpu.VMEM((lines, LANES), F32),
            pltpu.VMEM((layers - 1, width, width), BF16),
            pltpu.VMEM((owners * MSG, LANES), F32),
            pltpu.VMEM((lines, LANES), F32),
            pltpu.VMEM((owners * chunks, LANES), F32),
            pltpu.VMEM((owners * chunks, LANES), F32),
            pltpu.VMEM((2, stretch * chunks, LANES), F32),
            pltpu.VMEM((2, stretch * chunks, LANES), F32),
            pltpu.VMEM((2, rows, width), BF16),
            pltpu.VMEM((owners, LANES), F32),
            pltpu.VMEM((owners, LANES), I32),
            pltpu.SMEM((owners, LANES), I32),
            pltpu.SemaphoreType.DMA((layers + 2,)),
        ],
        compiler_params=pltpu.CompilerParams(vmem_limit_bytes=50 << 20),
        name="rank",
        cost_estimate=pl.CostEstimate(flops=12 << 30, bytes_accessed=10 << 20, transcendentals=0),
    )(got, table, item_features, cross_weights, cross_bias, out_weight.reshape(1, width))
    back = lax.all_to_all(answers, ("item", "req"), split_axis=0, concat_axis=0, tiled=True)
    looked = 14
    scores = pl.pallas_call(
        functools.partial(score_kernel, 512, looked),
        out_shape=jax.ShapeDtypeStruct((requests, items), F32),
        in_specs=[VMEM] * 3,
        out_specs=VMEM,
        scratch_shapes=[
            pltpu.VMEM((owners * MSG, LANES), F32),
            pltpu.VMEM((requests, item_codes.shape[1] * CODES), BF16),
            pltpu.VMEM((looked, requests, CODES), F32),
        ],
        compiler_params=limit,
        name="scores",
        cost_estimate=pl.CostEstimate(flops=2 << 30, bytes_accessed=40 << 20, transcendentals=0),
    )(got, user_emb, item_codes.T)
    logits = pl.pallas_call(
        collect_kernel,
        out_shape=jax.ShapeDtypeStruct((cand_dev, requests), F32),
        in_specs=[VMEM] * 2,
        out_specs=VMEM,
        compiler_params=limit,
        name="collect",
    )(back, meta)
    return scores, logits.T


def solution(mesh):
    placed = (
        P("req", None),
        P("item", None, None),
        P("item", None),
        P(),
        P("req", "item"),
        P(("item", "req"), None),
        P(),
        P(),
        P(),
    )
    return jax.shard_map(
        on_device,
        mesh=mesh,
        in_specs=placed,
        out_specs=(P("req", "item"), P("req", "item")),
        check_vma=False,
    )
```

```python
import functools

import jax
import jax.numpy as jnp
from jax import lax
from jax.experimental import pallas as pl
from jax.experimental.pallas import tpu as pltpu
from jax.sharding import PartitionSpec as P

F32 = jnp.float32
BF16 = jnp.bfloat16
I32 = jnp.int32
HBM = pl.BlockSpec(memory_space=pltpu.HBM)
VMEM = pl.BlockSpec(memory_space=pltpu.VMEM)
LANES = 128
MSG = 8
CB_ROWS = 4
USER_ROW = 4
WANT_ROW = 6
HALF = 64
CODES = 256
PIECE = 32


def dot(a, b, dims=(((1,), (0,)), ((), ()))):
    return lax.dot_general(a, b, dims, preferred_element_type=F32)


def iota(shape, axis):
    return lax.broadcasted_iota(I32, shape, axis)


def lane_sum(x):
    return jnp.sum(x, axis=1, keepdims=True)


def as_bf16(mask):
    return jnp.where(mask, 1.0, 0.0).astype(BF16)


def prepare_kernel(
    cand_in,
    place_in,
    codebook_in,
    user_in,
    message,
    meta_out,
    tiles,
    cand,
    place,
    codebook,
    user,
    meta,
    sems,
):
    pairs = ((cand_in, cand), (place_in, place), (codebook_in, codebook), (user_in, user))
    copies = [pltpu.make_async_copy(a, b, sems.at[i]) for i, (a, b) in enumerate(pairs)]
    for copy in copies:
        copy.start()
    cand_dev, requests = cand.shape
    total = cand_dev * requests
    owners = message.shape[0]
    blocks = place.shape[0]
    item = lax.axis_index("item")
    req = lax.axis_index("req")
    copies[0].wait()
    ids = cand[...].astype(F32)
    spread = jnp.concatenate(
        [jnp.broadcast_to(ids[c : c + 1, :], (requests, requests)) for c in range(cand_dev)], axis=0
    )
    own_request = iota((total, requests), 0) % requests
    diagonal = own_request == iota((total, requests), 1)
    ids = lane_sum(jnp.where(diagonal, spread, 0.0)).astype(I32)
    where_row = as_bf16((ids >> 7) == iota((total, blocks), 1))
    copies[1].wait()
    stored = place[...]
    parts = jnp.concatenate(
        [
            (stored & 255).astype(F32).astype(BF16),
            ((stored >> 8) & 255).astype(F32).astype(BF16),
            (stored >> 16).astype(F32).astype(BF16),
        ],
        axis=1,
    )
    found = dot(where_row, parts)
    found = found[:, :LANES] + 256.0 * found[:, LANES : 2 * LANES] + 65536.0 * found[:, 2 * LANES :]
    lane = iota((total, LANES), 1)
    slot = lane_sum(jnp.where((ids & 127) == lane, found, 0.0)).astype(I32)
    rows_dev = blocks * LANES // owners
    shift = rows_dev.bit_length() - 1
    owner = slot >> shift
    within = slot & (rows_dev - 1)
    hit = owner == lane
    hits = as_bf16(hit)
    earlier = as_bf16(iota((total, total), 1) < iota((total, total), 0))
    rank = lane_sum(jnp.where(hit, dot(earlier, hits), 0.0)).astype(I32)
    meta[...] = jnp.where(lane == 0, owner, rank)
    keep = pltpu.make_async_copy(meta, meta_out, sems.at[len(copies)])
    keep.start()
    request = iota((total, 1), 0) % requests
    low = (within & 255).astype(F32)
    high = ((within >> 8) + 4 * request + 128).astype(F32)
    entry = jnp.where(lane == rank, low, 0.0) + jnp.where(lane == rank + HALF, high, 0.0)
    wanted = dot(hits, entry.astype(BF16), (((0,), (0,)), ((), ())))
    copies[2].wait()
    copies[3].wait()
    book = codebook[...].astype(F32)
    sub = iota(book.shape, 0)
    first = jnp.sum(jnp.where(sub == 2 * req, book, 0.0), axis=0, keepdims=True)
    second = jnp.sum(jnp.where(sub == 2 * req + 1, book, 0.0), axis=0, keepdims=True)
    people = user[...].astype(F32)
    person = jnp.sum(jnp.where(iota(people.shape, 0) == item, people, 0.0), axis=0, keepdims=True)
    tile = jnp.concatenate(
        [
            first[:, :LANES],
            first[:, LANES:],
            second[:, :LANES],
            second[:, LANES:],
            person[:, :LANES],
            person[:, LANES:],
            jnp.zeros((2, LANES), F32),
        ],
        axis=0,
    )
    tiles[...] = jnp.broadcast_to(tile[None], (owners, MSG, LANES)).reshape(owners * MSG, LANES)
    tiles[pl.ds(WANT_ROW, owners, stride=MSG), :] = wanted
    message[...] = tiles[...].reshape(owners, MSG, LANES).astype(BF16)
    keep.wait()


def project_kernel(band, items_in, weights_in, table, items, weights, tiles, sems):
    stored, features = items.shape
    width = weights.shape[1]
    copies = [
        pltpu.make_async_copy(items_in, items, sems.at[0]),
        pltpu.make_async_copy(weights_in.at[0, pl.ds(width - features, features)], weights, sems.at[1]),
    ]
    for copy in copies:
        copy.start()
    for copy in copies:
        copy.wait()
    chunks = width // LANES
    copies = []
    for n in range(stored // band):
        for c in range(0, chunks, 2):
            left = items[n * band : (n + 1) * band, :]
            product = dot(left, weights[:, c * LANES : (c + 2) * LANES])
            for i in range(2):
                to = pl.ds(n * band * chunks + c + i, band, stride=chunks)
                tiles[to, :] = product[:, i * LANES : (i + 1) * LANES]
        whole = pl.ds(n * band * chunks, band * chunks)
        copies.append(pltpu.make_async_copy(tiles.at[whole], table.at[whole], sems.at[2 + n]))
        copies[-1].start()
    for copy in copies:
        copy.wait()


def rank_kernel(
    units,
    ranks,
    block,
    stretch,
    got,
    table_in,
    items,
    weights_in,
    bias,
    out_weight,
    logits,
    early,
    table,
    weights,
    tiles,
    features,
    people,
    greetings,
    first,
    state,
    rounded,
    answer,
    picks,
    picked,
    sems,
):
    sources = got.shape[0]
    rows = ranks * sources
    layers, width, _ = weights_in.shape
    stored = items.shape[0]
    chunks = width // LANES
    own = early.shape[0] // LANES
    copies = [(weights_in.at[0, pl.ds(0, own * LANES)], early), (table_in, table)]
    copies += [(weights_in.at[i], weights.at[i - 1]) for i in range(1, layers)]
    copies = [pltpu.make_async_copy(a, b, sems.at[i]) for i, (a, b) in enumerate(copies)]
    for copy in copies[:2]:
        copy.start()
    reqs = lax.axis_size("req")
    tiles[...] = got[...].astype(F32).reshape(sources * MSG, LANES)
    wanted = tiles[pl.ds(WANT_ROW, sources, stride=MSG), :]
    lane = iota((sources, LANES), 1)
    low = wanted.astype(I32)
    high = pltpu.roll(wanted, HALF, axis=1).astype(I32)
    within = low + 256 * (high & 3)
    person = ((high >> 2) & 31) * reqs + iota((sources, LANES), 0) % reqs
    split = (stored * chunks - 1).bit_length()
    picks[...] = within * chunks + ((person * chunks) << split)
    fetch = pltpu.make_async_copy(picks, picked, sems.at[len(copies)])
    fetch.start()
    users = [tiles[pl.ds(USER_ROW + i, sources, stride=MSG), :] for i in range(own)]
    blank = jnp.zeros((sources, LANES), F32)
    for c in range(chunks):
        people[pl.ds(c, sources, stride=chunks), :] = users[c] if c < own else blank
    flat = jnp.concatenate(users, axis=1).astype(BF16)

    def greet(sums):
        left = jnp.concatenate([flat] * (ranks // 2), axis=0)
        for turn in range(width // block):
            to = slice(turn * block, (turn + 1) * block)
            pltpu.matmul_push_rhs(early[:, to], turn // 2, turn % 2)
            pltpu.matmul_acc_lhs(sums[turn], left, turn // 2)
        for turn in range(width // block):
            product = pltpu.matmul_pop(sums[turn])[:sources]
            product = product + bias[0:1, turn * block : (turn + 1) * block]
            for i in range(0, block, LANES):
                c = (turn * block + i) // LANES
                greetings[pl.ds(c, sources, stride=chunks), :] = product[:, i : i + LANES]

    for c in range(chunks):
        part = jnp.zeros((stored, LANES), F32)
        if c >= own:
            part = items[:, (c - own) * LANES : (c - own + 1) * LANES].astype(F32)
        features[pl.ds(c, stored, stride=chunks), :] = part
    answer[...] = jnp.zeros(answer.shape, F32)

    def gather(slot, unit, some):
        values = []
        for n in some:
            k, source = n // sources, n % sources
            both = picked[source, unit * ranks + k]
            row = pl.ds(pl.multiple_of(both & ((1 << split) - 1), chunks), chunks)
            man = pl.ds(pl.multiple_of(both >> split, chunks), chunks)
            start = features[row, :] + people[man, :]
            values.append((n, start, start * (table[row, :] + greetings[man, :]) + start))
        for n, start, new in values:
            first[slot, pl.ds(n, chunks, stride=stretch), :] = start
            state[slot, pl.ds(n, chunks, stride=stretch), :] = new

    def lines(c, start, count):
        return slice(c * stretch + start, c * stretch + start + count)

    def begin(s, carry):
        for k in range(ranks):
            values = []
            for u in range(8):
                source = s * 8 + u
                both = picked[source, k]
                row = pl.ds(pl.multiple_of(both & ((1 << split) - 1), chunks), chunks)
                man = pl.ds(pl.multiple_of(both >> split, chunks), chunks)
                start = features[row, :] + people[man, :]
                new = start * (table[row, :] + greetings[man, :]) + start
                values.append((k * sources + source, start, new))
            for n, start, new in values:
                first[0, pl.ds(n, chunks, stride=stretch), :] = start
                state[0, pl.ds(n, chunks, stride=stretch), :] = new
        return carry

    halves = 2
    half = rows // halves
    depth = width // block
    blocks = [(u, l, p) for u in range(units) for l in range(1, layers) for p in range(depth // 2)]
    turns = [(*b, k) for b in blocks for k in range(depth)]
    share = -(-rows // (((layers - 1) * depth // 2 - 1) * depth))
    following = [list(range(rows)) for _ in range(units - 1)] + [[]]
    parts = [[jnp.zeros((half, LANES), F32) for _ in range(halves)] for _ in range(units)]

    def push(turn):
        _, layer, p, k = turns[turn]
        if p == 0 and k == 0 and turns[turn][0] == 0:
            copies[1 + layer].wait()
        for x in range(2):
            n = (2 * p + x) * block
            tile = weights[layer - 1, k * block : (k + 1) * block, n : n + block]
            pltpu.matmul_push_rhs(tile, turn % 2, x)

    def finish(unit, layer, p, h, x, total):
        n = (2 * p + x) * block
        product = pltpu.matmul_pop(total) + bias[layer : layer + 1, n : n + block]
        for i in range(0, block, LANES):
            at = lines((n + i) // LANES, h * half, half)
            new = first[unit % 2, at, :] * product[:, i : i + LANES] + state[unit % 2, at, :]
            if layer < layers - 1:
                state[unit % 2, at, :] = new
                rounded[layer % 2, h * half : (h + 1) * half, n + i : n + i + LANES] = new.astype(BF16)
            else:
                parts[unit][h] = parts[unit][h] + new * out_weight[:, n + i : n + i + LANES]
        if (layer, p, x) == (layers - 1, depth // 2 - 1, 1):
            value = lane_sum(parts[unit][h])
            for k in range(half // sources):
                j = unit * ranks + h * half // sources + k
                mine = value[k * sources : (k + 1) * sources]
                answer[...] += jnp.where(lane == j, mine, 0.0)

    def network(*sums):
        def total(block_at, h, x):
            return sums[(block_at % 2) * 4 + h * 2 + x]

        copies[0].wait()
        greet(sums)
        copies[2].start()
        fetch.wait()
        copies[1].wait()
        for copy in copies[3:]:
            copy.start()
        lax.fori_loop(0, sources // 8, begin, 0)
        push(0)
        for at, (unit, layer, p) in enumerate(blocks):
            waiting = [] if at == 0 else [(h, x) for h in range(halves) for x in range(2)]
            for k in range(depth):
                turn = at * depth + k
                if turn + 1 < len(turns):
                    push(turn + 1)
                for h in range(halves):
                    own_rows = slice(h * half, (h + 1) * half)
                    if layer == 1 and p == 0:
                        for c in range(k * block // LANES, (k + 1) * block // LANES):
                            entered = state[unit % 2, lines(c, h * half, half), :]
                            rounded[0, own_rows, c * LANES : (c + 1) * LANES] = entered.astype(BF16)
                    left = rounded[(layer + 1) % 2, own_rows, k * block : (k + 1) * block]
                    for x in range(2):
                        pltpu.matmul_acc_lhs(total(at, h, x), left, None if h else turn % 2)
                if (layer, p) != (1, 0):
                    gather(1 - unit % 2, unit + 1, following[unit][:share])
                    del following[unit][:share]
                for _ in range((1, 2, 1, 0)[k] if waiting else 0):
                    h, x = waiting.pop(0)
                    finish(*blocks[at - 1], h, x, total(at - 1, h, x))
        for h in range(halves):
            for x in range(2):
                finish(*blocks[-1], h, x, total(len(blocks) - 1, h, x))

    pl.run_scoped(network, *[pltpu.ACC(mxu_id=i % 2)((half, block), F32) for i in range(8)])
    logits[...] = answer[...].reshape(logits.shape)


def score_kernel(block, looked, got, user, codes, scores, tiles, tables, wide):
    sources = got.shape[0]
    requests, d_user = user.shape
    subs, count = codes.shape
    tiles[...] = got[...].astype(F32).reshape(sources * MSG, LANES)
    book = [tiles[pl.ds(i, sources, stride=MSG), :].astype(BF16) for i in range(CB_ROWS)]
    even = jnp.concatenate(book[:2], axis=1)
    odd = jnp.concatenate(book[2:], axis=1)
    column = iota((d_user, sources), 0)
    people = user[...]
    of_even = dot(people, as_bf16(column == 2 * iota((d_user, sources), 1))).astype(BF16)
    of_odd = dot(people, as_bf16(column == 2 * iota((d_user, sources), 1) + 1)).astype(BF16)
    per_sub = sources // subs
    zero = jnp.zeros((), BF16)
    for m in range(subs):
        mine = iota((requests, sources), 1) // per_sub == m
        table = dot(jnp.where(mine, of_even, zero), even) + dot(jnp.where(mine, of_odd, zero), odd)
        table = table.astype(BF16)
        if m < looked:
            wide[m] = table.astype(F32)
        else:
            tables[:, m * CODES : (m + 1) * CODES] = table

    code = lax.broadcasted_iota(jnp.int16, (CODES, block), 0)
    one = jnp.ones((), BF16)
    groups, spans = requests // 8, block // LANES
    order = sorted(
        [((i + 0.5) / looked, i) for i in range(looked)]
        + [((i + 0.5) / (subs - looked), i + looked) for i in range(subs - looked)]
    )

    def pick(values, index):
        return jnp.take_along_axis(values, index, axis=1, mode="promise_in_bounds")

    def step(j, carry):
        at = pl.ds(pl.multiple_of(j * block, block), block)
        total = jnp.zeros((requests, block), F32)
        sums = [[jnp.zeros((8, LANES), F32) for _ in range(spans)] for _ in range(groups)]
        for _, m in order:
            row = codes[m : m + 1, at]
            if m >= looked:
                now = jnp.broadcast_to(row, (16, block)).astype(jnp.int16)
                now = jnp.concatenate([now] * (CODES // 16), axis=0)
                onehot = jnp.where(code == now, one, zero)
                total = total + dot(tables[:, m * CODES : (m + 1) * CODES], onehot)
                continue
            for b in range(spans):
                now = jnp.broadcast_to(row[:, b * LANES : (b + 1) * LANES], (8, LANES))
                index = now & (LANES - 1)
                upper = now >= LANES
                for g in range(groups):
                    low = pick(wide[m, g * 8 : (g + 1) * 8, :LANES], index)
                    high = pick(wide[m, g * 8 : (g + 1) * 8, LANES:], index)
                    sums[g][b] = sums[g][b] + jnp.where(upper, high, low)
        rows = [jnp.concatenate(group, axis=1) for group in sums]
        scores[:, at] = total + jnp.concatenate(rows, axis=0)
        return carry

    lax.fori_loop(0, count // block, step, 0)


def collect_kernel(back, meta, logits):
    cand_dev, requests = logits.shape
    total = meta.shape[0]
    owners = back.shape[0]
    lane = iota((total, owners), 1)
    answers = back[...].reshape(owners, LANES)
    pick = as_bf16(meta[:, 0:1] == lane)
    top = answers.astype(BF16).astype(F32)
    rest = answers - top
    middle = rest.astype(BF16).astype(F32)
    last = rest - middle
    pieces = top + pltpu.roll(middle, PIECE, axis=1) + pltpu.roll(last, 2 * PIECE, axis=1)
    rows = dot(pick, pieces.astype(BF16))
    mine = (lane % PIECE == meta[:, 1:2]) & (lane < 3 * PIECE)
    value = lane_sum(jnp.where(mine, rows, 0.0))
    diagonal = iota((total, requests), 0) % requests == iota((total, requests), 1)
    spread = jnp.where(diagonal, value, 0.0)
    logits[...] = jnp.sum(spread.reshape(cand_dev, requests, requests), axis=1)


def on_device(
    user_emb,
    codebooks,
    item_codes,
    item_place,
    candidates,
    item_features,
    cross_weights,
    cross_bias,
    out_weight,
):
    requests, d_user = user_emb.shape
    cand_dev = candidates.shape[1]
    total = requests * cand_dev
    owners = lax.axis_size("item") * lax.axis_size("req")
    items = item_codes.shape[0]
    layers, width, _ = cross_weights.shape
    whole = pltpu.CompilerParams(vmem_limit_bytes=60 << 20)
    limit = pltpu.CompilerParams(vmem_limit_bytes=24 << 20)
    message, meta = pl.pallas_call(
        prepare_kernel,
        out_shape=(
            jax.ShapeDtypeStruct((owners, MSG, LANES), BF16),
            jax.ShapeDtypeStruct((total, LANES), I32),
        ),
        in_specs=[HBM] * 4,
        out_specs=(VMEM, HBM),
        scratch_shapes=[
            pltpu.VMEM((owners * MSG, LANES), F32),
            pltpu.VMEM((cand_dev, requests), I32),
            pltpu.VMEM((item_place.shape[0] // LANES, LANES), I32),
            pltpu.VMEM(codebooks.shape[:0:-1], BF16),
            pltpu.VMEM(user_emb.shape, BF16),
            pltpu.VMEM((total, LANES), I32),
            pltpu.SemaphoreType.DMA((5,)),
        ],
        compiler_params=whole,
        name="prepare",
    )(
        candidates.T,
        item_place.reshape(-1, LANES),
        jnp.swapaxes(codebooks, 1, 2)[0],
        user_emb,
    )
    got = lax.all_to_all(message, ("item", "req"), split_axis=0, concat_axis=0, tiled=True)
    stored, features = item_features.shape
    chunks = width // LANES
    lines = stored * chunks
    band = stored // 4
    table = pl.pallas_call(
        functools.partial(project_kernel, band),
        out_shape=jax.ShapeDtypeStruct((lines, LANES), F32),
        in_specs=[HBM, HBM],
        out_specs=HBM,
        scratch_shapes=[
            pltpu.VMEM(item_features.shape, BF16),
            pltpu.VMEM((features, width), BF16),
            pltpu.VMEM((lines, LANES), F32),
            pltpu.SemaphoreType.DMA((2 + stored // band,)),
        ],
        compiler_params=whole,
        name="project",
        cost_estimate=pl.CostEstimate(flops=2 << 30, bytes_accessed=12 << 20, transcendentals=0),
    )(item_features, cross_weights)
    capacity = 3 * total // owners
    ranks = 4
    rows = ranks * owners
    stretch = rows + 8
    answers = pl.pallas_call(
        functools.partial(rank_kernel, capacity // ranks, ranks, 256, stretch),
        out_shape=jax.ShapeDtypeStruct((owners, 1, LANES), F32),
        in_specs=[VMEM, HBM, VMEM, HBM, VMEM, VMEM],
        out_specs=VMEM,
        scratch_shapes=[
            pltpu.VMEM((d_user, width), BF16),
            pltpu.VMEM((lines, LANES), F32),
            pltpu.VMEM((layers - 1, width, width), BF16),
            pltpu.VMEM((owners * MSG, LANES), F32),
            pltpu.VMEM((lines, LANES), F32),
            pltpu.VMEM((owners * chunks, LANES), F32),
            pltpu.VMEM((owners * chunks, LANES), F32),
            pltpu.VMEM((2, stretch * chunks, LANES), F32),
            pltpu.VMEM((2, stretch * chunks, LANES), F32),
            pltpu.VMEM((2, rows, width), BF16),
            pltpu.VMEM((owners, LANES), F32),
            pltpu.VMEM((owners, LANES), I32),
            pltpu.SMEM((owners, LANES), I32),
            pltpu.SemaphoreType.DMA((layers + 2,)),
        ],
        compiler_params=pltpu.CompilerParams(vmem_limit_bytes=50 << 20),
        name="rank",
        cost_estimate=pl.CostEstimate(flops=12 << 30, bytes_accessed=10 << 20, transcendentals=0),
    )(got, table, item_features, cross_weights, cross_bias, out_weight.reshape(1, width))
    back = lax.all_to_all(answers, ("item", "req"), split_axis=0, concat_axis=0, tiled=True)
    looked = 14
    scores = pl.pallas_call(
        functools.partial(score_kernel, 512, looked),
        out_shape=jax.ShapeDtypeStruct((requests, items), F32),
        in_specs=[VMEM] * 3,
        out_specs=VMEM,
        scratch_shapes=[
            pltpu.VMEM((owners * MSG, LANES), F32),
            pltpu.VMEM((requests, item_codes.shape[1] * CODES), BF16),
            pltpu.VMEM((looked, requests, CODES), F32),
        ],
        compiler_params=limit,
        name="scores",
        cost_estimate=pl.CostEstimate(flops=2 << 30, bytes_accessed=40 << 20, transcendentals=0),
    )(got, user_emb, item_codes.T)
    logits = pl.pallas_call(
        collect_kernel,
        out_shape=jax.ShapeDtypeStruct((cand_dev, requests), F32),
        in_specs=[VMEM] * 2,
        out_specs=VMEM,
        compiler_params=limit,
        name="collect",
    )(back, meta)
    return scores, logits.T


def solution(mesh):
    placed = (
        P("req", None),
        P("item", None, None),
        P("item", None),
        P(),
        P("req", "item"),
        P(("item", "req"), None),
        P(),
        P(),
        P(),
    )
    return jax.shard_map(
        on_device,
        mesh=mesh,
        in_specs=placed,
        out_specs=(P("req", "item"), P("req", "item")),
        check_vma=False,
    )
```

```python
import functools

import jax
import jax.numpy as jnp
from jax import lax
from jax.experimental import pallas as pl
from jax.experimental.pallas import tpu as pltpu
from jax.sharding import PartitionSpec as P

F32 = jnp.float32
BF16 = jnp.bfloat16
I32 = jnp.int32
HBM = pl.BlockSpec(memory_space=pltpu.HBM)
VMEM = pl.BlockSpec(memory_space=pltpu.VMEM)
LANES = 128
MSG = 8
CB_ROWS = 4
USER_ROW = 4
WANT_ROW = 6
HALF = 64
CODES = 256
PIECE = 32


def dot(a, b, dims=(((1,), (0,)), ((), ()))):
    return lax.dot_general(a, b, dims, preferred_element_type=F32)


def iota(shape, axis):
    return lax.broadcasted_iota(I32, shape, axis)


def lane_sum(x):
    return jnp.sum(x, axis=1, keepdims=True)


def as_bf16(mask):
    return jnp.where(mask, 1.0, 0.0).astype(BF16)


def prepare_kernel(
    cand_in, place_in, codebook_in, user_in, message, meta, tiles, cand, place, codebook, user, sems
):
    pairs = ((cand_in, cand), (place_in, place), (codebook_in, codebook), (user_in, user))
    copies = [pltpu.make_async_copy(a, b, sems.at[i]) for i, (a, b) in enumerate(pairs)]
    for copy in copies:
        copy.start()
    for copy in copies:
        copy.wait()
    cand_dev, requests = cand.shape
    total = cand_dev * requests
    owners = message.shape[0]
    blocks = place.shape[0]
    item = lax.axis_index("item")
    req = lax.axis_index("req")
    ids = cand[...].astype(F32)
    spread = jnp.concatenate(
        [jnp.broadcast_to(ids[c : c + 1, :], (requests, requests)) for c in range(cand_dev)], axis=0
    )
    own_request = iota((total, requests), 0) % requests
    diagonal = own_request == iota((total, requests), 1)
    ids = lane_sum(jnp.where(diagonal, spread, 0.0)).astype(I32)
    where_row = as_bf16((ids >> 7) == iota((total, blocks), 1))
    stored = place[...]
    parts = jnp.concatenate(
        [
            (stored & 255).astype(F32).astype(BF16),
            ((stored >> 8) & 255).astype(F32).astype(BF16),
            (stored >> 16).astype(F32).astype(BF16),
        ],
        axis=1,
    )
    found = dot(where_row, parts)
    found = found[:, :LANES] + 256.0 * found[:, LANES : 2 * LANES] + 65536.0 * found[:, 2 * LANES :]
    lane = iota((total, LANES), 1)
    slot = lane_sum(jnp.where((ids & 127) == lane, found, 0.0)).astype(I32)
    rows_dev = blocks * LANES // owners
    shift = rows_dev.bit_length() - 1
    owner = slot >> shift
    within = slot & (rows_dev - 1)
    hit = owner == lane
    hits = as_bf16(hit)
    earlier = as_bf16(iota((total, total), 1) < iota((total, total), 0))
    rank = lane_sum(jnp.where(hit, dot(earlier, hits), 0.0)).astype(I32)
    meta[...] = jnp.where(lane == 0, owner, rank)
    request = iota((total, 1), 0) % requests
    low = (within & 255).astype(F32)
    high = ((within >> 8) + 4 * request + 128).astype(F32)
    entry = jnp.where(lane == rank, low, 0.0) + jnp.where(lane == rank + HALF, high, 0.0)
    wanted = dot(hits, entry.astype(BF16), (((0,), (0,)), ((), ())))
    book = codebook[...].astype(F32)
    sub = iota(book.shape, 0)
    first = jnp.sum(jnp.where(sub == 2 * req, book, 0.0), axis=0, keepdims=True)
    second = jnp.sum(jnp.where(sub == 2 * req + 1, book, 0.0), axis=0, keepdims=True)
    people = user[...].astype(F32)
    person = jnp.sum(jnp.where(iota(people.shape, 0) == item, people, 0.0), axis=0, keepdims=True)
    tile = jnp.concatenate(
        [
            first[:, :LANES],
            first[:, LANES:],
            second[:, :LANES],
            second[:, LANES:],
            person[:, :LANES],
            person[:, LANES:],
            jnp.zeros((2, LANES), F32),
        ],
        axis=0,
    )
    tiles[...] = jnp.broadcast_to(tile[None], (owners, MSG, LANES)).reshape(owners * MSG, LANES)
    tiles[pl.ds(WANT_ROW, owners, stride=MSG), :] = wanted
    message[...] = tiles[...].reshape(owners, MSG, LANES).astype(BF16)


def project_kernel(band, items_in, weights_in, table, items, weights, tiles, sems):
    stored, features = items.shape
    width = weights.shape[1]
    copies = [
        pltpu.make_async_copy(items_in, items, sems.at[0]),
        pltpu.make_async_copy(weights_in.at[0, pl.ds(width - features, features)], weights, sems.at[1]),
    ]
    for copy in copies:
        copy.start()
    for copy in copies:
        copy.wait()
    chunks = width // LANES
    copies = []
    for n in range(stored // band):
        for c in range(0, chunks, 2):
            left = items[n * band : (n + 1) * band, :]
            product = dot(left, weights[:, c * LANES : (c + 2) * LANES])
            for i in range(2):
                to = pl.ds(n * band * chunks + c + i, band, stride=chunks)
                tiles[to, :] = product[:, i * LANES : (i + 1) * LANES]
        whole = pl.ds(n * band * chunks, band * chunks)
        copies.append(pltpu.make_async_copy(tiles.at[whole], table.at[whole], sems.at[2 + n]))
        copies[-1].start()
    for copy in copies:
        copy.wait()


def rank_kernel(
    units,
    ranks,
    block,
    stretch,
    got,
    table_in,
    items,
    weights_in,
    bias,
    out_weight,
    logits,
    early,
    table,
    weights,
    tiles,
    features,
    people,
    greetings,
    first,
    state,
    rounded,
    answer,
    picks,
    picked,
    sems,
):
    sources = got.shape[0]
    rows = ranks * sources
    layers, width, _ = weights_in.shape
    stored = items.shape[0]
    chunks = width // LANES
    own = early.shape[0] // LANES
    copies = [(weights_in.at[0, pl.ds(0, own * LANES)], early), (table_in, table)]
    copies += [(weights_in.at[i], weights.at[i - 1]) for i in range(1, layers)]
    copies = [pltpu.make_async_copy(a, b, sems.at[i]) for i, (a, b) in enumerate(copies)]
    for copy in copies[:2]:
        copy.start()
    reqs = lax.axis_size("req")
    tiles[...] = got[...].astype(F32).reshape(sources * MSG, LANES)
    wanted = tiles[pl.ds(WANT_ROW, sources, stride=MSG), :]
    lane = iota((sources, LANES), 1)
    low = wanted.astype(I32)
    high = pltpu.roll(wanted, HALF, axis=1).astype(I32)
    within = low + 256 * (high & 3)
    person = ((high >> 2) & 31) * reqs + iota((sources, LANES), 0) % reqs
    split = (stored * chunks - 1).bit_length()
    picks[...] = within * chunks + ((person * chunks) << split)
    fetch = pltpu.make_async_copy(picks, picked, sems.at[len(copies)])
    fetch.start()
    users = [tiles[pl.ds(USER_ROW + i, sources, stride=MSG), :] for i in range(own)]
    blank = jnp.zeros((sources, LANES), F32)
    for c in range(chunks):
        people[pl.ds(c, sources, stride=chunks), :] = users[c] if c < own else blank
    flat = jnp.concatenate(users, axis=1).astype(BF16)

    def greet(sums):
        left = jnp.concatenate([flat] * (ranks // 2), axis=0)
        for turn in range(width // block):
            to = slice(turn * block, (turn + 1) * block)
            pltpu.matmul_push_rhs(early[:, to], turn // 2, turn % 2)
            pltpu.matmul_acc_lhs(sums[turn], left, turn // 2)
        for turn in range(width // block):
            product = pltpu.matmul_pop(sums[turn])[:sources]
            product = product + bias[0:1, turn * block : (turn + 1) * block]
            for i in range(0, block, LANES):
                c = (turn * block + i) // LANES
                greetings[pl.ds(c, sources, stride=chunks), :] = product[:, i : i + LANES]

    for c in range(chunks):
        part = jnp.zeros((stored, LANES), F32)
        if c >= own:
            part = items[:, (c - own) * LANES : (c - own + 1) * LANES].astype(F32)
        features[pl.ds(c, stored, stride=chunks), :] = part
    answer[...] = jnp.zeros(answer.shape, F32)

    def gather(slot, unit, some):
        values = []
        for n in some:
            k, source = n // sources, n % sources
            both = picked[source, unit * ranks + k]
            row = pl.ds(pl.multiple_of(both & ((1 << split) - 1), chunks), chunks)
            man = pl.ds(pl.multiple_of(both >> split, chunks), chunks)
            start = features[row, :] + people[man, :]
            values.append((n, start, start * (table[row, :] + greetings[man, :]) + start))
        for n, start, new in values:
            first[slot, pl.ds(n, chunks, stride=stretch), :] = start
            state[slot, pl.ds(n, chunks, stride=stretch), :] = new

    def lines(c, start, count):
        return slice(c * stretch + start, c * stretch + start + count)

    def begin(s, carry):
        for k in range(ranks):
            values = []
            for u in range(8):
                source = s * 8 + u
                both = picked[source, k]
                row = pl.ds(pl.multiple_of(both & ((1 << split) - 1), chunks), chunks)
                man = pl.ds(pl.multiple_of(both >> split, chunks), chunks)
                start = features[row, :] + people[man, :]
                new = start * (table[row, :] + greetings[man, :]) + start
                values.append((k * sources + source, start, new))
            for n, start, new in values:
                first[0, pl.ds(n, chunks, stride=stretch), :] = start
                state[0, pl.ds(n, chunks, stride=stretch), :] = new
        return carry

    halves = 2
    half = rows // halves
    depth = width // block
    blocks = [(u, l, p) for u in range(units) for l in range(1, layers) for p in range(depth // 2)]
    turns = [(*b, k) for b in blocks for k in range(depth)]
    share = -(-rows // (((layers - 1) * depth // 2 - 1) * depth))
    following = [list(range(rows)) for _ in range(units - 1)] + [[]]
    parts = [[jnp.zeros((half, LANES), F32) for _ in range(halves)] for _ in range(units)]

    def push(turn):
        _, layer, p, k = turns[turn]
        if p == 0 and k == 0 and turns[turn][0] == 0:
            copies[1 + layer].wait()
        for x in range(2):
            n = (2 * p + x) * block
            tile = weights[layer - 1, k * block : (k + 1) * block, n : n + block]
            pltpu.matmul_push_rhs(tile, turn % 2, x)

    def finish(unit, layer, p, h, x, total):
        n = (2 * p + x) * block
        product = pltpu.matmul_pop(total) + bias[layer : layer + 1, n : n + block]
        for i in range(0, block, LANES):
            at = lines((n + i) // LANES, h * half, half)
            new = first[unit % 2, at, :] * product[:, i : i + LANES] + state[unit % 2, at, :]
            if layer < layers - 1:
                state[unit % 2, at, :] = new
                rounded[layer % 2, h * half : (h + 1) * half, n + i : n + i + LANES] = new.astype(BF16)
            else:
                parts[unit][h] = parts[unit][h] + new * out_weight[:, n + i : n + i + LANES]
        if (layer, p, x) == (layers - 1, depth // 2 - 1, 1):
            value = lane_sum(parts[unit][h])
            for k in range(half // sources):
                j = unit * ranks + h * half // sources + k
                mine = value[k * sources : (k + 1) * sources]
                answer[...] += jnp.where(lane == j, mine, 0.0)

    def network(*sums):
        def total(block_at, h, x):
            return sums[(block_at % 2) * 4 + h * 2 + x]

        copies[0].wait()
        greet(sums)
        copies[2].start()
        fetch.wait()
        copies[1].wait()
        for copy in copies[3:]:
            copy.start()
        lax.fori_loop(0, sources // 8, begin, 0)
        push(0)
        for at, (unit, layer, p) in enumerate(blocks):
            waiting = [] if at == 0 else [(h, x) for h in range(halves) for x in range(2)]
            for k in range(depth):
                turn = at * depth + k
                if turn + 1 < len(turns):
                    push(turn + 1)
                for h in range(halves):
                    own_rows = slice(h * half, (h + 1) * half)
                    if layer == 1 and p == 0:
                        for c in range(k * block // LANES, (k + 1) * block // LANES):
                            entered = state[unit % 2, lines(c, h * half, half), :]
                            rounded[0, own_rows, c * LANES : (c + 1) * LANES] = entered.astype(BF16)
                    left = rounded[(layer + 1) % 2, own_rows, k * block : (k + 1) * block]
                    for x in range(2):
                        pltpu.matmul_acc_lhs(total(at, h, x), left, None if h else turn % 2)
                if (layer, p) != (1, 0):
                    gather(1 - unit % 2, unit + 1, following[unit][:share])
                    del following[unit][:share]
                for _ in range((1, 2, 1, 0)[k] if waiting else 0):
                    h, x = waiting.pop(0)
                    finish(*blocks[at - 1], h, x, total(at - 1, h, x))
        for h in range(halves):
            for x in range(2):
                finish(*blocks[-1], h, x, total(len(blocks) - 1, h, x))

    pl.run_scoped(network, *[pltpu.ACC(mxu_id=i % 2)((half, block), F32) for i in range(8)])
    logits[...] = answer[...].reshape(logits.shape)


def score_kernel(block, looked, got, user, codes, scores, tiles, tables, wide):
    sources = got.shape[0]
    requests, d_user = user.shape
    subs, count = codes.shape
    tiles[...] = got[...].astype(F32).reshape(sources * MSG, LANES)
    book = [tiles[pl.ds(i, sources, stride=MSG), :].astype(BF16) for i in range(CB_ROWS)]
    even = jnp.concatenate(book[:2], axis=1)
    odd = jnp.concatenate(book[2:], axis=1)
    column = iota((d_user, sources), 0)
    people = user[...]
    of_even = dot(people, as_bf16(column == 2 * iota((d_user, sources), 1))).astype(BF16)
    of_odd = dot(people, as_bf16(column == 2 * iota((d_user, sources), 1) + 1)).astype(BF16)
    per_sub = sources // subs
    zero = jnp.zeros((), BF16)
    for m in range(subs):
        mine = iota((requests, sources), 1) // per_sub == m
        table = dot(jnp.where(mine, of_even, zero), even) + dot(jnp.where(mine, of_odd, zero), odd)
        table = table.astype(BF16)
        if m < looked:
            wide[m] = table.astype(F32)
        else:
            tables[:, m * CODES : (m + 1) * CODES] = table

    code = lax.broadcasted_iota(jnp.int16, (CODES, block), 0)
    one = jnp.ones((), BF16)
    groups, spans = requests // 8, block // LANES
    order = sorted(
        [((i + 0.5) / looked, i) for i in range(looked)]
        + [((i + 0.5) / (subs - looked), i + looked) for i in range(subs - looked)]
    )

    def pick(values, index):
        return jnp.take_along_axis(values, index, axis=1, mode="promise_in_bounds")

    def step(j, carry):
        at = pl.ds(pl.multiple_of(j * block, block), block)
        total = jnp.zeros((requests, block), F32)
        sums = [[jnp.zeros((8, LANES), F32) for _ in range(spans)] for _ in range(groups)]
        for _, m in order:
            row = codes[m : m + 1, at]
            if m >= looked:
                now = jnp.broadcast_to(row, (16, block)).astype(jnp.int16)
                now = jnp.concatenate([now] * (CODES // 16), axis=0)
                onehot = jnp.where(code == now, one, zero)
                total = total + dot(tables[:, m * CODES : (m + 1) * CODES], onehot)
                continue
            for b in range(spans):
                now = jnp.broadcast_to(row[:, b * LANES : (b + 1) * LANES], (8, LANES))
                index = now & (LANES - 1)
                upper = now >= LANES
                for g in range(groups):
                    low = pick(wide[m, g * 8 : (g + 1) * 8, :LANES], index)
                    high = pick(wide[m, g * 8 : (g + 1) * 8, LANES:], index)
                    sums[g][b] = sums[g][b] + jnp.where(upper, high, low)
        rows = [jnp.concatenate(group, axis=1) for group in sums]
        scores[:, at] = total + jnp.concatenate(rows, axis=0)
        return carry

    lax.fori_loop(0, count // block, step, 0)


def collect_kernel(back, meta, logits):
    cand_dev, requests = logits.shape
    total = meta.shape[0]
    owners = back.shape[0]
    lane = iota((total, owners), 1)
    answers = back[...].reshape(owners, LANES)
    pick = as_bf16(meta[:, 0:1] == lane)
    top = answers.astype(BF16).astype(F32)
    rest = answers - top
    middle = rest.astype(BF16).astype(F32)
    last = rest - middle
    pieces = top + pltpu.roll(middle, PIECE, axis=1) + pltpu.roll(last, 2 * PIECE, axis=1)
    rows = dot(pick, pieces.astype(BF16))
    mine = (lane % PIECE == meta[:, 1:2]) & (lane < 3 * PIECE)
    value = lane_sum(jnp.where(mine, rows, 0.0))
    diagonal = iota((total, requests), 0) % requests == iota((total, requests), 1)
    spread = jnp.where(diagonal, value, 0.0)
    logits[...] = jnp.sum(spread.reshape(cand_dev, requests, requests), axis=1)


def on_device(
    user_emb,
    codebooks,
    item_codes,
    item_place,
    candidates,
    item_features,
    cross_weights,
    cross_bias,
    out_weight,
):
    requests, d_user = user_emb.shape
    cand_dev = candidates.shape[1]
    total = requests * cand_dev
    owners = lax.axis_size("item") * lax.axis_size("req")
    items = item_codes.shape[0]
    layers, width, _ = cross_weights.shape
    whole = pltpu.CompilerParams(vmem_limit_bytes=60 << 20)
    limit = pltpu.CompilerParams(vmem_limit_bytes=24 << 20)
    message, meta = pl.pallas_call(
        prepare_kernel,
        out_shape=(
            jax.ShapeDtypeStruct((owners, MSG, LANES), BF16),
            jax.ShapeDtypeStruct((total, LANES), I32),
        ),
        in_specs=[HBM] * 4,
        out_specs=(VMEM, VMEM),
        scratch_shapes=[
            pltpu.VMEM((owners * MSG, LANES), F32),
            pltpu.VMEM((cand_dev, requests), I32),
            pltpu.VMEM((item_place.shape[0] // LANES, LANES), I32),
            pltpu.VMEM(codebooks.shape[:0:-1], BF16),
            pltpu.VMEM(user_emb.shape, BF16),
            pltpu.SemaphoreType.DMA((4,)),
        ],
        compiler_params=whole,
        name="prepare",
    )(
        candidates.T,
        item_place.reshape(-1, LANES),
        jnp.swapaxes(codebooks, 1, 2)[0],
        user_emb,
    )
    got = lax.all_to_all(message, ("item", "req"), split_axis=0, concat_axis=0, tiled=True)
    stored, features = item_features.shape
    chunks = width // LANES
    lines = stored * chunks
    band = stored // 4
    table = pl.pallas_call(
        functools.partial(project_kernel, band),
        out_shape=jax.ShapeDtypeStruct((lines, LANES), F32),
        in_specs=[HBM, HBM],
        out_specs=HBM,
        scratch_shapes=[
            pltpu.VMEM(item_features.shape, BF16),
            pltpu.VMEM((features, width), BF16),
            pltpu.VMEM((lines, LANES), F32),
            pltpu.SemaphoreType.DMA((2 + stored // band,)),
        ],
        compiler_params=whole,
        name="project",
        cost_estimate=pl.CostEstimate(flops=2 << 30, bytes_accessed=12 << 20, transcendentals=0),
    )(item_features, cross_weights)
    capacity = 3 * total // owners
    ranks = 4
    rows = ranks * owners
    stretch = rows + 8
    answers = pl.pallas_call(
        functools.partial(rank_kernel, capacity // ranks, ranks, 256, stretch),
        out_shape=jax.ShapeDtypeStruct((owners, 1, LANES), F32),
        in_specs=[VMEM, HBM, VMEM, HBM, VMEM, VMEM],
        out_specs=VMEM,
        scratch_shapes=[
            pltpu.VMEM((d_user, width), BF16),
            pltpu.VMEM((lines, LANES), F32),
            pltpu.VMEM((layers - 1, width, width), BF16),
            pltpu.VMEM((owners * MSG, LANES), F32),
            pltpu.VMEM((lines, LANES), F32),
            pltpu.VMEM((owners * chunks, LANES), F32),
            pltpu.VMEM((owners * chunks, LANES), F32),
            pltpu.VMEM((2, stretch * chunks, LANES), F32),
            pltpu.VMEM((2, stretch * chunks, LANES), F32),
            pltpu.VMEM((2, rows, width), BF16),
            pltpu.VMEM((owners, LANES), F32),
            pltpu.VMEM((owners, LANES), I32),
            pltpu.SMEM((owners, LANES), I32),
            pltpu.SemaphoreType.DMA((layers + 2,)),
        ],
        compiler_params=pltpu.CompilerParams(vmem_limit_bytes=50 << 20),
        name="rank",
        cost_estimate=pl.CostEstimate(flops=12 << 30, bytes_accessed=10 << 20, transcendentals=0),
    )(got, table, item_features, cross_weights, cross_bias, out_weight.reshape(1, width))
    back = lax.all_to_all(answers, ("item", "req"), split_axis=0, concat_axis=0, tiled=True)
    looked = 14
    scores = pl.pallas_call(
        functools.partial(score_kernel, 512, looked),
        out_shape=jax.ShapeDtypeStruct((requests, items), F32),
        in_specs=[VMEM] * 3,
        out_specs=VMEM,
        scratch_shapes=[
            pltpu.VMEM((owners * MSG, LANES), F32),
            pltpu.VMEM((requests, item_codes.shape[1] * CODES), BF16),
            pltpu.VMEM((looked, requests, CODES), F32),
        ],
        compiler_params=limit,
        name="scores",
        cost_estimate=pl.CostEstimate(flops=2 << 30, bytes_accessed=40 << 20, transcendentals=0),
    )(got, user_emb, item_codes.T)
    logits = pl.pallas_call(
        collect_kernel,
        out_shape=jax.ShapeDtypeStruct((cand_dev, requests), F32),
        in_specs=[VMEM] * 2,
        out_specs=VMEM,
        compiler_params=limit,
        name="collect",
    )(back, meta)
    return scores, logits.T


def solution(mesh):
    placed = (
        P("req", None),
        P("item", None, None),
        P("item", None),
        P(),
        P("req", "item"),
        P(("item", "req"), None),
        P(),
        P(),
        P(),
    )
    return jax.shard_map(
        on_device,
        mesh=mesh,
        in_specs=placed,
        out_specs=(P("req", "item"), P("req", "item")),
        check_vma=False,
    )
```

```python
import functools

import jax
import jax.numpy as jnp
from jax import lax
from jax.experimental import pallas as pl
from jax.experimental.pallas import tpu as pltpu
from jax.sharding import PartitionSpec as P

F32 = jnp.float32
BF16 = jnp.bfloat16
I32 = jnp.int32
HBM = pl.BlockSpec(memory_space=pltpu.HBM)
VMEM = pl.BlockSpec(memory_space=pltpu.VMEM)
LANES = 128
MSG = 8
CB_ROWS = 4
USER_ROW = 4
WANT_ROW = 6
HALF = 64
CODES = 256
PIECE = 32


def dot(a, b, dims=(((1,), (0,)), ((), ()))):
    return lax.dot_general(a, b, dims, preferred_element_type=F32)


def iota(shape, axis):
    return lax.broadcasted_iota(I32, shape, axis)


def lane_sum(x):
    return jnp.sum(x, axis=1, keepdims=True)


def as_bf16(mask):
    return jnp.where(mask, 1.0, 0.0).astype(BF16)


def prepare_kernel(
    cand_in, place_in, codebook_in, user_in, message, meta, tiles, cand, place, codebook, user, sems
):
    pairs = ((cand_in, cand), (place_in, place), (codebook_in, codebook), (user_in, user))
    copies = [pltpu.make_async_copy(a, b, sems.at[i]) for i, (a, b) in enumerate(pairs)]
    for copy in copies:
        copy.start()
    for copy in copies:
        copy.wait()
    cand_dev, requests = cand.shape
    total = cand_dev * requests
    owners = message.shape[0]
    blocks = place.shape[0]
    item = lax.axis_index("item")
    req = lax.axis_index("req")
    ids = cand[...].astype(F32)
    spread = jnp.concatenate(
        [jnp.broadcast_to(ids[c : c + 1, :], (requests, requests)) for c in range(cand_dev)], axis=0
    )
    own_request = iota((total, requests), 0) % requests
    diagonal = own_request == iota((total, requests), 1)
    ids = lane_sum(jnp.where(diagonal, spread, 0.0)).astype(I32)
    where_row = as_bf16((ids >> 7) == iota((total, blocks), 1))
    stored = place[...]
    parts = jnp.concatenate(
        [
            (stored & 255).astype(F32).astype(BF16),
            ((stored >> 8) & 255).astype(F32).astype(BF16),
            (stored >> 16).astype(F32).astype(BF16),
        ],
        axis=1,
    )
    found = dot(where_row, parts)
    found = found[:, :LANES] + 256.0 * found[:, LANES : 2 * LANES] + 65536.0 * found[:, 2 * LANES :]
    lane = iota((total, LANES), 1)
    slot = lane_sum(jnp.where((ids & 127) == lane, found, 0.0)).astype(I32)
    rows_dev = blocks * LANES // owners
    shift = rows_dev.bit_length() - 1
    owner = slot >> shift
    within = slot & (rows_dev - 1)
    hit = owner == lane
    hits = as_bf16(hit)
    earlier = as_bf16(iota((total, total), 1) < iota((total, total), 0))
    rank = lane_sum(jnp.where(hit, dot(earlier, hits), 0.0)).astype(I32)
    meta[...] = jnp.where(lane == 0, owner, rank)
    request = iota((total, 1), 0) % requests
    low = (within & 255).astype(F32)
    high = ((within >> 8) + 4 * request + 128).astype(F32)
    entry = jnp.where(lane == rank, low, 0.0) + jnp.where(lane == rank + HALF, high, 0.0)
    wanted = dot(hits, entry.astype(BF16), (((0,), (0,)), ((), ())))
    book = codebook[...].astype(F32)
    sub = iota(book.shape, 0)
    first = jnp.sum(jnp.where(sub == 2 * req, book, 0.0), axis=0, keepdims=True)
    second = jnp.sum(jnp.where(sub == 2 * req + 1, book, 0.0), axis=0, keepdims=True)
    people = user[...].astype(F32)
    person = jnp.sum(jnp.where(iota(people.shape, 0) == item, people, 0.0), axis=0, keepdims=True)
    tile = jnp.concatenate(
        [
            first[:, :LANES],
            first[:, LANES:],
            second[:, :LANES],
            second[:, LANES:],
            person[:, :LANES],
            person[:, LANES:],
            jnp.zeros((2, LANES), F32),
        ],
        axis=0,
    )
    tiles[...] = jnp.broadcast_to(tile[None], (owners, MSG, LANES)).reshape(owners * MSG, LANES)
    tiles[pl.ds(WANT_ROW, owners, stride=MSG), :] = wanted
    message[...] = tiles[...].reshape(owners, MSG, LANES).astype(BF16)


def project_kernel(band, items_in, weights_in, table, items, weights, tiles, sems):
    stored, features = items.shape
    width = weights.shape[1]
    copies = [
        pltpu.make_async_copy(items_in, items, sems.at[0]),
        pltpu.make_async_copy(weights_in.at[0, pl.ds(width - features, features)], weights, sems.at[1]),
    ]
    for copy in copies:
        copy.start()
    for copy in copies:
        copy.wait()
    chunks = width // LANES
    copies = []
    for n in range(stored // band):
        for c in range(0, chunks, 2):
            left = items[n * band : (n + 1) * band, :]
            product = dot(left, weights[:, c * LANES : (c + 2) * LANES])
            for i in range(2):
                to = pl.ds(n * band * chunks + c + i, band, stride=chunks)
                tiles[to, :] = product[:, i * LANES : (i + 1) * LANES]
        whole = pl.ds(n * band * chunks, band * chunks)
        copies.append(pltpu.make_async_copy(tiles.at[whole], table.at[whole], sems.at[2 + n]))
        copies[-1].start()
    for copy in copies:
        copy.wait()


def rank_kernel(
    units,
    ranks,
    block,
    stretch,
    got,
    table_in,
    items,
    weights_in,
    bias,
    out_weight,
    logits,
    early,
    table,
    weights,
    tiles,
    features,
    people,
    greetings,
    first,
    state,
    rounded,
    answer,
    picks,
    picked,
    sems,
):
    sources = got.shape[0]
    rows = ranks * sources
    layers, width, _ = weights_in.shape
    stored = items.shape[0]
    chunks = width // LANES
    own = early.shape[0] // LANES
    copies = [(weights_in.at[0, pl.ds(0, own * LANES)], early), (table_in, table)]
    copies += [(weights_in.at[i], weights.at[i - 1]) for i in range(1, layers)]
    copies = [pltpu.make_async_copy(a, b, sems.at[i]) for i, (a, b) in enumerate(copies)]
    for copy in copies[:2]:
        copy.start()
    reqs = lax.axis_size("req")
    tiles[...] = got[...].astype(F32).reshape(sources * MSG, LANES)
    wanted = tiles[pl.ds(WANT_ROW, sources, stride=MSG), :]
    lane = iota((sources, LANES), 1)
    low = wanted.astype(I32)
    high = pltpu.roll(wanted, HALF, axis=1).astype(I32)
    within = low + 256 * (high & 3)
    person = ((high >> 2) & 31) * reqs + iota((sources, LANES), 0) % reqs
    split = (stored * chunks - 1).bit_length()
    picks[...] = within * chunks + ((person * chunks) << split)
    fetch = pltpu.make_async_copy(picks, picked, sems.at[len(copies)])
    fetch.start()
    users = [tiles[pl.ds(USER_ROW + i, sources, stride=MSG), :] for i in range(own)]
    blank = jnp.zeros((sources, LANES), F32)
    for c in range(chunks):
        people[pl.ds(c, sources, stride=chunks), :] = users[c] if c < own else blank
    flat = jnp.concatenate(users, axis=1).astype(BF16)

    def greet(sums):
        left = jnp.concatenate([flat] * (ranks // 2), axis=0)
        for turn in range(width // block):
            to = slice(turn * block, (turn + 1) * block)
            pltpu.matmul_push_rhs(early[:, to], turn // 2, turn % 2)
            pltpu.matmul_acc_lhs(sums[turn], left, turn // 2)
        for turn in range(width // block):
            product = pltpu.matmul_pop(sums[turn])[:sources]
            product = product + bias[0:1, turn * block : (turn + 1) * block]
            for i in range(0, block, LANES):
                c = (turn * block + i) // LANES
                greetings[pl.ds(c, sources, stride=chunks), :] = product[:, i : i + LANES]

    for c in range(chunks):
        part = jnp.zeros((stored, LANES), F32)
        if c >= own:
            part = items[:, (c - own) * LANES : (c - own + 1) * LANES].astype(F32)
        features[pl.ds(c, stored, stride=chunks), :] = part
    answer[...] = jnp.zeros(answer.shape, F32)

    def gather(slot, unit, some):
        values = []
        for n in some:
            k, source = n // sources, n % sources
            both = picked[source, unit * ranks + k]
            row = pl.ds(pl.multiple_of(both & ((1 << split) - 1), chunks), chunks)
            man = pl.ds(pl.multiple_of(both >> split, chunks), chunks)
            start = features[row, :] + people[man, :]
            values.append((n, start, start * (table[row, :] + greetings[man, :]) + start))
        for n, start, new in values:
            first[slot, pl.ds(n, chunks, stride=stretch), :] = start
            state[slot, pl.ds(n, chunks, stride=stretch), :] = new

    def lines(c, start, count):
        return slice(c * stretch + start, c * stretch + start + count)

    def begin(s, carry):
        for k in range(ranks):
            values = []
            for u in range(8):
                source = s * 8 + u
                both = picked[source, k]
                row = pl.ds(pl.multiple_of(both & ((1 << split) - 1), chunks), chunks)
                man = pl.ds(pl.multiple_of(both >> split, chunks), chunks)
                start = features[row, :] + people[man, :]
                new = start * (table[row, :] + greetings[man, :]) + start
                values.append((k * sources + source, start, new))
            for n, start, new in values:
                first[0, pl.ds(n, chunks, stride=stretch), :] = start
                state[0, pl.ds(n, chunks, stride=stretch), :] = new
        return carry

    halves = 2
    half = rows // halves
    depth = width // block
    blocks = [(u, l, p) for u in range(units) for l in range(1, layers) for p in range(depth // 2)]
    turns = [(*b, k) for b in blocks for k in range(depth)]
    share = -(-rows // (((layers - 1) * depth // 2 - 1) * depth))
    following = [list(range(rows)) for _ in range(units - 1)] + [[]]
    parts = [[jnp.zeros((half, LANES), F32) for _ in range(halves)] for _ in range(units)]

    def push(turn):
        _, layer, p, k = turns[turn]
        if p == 0 and k == 0 and turns[turn][0] == 0:
            copies[1 + layer].wait()
        for x in range(2):
            n = (2 * p + x) * block
            tile = weights[layer - 1, k * block : (k + 1) * block, n : n + block]
            pltpu.matmul_push_rhs(tile, turn % 2, x)

    def finish(unit, layer, p, h, x, total):
        n = (2 * p + x) * block
        product = pltpu.matmul_pop(total) + bias[layer : layer + 1, n : n + block]
        for i in range(0, block, LANES):
            at = lines((n + i) // LANES, h * half, half)
            new = first[unit % 2, at, :] * product[:, i : i + LANES] + state[unit % 2, at, :]
            if layer < layers - 1:
                state[unit % 2, at, :] = new
                rounded[layer % 2, h * half : (h + 1) * half, n + i : n + i + LANES] = new.astype(BF16)
            else:
                parts[unit][h] = parts[unit][h] + new * out_weight[:, n + i : n + i + LANES]
        if (layer, p, x) == (layers - 1, depth // 2 - 1, 1):
            value = lane_sum(parts[unit][h])
            for k in range(half // sources):
                j = unit * ranks + h * half // sources + k
                mine = value[k * sources : (k + 1) * sources]
                answer[...] += jnp.where(lane == j, mine, 0.0)

    def network(*sums):
        def total(block_at, h, x):
            return sums[(block_at % 2) * 4 + h * 2 + x]

        copies[0].wait()
        greet(sums)
        copies[2].start()
        fetch.wait()
        copies[1].wait()
        for copy in copies[3:]:
            copy.start()
        lax.fori_loop(0, sources // 8, begin, 0)
        push(0)
        for at, (unit, layer, p) in enumerate(blocks):
            waiting = [] if at == 0 else [(h, x) for h in range(halves) for x in range(2)]
            for k in range(depth):
                turn = at * depth + k
                if turn + 1 < len(turns):
                    push(turn + 1)
                for h in range(halves):
                    own_rows = slice(h * half, (h + 1) * half)
                    if layer == 1 and p == 0:
                        for c in range(k * block // LANES, (k + 1) * block // LANES):
                            entered = state[unit % 2, lines(c, h * half, half), :]
                            rounded[0, own_rows, c * LANES : (c + 1) * LANES] = entered.astype(BF16)
                    left = rounded[(layer + 1) % 2, own_rows, k * block : (k + 1) * block]
                    for x in range(2):
                        pltpu.matmul_acc_lhs(total(at, h, x), left, None if h else turn % 2)
                if (layer, p) != (1, 0):
                    gather(1 - unit % 2, unit + 1, following[unit][:share])
                    del following[unit][:share]
                for _ in range((1, 2, 1, 0)[k] if waiting else 0):
                    h, x = waiting.pop(0)
                    finish(*blocks[at - 1], h, x, total(at - 1, h, x))
        for h in range(halves):
            for x in range(2):
                finish(*blocks[-1], h, x, total(len(blocks) - 1, h, x))

    pl.run_scoped(network, *[pltpu.ACC(mxu_id=i % 2)((half, block), F32) for i in range(8)])
    logits[...] = answer[...].reshape(logits.shape)


def score_kernel(block, looked, got, user, codes, scores, tiles, tables, wide):
    sources = got.shape[0]
    requests, d_user = user.shape
    subs, count = codes.shape
    tiles[...] = got[...].astype(F32).reshape(sources * MSG, LANES)
    book = [tiles[pl.ds(i, sources, stride=MSG), :].astype(BF16) for i in range(CB_ROWS)]
    even = jnp.concatenate(book[:2], axis=1)
    odd = jnp.concatenate(book[2:], axis=1)
    column = iota((d_user, sources), 0)
    people = user[...]
    of_even = dot(people, as_bf16(column == 2 * iota((d_user, sources), 1))).astype(BF16)
    of_odd = dot(people, as_bf16(column == 2 * iota((d_user, sources), 1) + 1)).astype(BF16)
    per_sub = sources // subs
    zero = jnp.zeros((), BF16)
    for m in range(subs):
        mine = iota((requests, sources), 1) // per_sub == m
        table = dot(jnp.where(mine, of_even, zero), even) + dot(jnp.where(mine, of_odd, zero), odd)
        table = table.astype(BF16)
        if m < looked:
            wide[m] = table.astype(F32)
        else:
            tables[:, m * CODES : (m + 1) * CODES] = table

    code = lax.broadcasted_iota(jnp.int16, (CODES, block), 0)
    one = jnp.ones((), BF16)
    groups, spans = requests // 8, block // LANES
    order = sorted(
        [((i + 0.5) / looked, i) for i in range(looked)]
        + [((i + 0.5) / (subs - looked), i + looked) for i in range(subs - looked)]
    )

    def pick(values, index):
        return jnp.take_along_axis(values, index, axis=1, mode="promise_in_bounds")

    def step(j, carry):
        at = pl.ds(pl.multiple_of(j * block, block), block)
        total = jnp.zeros((requests, block), F32)
        sums = [[jnp.zeros((8, LANES), F32) for _ in range(spans)] for _ in range(groups)]
        for _, m in order:
            row = codes[m : m + 1, at]
            if m >= looked:
                now = jnp.broadcast_to(row, (16, block)).astype(jnp.int16)
                now = jnp.concatenate([now] * (CODES // 16), axis=0)
                onehot = jnp.where(code == now, one, zero)
                total = total + dot(tables[:, m * CODES : (m + 1) * CODES], onehot)
                continue
            for b in range(spans):
                now = jnp.broadcast_to(row[:, b * LANES : (b + 1) * LANES], (8, LANES))
                index = now & (LANES - 1)
                upper = now >= LANES
                for g in range(groups):
                    low = pick(wide[m, g * 8 : (g + 1) * 8, :LANES], index)
                    high = pick(wide[m, g * 8 : (g + 1) * 8, LANES:], index)
                    sums[g][b] = sums[g][b] + jnp.where(upper, high, low)
        rows = [jnp.concatenate(group, axis=1) for group in sums]
        scores[:, at] = total + jnp.concatenate(rows, axis=0)
        return carry

    lax.fori_loop(0, count // block, step, 0)


def collect_kernel(back, meta, logits):
    cand_dev, requests = logits.shape
    total = meta.shape[0]
    owners = back.shape[0]
    lane = iota((total, owners), 1)
    answers = back[...].reshape(owners, LANES)
    pick = as_bf16(meta[:, 0:1] == lane)
    top = answers.astype(BF16).astype(F32)
    rest = answers - top
    middle = rest.astype(BF16).astype(F32)
    last = rest - middle
    pieces = top + pltpu.roll(middle, PIECE, axis=1) + pltpu.roll(last, 2 * PIECE, axis=1)
    rows = dot(pick, pieces.astype(BF16))
    mine = (lane % PIECE == meta[:, 1:2]) & (lane < 3 * PIECE)
    value = lane_sum(jnp.where(mine, rows, 0.0))
    diagonal = iota((total, requests), 0) % requests == iota((total, requests), 1)
    spread = jnp.where(diagonal, value, 0.0)
    logits[...] = jnp.sum(spread.reshape(cand_dev, requests, requests), axis=1)


def on_device(
    user_emb,
    codebooks,
    item_codes,
    item_place,
    candidates,
    item_features,
    cross_weights,
    cross_bias,
    out_weight,
):
    requests, d_user = user_emb.shape
    cand_dev = candidates.shape[1]
    total = requests * cand_dev
    owners = lax.axis_size("item") * lax.axis_size("req")
    items = item_codes.shape[0]
    layers, width, _ = cross_weights.shape
    whole = pltpu.CompilerParams(vmem_limit_bytes=60 << 20)
    limit = pltpu.CompilerParams(vmem_limit_bytes=24 << 20)
    message, meta = pl.pallas_call(
        prepare_kernel,
        out_shape=(
            jax.ShapeDtypeStruct((owners, MSG, LANES), BF16),
            jax.ShapeDtypeStruct((total, LANES), I32),
        ),
        in_specs=[HBM] * 4,
        out_specs=(VMEM, VMEM),
        scratch_shapes=[
            pltpu.VMEM((owners * MSG, LANES), F32),
            pltpu.VMEM((cand_dev, requests), I32),
            pltpu.VMEM((item_place.shape[0] // LANES, LANES), I32),
            pltpu.VMEM(codebooks.shape[:0:-1], BF16),
            pltpu.VMEM(user_emb.shape, BF16),
            pltpu.SemaphoreType.DMA((4,)),
        ],
        compiler_params=whole,
        name="prepare",
    )(
        candidates.T,
        item_place.reshape(-1, LANES),
        jnp.swapaxes(codebooks, 1, 2)[0],
        user_emb,
    )
    got = lax.all_to_all(message, ("item", "req"), split_axis=0, concat_axis=0, tiled=True)
    stored, features = item_features.shape
    chunks = width // LANES
    lines = stored * chunks
    band = stored // 8
    table = pl.pallas_call(
        functools.partial(project_kernel, band),
        out_shape=jax.ShapeDtypeStruct((lines, LANES), F32),
        in_specs=[HBM, HBM],
        out_specs=HBM,
        scratch_shapes=[
            pltpu.VMEM(item_features.shape, BF16),
            pltpu.VMEM((features, width), BF16),
            pltpu.VMEM((lines, LANES), F32),
            pltpu.SemaphoreType.DMA((2 + stored // band,)),
        ],
        compiler_params=whole,
        name="project",
        cost_estimate=pl.CostEstimate(flops=2 << 30, bytes_accessed=12 << 20, transcendentals=0),
    )(item_features, cross_weights)
    capacity = 3 * total // owners
    ranks = 4
    rows = ranks * owners
    stretch = rows + 8
    answers = pl.pallas_call(
        functools.partial(rank_kernel, capacity // ranks, ranks, 256, stretch),
        out_shape=jax.ShapeDtypeStruct((owners, 1, LANES), F32),
        in_specs=[VMEM, HBM, VMEM, HBM, VMEM, VMEM],
        out_specs=VMEM,
        scratch_shapes=[
            pltpu.VMEM((d_user, width), BF16),
            pltpu.VMEM((lines, LANES), F32),
            pltpu.VMEM((layers - 1, width, width), BF16),
            pltpu.VMEM((owners * MSG, LANES), F32),
            pltpu.VMEM((lines, LANES), F32),
            pltpu.VMEM((owners * chunks, LANES), F32),
            pltpu.VMEM((owners * chunks, LANES), F32),
            pltpu.VMEM((2, stretch * chunks, LANES), F32),
            pltpu.VMEM((2, stretch * chunks, LANES), F32),
            pltpu.VMEM((2, rows, width), BF16),
            pltpu.VMEM((owners, LANES), F32),
            pltpu.VMEM((owners, LANES), I32),
            pltpu.SMEM((owners, LANES), I32),
            pltpu.SemaphoreType.DMA((layers + 2,)),
        ],
        compiler_params=pltpu.CompilerParams(vmem_limit_bytes=50 << 20),
        name="rank",
        cost_estimate=pl.CostEstimate(flops=12 << 30, bytes_accessed=10 << 20, transcendentals=0),
    )(got, table, item_features, cross_weights, cross_bias, out_weight.reshape(1, width))
    back = lax.all_to_all(answers, ("item", "req"), split_axis=0, concat_axis=0, tiled=True)
    looked = 14
    scores = pl.pallas_call(
        functools.partial(score_kernel, 512, looked),
        out_shape=jax.ShapeDtypeStruct((requests, items), F32),
        in_specs=[VMEM] * 3,
        out_specs=VMEM,
        scratch_shapes=[
            pltpu.VMEM((owners * MSG, LANES), F32),
            pltpu.VMEM((requests, item_codes.shape[1] * CODES), BF16),
            pltpu.VMEM((looked, requests, CODES), F32),
        ],
        compiler_params=limit,
        name="scores",
        cost_estimate=pl.CostEstimate(flops=2 << 30, bytes_accessed=40 << 20, transcendentals=0),
    )(got, user_emb, item_codes.T)
    logits = pl.pallas_call(
        collect_kernel,
        out_shape=jax.ShapeDtypeStruct((cand_dev, requests), F32),
        in_specs=[VMEM] * 2,
        out_specs=VMEM,
        compiler_params=limit,
        name="collect",
    )(back, meta)
    return scores, logits.T


def solution(mesh):
    placed = (
        P("req", None),
        P("item", None, None),
        P("item", None),
        P(),
        P("req", "item"),
        P(("item", "req"), None),
        P(),
        P(),
        P(),
    )
    return jax.shard_map(
        on_device,
        mesh=mesh,
        in_specs=placed,
        out_specs=(P("req", "item"), P("req", "item")),
        check_vma=False,
    )
```
